512 devices in a mesh: lat: 32 (over x_hi, y, core), lon: 16 (over x_lo, z).
Axes of the slice: x: 4 (x_hi: 2, x_lo: 2; x = x_hi * 2 + x_lo), y: 8, z: 8, core: 2. Of those that a mesh axis runs over, the one named last changes fastest.
Arguments:
- level_fields: float32 [2, 2, 640, 2560], P(None, None, 'lat', 'lon'), may hold values from -6 to 6
- wind_field: float32 [2, 2, 640, 2560], P(None, None, 'lat', 'lon'), may hold values from -6 to 6
- zonal_step: float32 [640], P('lat'), may hold values from 0.1 to 1
- quad_weight: float32 [640], P('lat'), may hold values from 0.005 to 0.05
- legendre: bfloat16 [640, 640, 640], P('lon', 'lat'), may hold values from -6 to 6
- wave_table: int32 [640], replicated, may hold values from 0 to 639, as said below
- damping: float32 [2], replicated, may hold values from 0.5 to 20
- vertical: float32 [2, 2], replicated, may hold values from -4 to 4
Outputs:
- new_fields: float32 [2, 2, 640, 2560], P(None, None, 'lat', 'lon')
- spectrum: float32 [640, 640, 2, 2], P('lat', 'lon')
The draws below stay inside these ranges and needn't reach their ends.
Inputs may be any that keep to these rules, and one draw needn't show every extreme that they name: `wave_table`: slots 2k and 2k+1 hold wavenumbers p and 639 - p; every wavenumber appears in exactly one slot.
All inputs are finite; a program needn't handle non-finite values.
Results may differ from the reference program's by a relative error of at most 0.0038.
Values may be sent and summed in bfloat16 or wider, within the bound.
A program may use at most 64 MiB of HBM per device.

```python
import math
import jax
import jax.numpy as jnp
from jax import lax

NLON = 2560
M = 640
LEVELS = 2
NHALF = 640


def draw_wave_table(key, part):
    order = jax.random.permutation(key, M // 2).astype(jnp.int32)
    return jnp.stack([order, M - 1 - order], axis=1).reshape(M)


def shard_levels(rng, extent, cuts, smallest, top_value):
    def one(dim, blocks):
        draws = jax.random.uniform(jax.random.fold_in(jax.random.fold_in(rng, 6), dim), (blocks,), jnp.float32, smallest / len(cuts), top_value / len(cuts))
        return jnp.repeat(jnp.exp(draws), extent[dim] // blocks).reshape((-1,) + (1,) * (len(extent) - dim - 1))

    loudness = one(*cuts[0])
    for cut in cuts[1:]:
        loudness = loudness * one(*cut)
    return loudness


def centred(key, dims, spread, limit, pieces=(), kind=jnp.bfloat16):
    level = shard_levels(key, dims, pieces, -0.22, 0.18) if pieces else 1.0
    entries = jax.random.normal(key, dims, jnp.float32) * spread * level
    return jnp.minimum(jnp.maximum(entries, -limit), limit).astype(kind)


def setup_inputs(seed: int = 0) -> dict:
    keys = jax.random.split(jax.random.key(seed), 9)
    return {
        "level_fields": centred(keys[0], (LEVELS, 2, NHALF, NLON), 1.0, 6.0, ((2, 32), (3, 16)), jnp.float32),
        "wind_field": centred(keys[1], (2, 2, NHALF, NLON), 1.0, 6.0, ((2, 32), (3, 16)), jnp.float32),
        "zonal_step": jnp.clip(jnp.exp(math.log(1.0) - 2.3025851 * jax.random.uniform(keys[2], (NHALF,), jnp.float32) ** shard_levels(keys[2], (NHALF,), ((0, 32),), -0.2, 0.2)), 0.1, 1.0),
        "quad_weight": jnp.clip(jnp.exp(math.log(0.05) - 2.3025851 * jax.random.uniform(keys[3], (NHALF,), jnp.float32) ** shard_levels(keys[3], (NHALF,), ((0, 32),), -0.2, 0.2)), 0.005, 0.05),
        "legendre": centred(keys[4], (M, NHALF, M), 1.0, 6.0, ((0, 16), (1, 32))),
        "wave_table": draw_wave_table(jax.random.fold_in(keys[8], 71), 0),
        "damping": jnp.clip(jnp.exp(jax.random.uniform(keys[6], (LEVELS,), jnp.float32, math.log(0.5), math.log(20.0))), 0.5, 20.0),
        "vertical": centred(keys[7], (LEVELS, LEVELS), LEVELS ** -0.5, 4.0, (), jnp.float32),
    }


HIGHEST_PRECISION = lax.Precision.HIGHEST

def angle_table(waves, columns):
    return (waves[:, None] * columns[None, :] % NLON).astype(jnp.float32) * (2.0 * math.pi / NLON)

def advect(level_fields, wind_field, zonal_step):
    eastward = jnp.roll(level_fields, -1, axis=3)
    westward = jnp.roll(level_fields, 1, axis=3)
    equator_row = level_fields[:, ::-1, -1:, :]
    toward = jnp.concatenate([level_fields[:, :, 1:, :], equator_row], axis=2)
    poleward = jnp.concatenate([jnp.zeros_like(level_fields[:, :, :1, :]), level_fields[:, :, :-1, :]], axis=2)
    tendency = wind_field[0] * zonal_step[:, None] * (eastward - westward) + 0.25 * wind_field[1] * (toward - poleward)
    return level_fields - tendency

def correct(spectrum, degrees, damping, vertical):
    modal = jnp.einsum('kl,nmcl->nmck', vertical, spectrum, precision=HIGHEST_PRECISION)
    divisor = 1.0 + damping[None, :] * (degrees * (degrees + 1)).astype(jnp.float32)[:, None] / float(M * M)
    modal = modal / divisor[:, None, None, :]
    return jnp.einsum('kl,nmck->nmcl', vertical, modal, precision=HIGHEST_PRECISION)

def reference(level_fields, wind_field, zonal_step, quad_weight, legendre, wave_table, damping, vertical):
    stepped = advect(level_fields, wind_field, zonal_step)
    flat_grid = stepped.reshape(-1, NLON)
    angles = angle_table(wave_table, jnp.arange(NLON, dtype=jnp.int32))
    cosine_part = jnp.dot(jnp.cos(angles), flat_grid.T, precision=HIGHEST_PRECISION)
    sine_part = -jnp.dot(jnp.sin(angles), flat_grid.T, precision=HIGHEST_PRECISION)
    fourier = jnp.stack([cosine_part, sine_part], axis=1) / math.sqrt(NLON)
    weighted = (fourier.reshape(M, 2, LEVELS, 2, NHALF) * quad_weight).astype(jnp.bfloat16)
    weighted = weighted.reshape(M, 4 * LEVELS, NHALF)
    degrees = jnp.arange(M, dtype=jnp.int32)

    def forward_slot(inputs):
        weight_slot, table_slot, wave = inputs
        summed = jnp.dot(weight_slot, table_slot, preferred_element_type=jnp.float32).reshape(2, LEVELS, 2, M)
        parity = jnp.where((degrees - wave) % 2 == 0, 1.0, -1.0)
        combined = summed[:, :, 0] + parity * summed[:, :, 1]
        return jnp.where(degrees >= wave, combined, 0.0)
    raw = lax.map(forward_slot, (weighted, legendre, wave_table))
    raw = raw.transpose(3, 0, 1, 2)
    spectrum = correct(raw, degrees, damping, vertical)
    rounded = spectrum.astype(jnp.bfloat16).transpose(1, 0, 2, 3).reshape(M, M, 2 * LEVELS)

    def inverse_slot(inputs):
        table_slot, coef_slot, wave = inputs
        even_mask = ((degrees - wave) % 2 == 0)[:, None]
        even_part = jnp.dot(table_slot, jnp.where(even_mask, coef_slot, 0), preferred_element_type=jnp.float32)
        odd_part = jnp.dot(table_slot, jnp.where(even_mask, 0, coef_slot), preferred_element_type=jnp.float32)
        return jnp.stack([even_part + odd_part, even_part - odd_part], axis=0) / math.sqrt(M)
    coefs = lax.map(inverse_slot, (legendre, rounded, wave_table))
    coefs = coefs.reshape(M, 2, NHALF, 2, LEVELS).transpose(0, 3, 4, 1, 2).reshape(M, 2, -1)
    factor = jnp.where(wave_table == 0, 1.0, 2.0)[:, None]
    grid_out = jnp.dot(coefs[:, 0].T, jnp.cos(angles) * factor, precision=HIGHEST_PRECISION)
    grid_out = grid_out - jnp.dot(coefs[:, 1].T, jnp.sin(angles) * factor, precision=HIGHEST_PRECISION)
    new_fields = (grid_out / math.sqrt(NLON)).reshape(LEVELS, 2, NHALF, NLON)
    return (new_fields, spectrum)
```

```python
import functools

import jax
import jax.numpy as jnp
from jax import lax
from jax.experimental import pallas as pl
from jax.experimental.pallas import tpu as pltpu
from jax.sharding import PartitionSpec as P

NLON = 2560
M = 640
ROWS = 20
GRID = 80
SLOTS = 40
LANES = 256
K = ROWS * SLOTS
CHIPS = 16
BLOCKS = 16
PACK = 48
F32 = jnp.float32
BF16 = jnp.bfloat16
MESH = pl.DeviceIdType.MESH


def fiota(shape, dim):
    return lax.broadcasted_iota(jnp.int32, shape, dim).astype(F32)


def fdiv(x, by):
    return jnp.floor((x + 0.5) * (1.0 / by))


def fmod(x, by):
    return x - by * fdiv(x, by)


def dot(a, b):
    return lax.dot_general(a, b, (((1,), (0,)), ((), ())), preferred_element_type=F32)


def dot_nt(a, b):
    return lax.dot_general(a, b, (((1,), (1,)), ((), ())), preferred_element_type=F32)


def split(x):
    high = x.astype(BF16)
    return high, (x - high.astype(F32)).astype(BF16)


def column(row, picked):
    n = row.shape[1]
    rows = picked.shape[0]
    hit = fiota((rows, n), 1) == picked
    return jnp.sum(jnp.where(hit, jnp.broadcast_to(row, (rows, n)), 0.0), axis=1, keepdims=True)


def as_row(col):
    hit = fiota((GRID, 128), 1) == fiota((GRID, 128), 0)
    return jnp.sum(jnp.where(hit, jnp.broadcast_to(col, (GRID, 128)), 0.0), axis=0, keepdims=True)


def trig(waves, first):
    lons = first + fiota((1, LANES), 1)
    turns = waves * lons
    quarter = jnp.floor(turns * (4.0 / NLON) + 0.5)
    rest = turns - quarter * (NLON / 4.0)
    t = rest * (6.283185307179586 / NLON)
    t2 = t * t
    sine = t * (1.0 + t2 * (-1.6666667e-1 + t2 * (8.3333333e-3 + t2 * (-1.9841270e-4 + t2 * 2.7557319e-6))))
    cosine = 1.0 + t2 * (-0.5 + t2 * (4.1666667e-2 + t2 * (-1.3888889e-3 + t2 * 2.4801587e-5)))
    which = quarter.astype(jnp.int32) & 3
    swap = (which & 1) == 1
    c = jnp.where(swap, sine, cosine)
    s = jnp.where(swap, cosine, sine)
    c = jnp.where((which == 1) | (which == 2), -c, c)
    s = jnp.where(which >= 2, s, -s)
    return c, s


def step_field(level, wind, up, down, at_pole, at_equator, east, west, zonal, weight, roll):
    lane = fiota((40, LANES), 1)
    wide = jnp.where(lane == 160.0, east, jnp.where(lane == 255.0, west, level))
    eastward = roll(wide, LANES - 1, 1)
    westward = roll(wide, 1, 1)
    last = level[32:40]
    row8 = fiota((8, LANES), 0)
    swapped = jnp.where(row8 == 0.0, roll(last, 1, 0), roll(last, 3, 0))
    down = jnp.where(at_equator, swapped, down)
    up = jnp.where(at_pole, 0.0, up)
    tall = jnp.concatenate([up, level, down], axis=0)
    toward = roll(tall, 54, 0)[8:48]
    poleward = roll(tall, 2, 0)[8:48]
    change = wind[0] * zonal * (eastward - westward) + 0.25 * wind[1] * (toward - poleward)
    return (level - change) * weight


def row_codes():
    r = fiota((384, 1), 0)
    parity = fdiv(r, 192.0)
    r1 = fmod(r, 192.0)
    h = fdiv(r1, 96.0)
    c = fdiv(fmod(r1, 96.0), 48.0)
    r2 = fmod(r1, 48.0)
    group = fdiv(r2, 16.0)
    level = fdiv(fmod(r2, 16.0), 8.0)
    pair = group * 8.0 + fmod(r2, 8.0)
    slot = jnp.where(pair < 20.0, 2.0 * pair + parity, -1.0)
    return slot, c, level, h


def select_rows():
    slot, c, level, h = row_codes()
    lane = fiota((1, 2 * SLOTS), 1)
    hit = (slot == fmod(lane, 40.0)) & (c == fdiv(lane, 40.0))
    return jnp.where(hit, 1.0, 0.0).astype(BF16)


def select_rows_t():
    r = fiota((1, 384), 1)
    parity = fdiv(r, 192.0)
    r1 = fmod(r, 192.0)
    c = fdiv(fmod(r1, 96.0), 48.0)
    r2 = fmod(r1, 48.0)
    pair = fdiv(r2, 16.0) * 8.0 + fmod(r2, 8.0)
    slot = jnp.where(pair < 20.0, 2.0 * pair + parity, -1.0)
    row = fiota((2 * SLOTS, 1), 0)
    hit = (slot == fmod(row, 40.0)) & (c == fdiv(row, 40.0))
    return jnp.where(hit, 1.0, 0.0).astype(BF16)


def spread_rows():
    g = fiota((128, 1), 0)
    lane = fiota((1, K), 1)
    hit = (fdiv(fmod(g, 40.0), 2.0) == fdiv(lane, 40.0)) & (g < 80.0)
    return jnp.where(hit, 1.0, 0.0).astype(BF16)


def level_mask():
    slot, c, level, h = row_codes()
    g = fiota((1, 128), 1)
    hit = (level == fdiv(g, 40.0)) & (h == fmod(g, 2.0)) & (g < 80.0)
    return hit


def slot_lanes():
    return fmod(fiota((1, K), 1), 40.0)


def reverse_matrix():
    n = fiota((M, M), 0)
    j = fiota((M, M), 1)
    hit = (n + j == M - 2.0) | (n + j == 2.0 * M - 2.0)
    return jnp.where(hit, 1.0, 0.0).astype(BF16)


def first_wave(waves, lon):
    r = fiota((64, 1), 0)
    pair = fdiv(r, 16.0) * 8.0 + fmod(r, 8.0)
    picked = jnp.where(pair < 20.0, lon * 40.0 + 2.0 * pair, -1.0)
    return column(waves, picked)


def parity_sign(first):
    j = fiota((PACK, M), 1)
    odd = (j - first).astype(jnp.int32) & 1
    return jnp.where(odd == 1, -1.0, 1.0)


def spread_weighted(weighted, selector, spreader):
    chosen = dot(selector, weighted)
    chosen = jnp.where(level_mask(), chosen, 0.0).astype(BF16)
    wide = dot(chosen, spreader)
    slot = row_codes()[0]
    return jnp.where(slot == slot_lanes(), wide, 0.0).astype(BF16)


def pack(even, odd, sign, first, c):
    lo = c * PACK
    hi = 96 + c * PACK
    kept = fiota((PACK, M), 1) >= first
    from_odd = odd[lo:lo + PACK] - sign * odd[hi:hi + PACK]
    packed = jnp.where(kept, even[lo:lo + PACK] + sign * even[hi:hi + PACK], from_odd)
    return packed, from_odd[:, M - 1:M]


def correct(total, first, lane0, extra, damping, vertical):
    j = lane0 + fiota((8, 128), 1)
    n = jnp.where(j >= first, j, (M - 2.0) - j)
    n = jnp.where(extra, M - 1.0, n)
    square = n * (n + 1.0) / float(M * M)
    raw = (total[0:8], total[8:16])
    modal = [
        (vertical[k][0] * raw[0] + vertical[k][1] * raw[1]) / (1.0 + damping[k] * square)
        for k in range(2)
    ]
    return jnp.concatenate(
        [vertical[0][l] * modal[0] + vertical[1][l] * modal[1] for l in range(2)], axis=0
    )


def unpack(packed, extra, first):
    j = fiota((PACK, M), 1)
    kept = j >= first
    even = jnp.where(kept, packed, 0.0)
    odd = jnp.where(j == M - 1.0, extra, jnp.where(kept, 0.0, packed))
    return even, odd


def spectrum_rows(even, odd, lat):
    r = fiota((32, 1), 0)
    n = jnp.where(r < ROWS, lat * ROWS + r, -5.0)
    j = fiota((1, M), 1)
    want_even = jnp.where(n == j, 1.0, 0.0).astype(BF16)
    want_odd = jnp.where((n + j == M - 2.0) | (n + j == 2.0 * M - 2.0), 1.0, 0.0).astype(BF16)
    q = fiota((96, 1), 0)
    c = fdiv(q, 48.0)
    q1 = fmod(q, 48.0)
    level = fdiv(fmod(q1, 16.0), 8.0)
    pair = fdiv(q1, 16.0) * 8.0 + fmod(q1, 8.0)
    lane = fiota((1, 160), 1)
    same = (c == fdiv(lane, 80.0)) & (level == fdiv(fmod(lane, 80.0), 40.0)) & (pair < 20.0)
    slot = fmod(lane, 40.0)
    to_even = jnp.where(same & (slot == 2.0 * pair), 1.0, 0.0).astype(BF16)
    to_odd = jnp.where(same & (slot == 2.0 * pair + 1.0), 1.0, 0.0).astype(BF16)
    return dot(dot_nt(want_even, even).astype(BF16), to_even) + dot(
        dot_nt(want_odd, odd).astype(BF16), to_odd
    )


def collapse(x_even, x_odd, selector_t, spreader):
    both = jnp.concatenate([x_even, x_odd], axis=0)
    slot = row_codes()[0]
    both = jnp.where(slot == slot_lanes(), both, 0.0).astype(BF16)
    rows = dot_nt(both, spreader)
    rows = jnp.where(level_mask(), rows, 0.0).astype(BF16)
    return dot(selector_t, rows).astype(BF16)


def kernel(
    level_ref, wind_ref, zonal_ref, weight_ref, leg_ref, wave_ref, damp_ref, vert_ref,
    grid_ref, spec_ref,
    column_out, column_in, edge_in, own_block, near_block, cos_wide, table_hi, table_lo,
    near_hi, near_lo, reversed_ref, part_out, part_in, spread_ref, packed_ref, core_in,
    sum_out, sum_in, first_ref, gathered, coefs,
    edge_send, edge_recv, near_send, near_recv, part_send, part_recv, core_send, core_recv,
    sum_send, sum_recv, all_send, all_recv, pair_send, pair_recv, coef_send, coef_recv,
    fwd_send, fwd_recv,
):
    lat = lax.axis_index("lat")
    lon = lax.axis_index("lon")
    chip = lat // 2
    core = lat % 2
    x_lo = lon // 8
    z = lon % 8
    lat_next, lat_prev = (lat + 1) % 32, (lat + 31) % 32
    lon_next, lon_prev = (lon + 1) % 16, (lon + 15) % 16
    near = (1 - x_lo) * 8 + z
    sibling = chip * 2 + 1 - core
    flat = lat.astype(F32)
    flon = lon.astype(F32)

    def chip_at(offset):
        return (chip + offset) % CHIPS

    def z_at(offset):
        return (z + offset) % 8

    def send(src, dst, send_sem, recv_sem, device):
        copy = pltpu.make_async_remote_copy(
            src_ref=src, dst_ref=dst, send_sem=send_sem, recv_sem=recv_sem,
            device_id=device, device_id_type=MESH,
        )
        copy.start()
        return copy

    def roll(x, amount, axis):
        return pltpu.roll(x, amount, axis)

    barrier = pltpu.get_barrier_semaphore()

    def greet(device):
        pl.semaphore_signal(barrier, inc=1, device_id=device, device_id_type=MESH)

    for device in (
        (lat_next, lon), (lat_prev, lon), (lat, lon_next), (lat, lon_prev), (lat, near), (sibling, lon)
    ):
        greet(device)

    @pl.loop(1, 8)
    def _(o):
        greet((lat, x_lo * 8 + z_at(o)))

    @pl.loop(1, CHIPS)
    def _(o):
        greet((chip_at(o) * 2 + core, lon))

    flat_level = jnp.reshape(level_ref[...], (GRID, LANES))
    column_out[0] = jnp.broadcast_to(as_row(flat_level[:, 0:1]), (8, 128))
    column_out[1] = jnp.broadcast_to(as_row(flat_level[:, 159:160]), (8, 128))
    waves = wave_ref[...].astype(F32)
    tall = jnp.broadcast_to(waves, (128, M))
    for t in range(5):
        cos_wide[128 * t:128 * (t + 1), :] = tall[:, 128 * t:128 * (t + 1)].T
    first_ref[...] = jnp.broadcast_to(first_wave(waves, flon), (64, 128))

    pl.semaphore_wait(barrier, 6 + 7 + 15)

    edges = [
        send(level_ref.at[:, 32:40, :], edge_in.at[0], edge_send.at[0], edge_recv.at[0], (lat_next, lon)),
        send(level_ref.at[:, 0:8, :], edge_in.at[1], edge_send.at[1], edge_recv.at[1], (lat_prev, lon)),
        send(column_out.at[0], column_in.at[0], edge_send.at[2], edge_recv.at[2], (lat, lon_prev)),
        send(column_out.at[1], column_in.at[1], edge_send.at[3], edge_recv.at[3], (lat, lon_next)),
    ]

    def fill(source, hi, lo, at, first):
        w = cos_wide[pl.ds(pl.multiple_of(source * SLOTS, 8), SLOTS), 0:1]
        c, s = trig(w, first)
        high, low = split(jnp.concatenate([c, s], axis=0))
        hi[at] = high
        lo[at] = low

    @pl.loop(0, 16)
    def _(source):
        fill(source, table_hi, table_lo, source, flon * 160.0)

    for copy in edges:
        copy.wait()

    picked = fdiv(fiota((40, 1), 0), 2.0)
    zonal = column(zonal_ref[...], picked)
    weight = column(weight_ref[...], picked) * (1.0 / float(NLON) ** 0.5)
    g = fiota((40, 1), 0)
    own_block[80:128, :] = jnp.zeros((48, LANES), F32)
    for l in range(2):
        east = column(column_in[0, 0:1, :], g + 40.0 * l)
        west = column(column_in[1, 0:1, :], g + 40.0 * l)
        own_block[40 * l:40 * (l + 1), :] = step_field(
            level_ref[l], (wind_ref[0], wind_ref[1]), edge_in[0, l], edge_in[1, l],
            lat == 0, lat == 31, east, west, zonal, weight, roll,
        )
    to_near = send(own_block, near_block, near_send, near_recv, (lat, near))

    near_first = near.astype(F32) * 160.0

    @pl.loop(0, 8)
    def _(zz):
        fill(x_lo * 8 + zz, near_hi, near_lo, zz, near_first)

    def wide(ref):
        return jnp.reshape(ref[...], (8 * 80, LANES))

    own_hi, own_lo = split(own_block[...])
    mine = pl.ds(x_lo * 8, 8)
    t_hi = jnp.reshape(table_hi[mine], (640, LANES))
    t_lo = jnp.reshape(table_lo[mine], (640, LANES))
    partial = dot_nt(t_hi, own_hi) + dot_nt(t_hi, own_lo) + dot_nt(t_lo, own_hi)
    to_near.wait()
    near_h, near_l = split(near_block[...])
    n_hi, n_lo = wide(near_hi), wide(near_lo)
    partial = partial + dot_nt(n_hi, near_h) + dot_nt(n_hi, near_l) + dot_nt(n_lo, near_h)
    part_out[...] = jnp.reshape(partial, (8, 80, 128))

    def part_copy(o):
        other = z_at(o)
        return pltpu.make_async_remote_copy(
            src_ref=part_out.at[other], dst_ref=part_in.at[z], send_sem=part_send.at[o],
            recv_sem=part_recv.at[z], device_id=(lat, x_lo * 8 + other), device_id_type=MESH,
        )

    @pl.loop(1, 8)
    def _(o):
        part_copy(o).start()

    part_in[z] = part_out[z]
    leg = leg_ref[...]
    reversed_ref[...] = dot(leg, reverse_matrix()).astype(BF16)
    sign = parity_sign(first_ref[0:PACK, 0:1])
    first = first_ref[0:PACK, 0:1]
    selector, spreader = select_rows(), spread_rows()

    @pl.loop(1, 8)
    def _(o):
        other = z_at(o)
        pltpu.make_async_remote_copy(
            src_ref=part_out.at[other], dst_ref=part_in.at[other], send_sem=part_send.at[o],
            recv_sem=part_recv.at[other], device_id=(lat, x_lo * 8 + other), device_id_type=MESH,
        ).wait_recv()

    weighted = jnp.sum(part_in[...], axis=0).astype(BF16)
    spread_ref[...] = spread_weighted(weighted, selector, spreader)
    even = dot(spread_ref[0:192], leg)
    odd = dot(spread_ref[192:384], reversed_ref[...])
    lane128 = fiota((16, 128), 1)
    for c in range(2):
        packed, extra = pack(even, odd, sign, first, c)
        rest = jnp.zeros((16, 128), F32)
        for kb in range(3):
            for t in range(5):
                packed_ref[c, kb * 5 + t] = packed[16 * kb:16 * (kb + 1), 128 * t:128 * (t + 1)]
            rest = jnp.where(lane128 == float(kb), extra[16 * kb:16 * (kb + 1)], rest)
        packed_ref[c, 15] = rest

    to_core = send(packed_ref.at[1 - core], core_in, core_send, core_recv, (sibling, lon))
    to_core.wait()
    sum_out[...] = packed_ref[core] + core_in[...]

    @pl.loop(1, CHIPS)
    def _(o):
        other = chip_at(o)
        pltpu.make_async_remote_copy(
            src_ref=sum_out.at[other], dst_ref=sum_in.at[chip], send_sem=sum_send.at[o],
            recv_sem=sum_recv.at[chip], device_id=(other * 2 + core, lon), device_id_type=MESH,
        ).start()

    sum_in[chip] = sum_out[chip]

    @pl.loop(1, CHIPS)
    def _(o):
        other = chip_at(o)
        pltpu.make_async_remote_copy(
            src_ref=sum_out.at[other], dst_ref=sum_in.at[other], send_sem=sum_send.at[o],
            recv_sem=sum_recv.at[other], device_id=(other * 2 + core, lon), device_id_type=MESH,
        ).wait_recv()

    total = jnp.sum(sum_in[...], axis=0)
    damping = (damp_ref[0], damp_ref[1])
    vertical = ((vert_ref[0, 0], vert_ref[0, 1]), (vert_ref[1, 0], vert_ref[1, 1]))
    first8 = first_ref[pl.ds(pl.multiple_of((chip // 5) * 16, 8), 8), 0:1]
    lane0 = ((chip % 5) * 128).astype(F32)
    spec = correct(total, first8, lane0, chip == 15, damping, vertical)
    gathered[core, chip] = spec.astype(BF16)

    @pl.loop(1, CHIPS)
    def _(o):
        other = chip_at(o)
        pltpu.make_async_remote_copy(
            src_ref=gathered.at[core, chip], dst_ref=gathered.at[core, chip], send_sem=all_send.at[o],
            recv_sem=all_recv.at[chip], device_id=(other * 2 + core, lon), device_id_type=MESH,
        ).start()

    @pl.loop(1, CHIPS)
    def _(o):
        other = chip_at(o)
        pltpu.make_async_remote_copy(
            src_ref=gathered.at[core, other], dst_ref=gathered.at[core, other], send_sem=all_send.at[o],
            recv_sem=all_recv.at[other], device_id=(other * 2 + core, lon), device_id_type=MESH,
        ).wait_recv()

    to_pair = send(gathered.at[core], gathered.at[core], pair_send, pair_recv, (sibling, lon))
    to_pair.wait()

    evens, odds = [], []
    for c in range(2):
        tiles = [[gathered[c, kb * 5 + t].astype(F32) for t in range(5)] for kb in range(3)]
        packed = jnp.concatenate([jnp.concatenate(row, axis=1) for row in tiles], axis=0)
        last = gathered[c, 15].astype(F32)
        extra = jnp.concatenate([last[:, kb:kb + 1] for kb in range(3)], axis=0)
        e, o = unpack(packed, extra, first)
        evens.append(e)
        odds.append(o)
    scale_even = jnp.where(first == 0.0, 1.0, 2.0)
    scale_odd = jnp.where(first == M - 1.0, 1.0, 2.0)
    north_e = [e * scale_even for e in evens]
    north_o = [o * scale_odd for o in odds]
    rows_e = jnp.concatenate(north_e + [e * sign for e in north_e], axis=0).astype(BF16)
    rows_o = jnp.concatenate(north_o + [-(o * sign) for o in north_o], axis=0).astype(BF16)
    x_even = dot_nt(rows_e, leg)
    x_odd = dot_nt(rows_o, reversed_ref[...])
    coefs[lon] = collapse(x_even, x_odd, select_rows_t(), spreader)

    def coef_copy(o):
        return pltpu.make_async_remote_copy(
            src_ref=coefs.at[lon], dst_ref=coefs.at[lon], send_sem=coef_send.at[o],
            recv_sem=coef_recv.at[z], device_id=(lat, x_lo * 8 + z_at(o)), device_id_type=MESH,
        )

    def forward_copy(source):
        at = x_lo * 8 + source
        return pltpu.make_async_remote_copy(
            src_ref=coefs.at[at], dst_ref=coefs.at[at], send_sem=fwd_send.at[source],
            recv_sem=fwd_recv.at[source], device_id=(lat, near), device_id_type=MESH,
        )

    forward_copy(z).start()

    @pl.loop(1, 8)
    def _(o):
        coef_copy(o).start()

    evens = jnp.concatenate(evens, axis=0).astype(BF16)
    odds = jnp.concatenate(odds, axis=0).astype(BF16)
    spec_ref[...] = spectrum_rows(evens, odds, flat)

    @pl.loop(1, 8)
    def _(o):
        other = z_at(o)
        at = x_lo * 8 + other
        pltpu.make_async_remote_copy(
            src_ref=coefs.at[at], dst_ref=coefs.at[at], send_sem=coef_send.at[o],
            recv_sem=coef_recv.at[other], device_id=(lat, at), device_id_type=MESH,
        ).wait_recv()
        forward_copy(other).start()

    def inverse(half):
        rows = pl.ds(half * 8, 8)
        values = jnp.reshape(coefs[rows], (640, 128)).T
        return dot(values, jnp.reshape(table_hi[rows], (640, LANES))) + dot(
            values, jnp.reshape(table_lo[rows], (640, LANES))
        )

    grid = inverse(x_lo)

    @pl.loop(0, 8)
    def _(source):
        at = (1 - x_lo) * 8 + source
        pltpu.make_async_remote_copy(
            src_ref=coefs.at[at], dst_ref=coefs.at[at], send_sem=fwd_send.at[source],
            recv_sem=fwd_recv.at[source], device_id=(lat, near), device_id_type=MESH,
        ).wait_recv()

    grid = grid + inverse(1 - x_lo)
    grid_ref[...] = grid[0:GRID] * (1.0 / float(NLON * M) ** 0.5)

    @pl.loop(1, 8)
    def _(o):
        part_copy(o).wait_send()
        coef_copy(o).wait_send()

    @pl.loop(0, 8)
    def _(source):
        forward_copy(source).wait_send()

    @pl.loop(1, CHIPS)
    def _(o):
        other = chip_at(o)
        pltpu.make_async_remote_copy(
            src_ref=sum_out.at[other], dst_ref=sum_in.at[chip], send_sem=sum_send.at[o],
            recv_sem=sum_recv.at[chip], device_id=(other * 2 + core, lon), device_id_type=MESH,
        ).wait_send()
        pltpu.make_async_remote_copy(
            src_ref=gathered.at[core, chip], dst_ref=gathered.at[core, chip], send_sem=all_send.at[o],
            recv_sem=all_recv.at[chip], device_id=(other * 2 + core, lon), device_id_type=MESH,
        ).wait_send()


def shards(level_fields, wind_field, zonal_step, quad_weight, legendre, wave_table, damping, vertical):
    def rows(x):
        x = x.transpose(0, 2, 1, 3).reshape(2, 2 * ROWS, 160)
        return jnp.pad(x, ((0, 0), (0, 0), (0, LANES - 160)))

    vmem = pl.BlockSpec(memory_space=pltpu.VMEM)
    smem = pl.BlockSpec(memory_space=pltpu.SMEM)
    dma = pltpu.SemaphoreType.DMA
    grid, spec = pl.pallas_call(
        kernel,
        out_shape=(
            jax.ShapeDtypeStruct((GRID, LANES), F32),
            jax.ShapeDtypeStruct((32, 160), F32),
        ),
        in_specs=[vmem] * 6 + [smem] * 2,
        out_specs=(vmem, vmem),
        scratch_shapes=[
            pltpu.VMEM((2, 8, 128), F32),
            pltpu.VMEM((2, 8, 128), F32),
            pltpu.VMEM((2, 2, 8, LANES), F32),
            pltpu.VMEM((128, LANES), F32),
            pltpu.VMEM((128, LANES), F32),
            pltpu.VMEM((M, 128), F32),
            pltpu.VMEM((16, 80, LANES), BF16),
            pltpu.VMEM((16, 80, LANES), BF16),
            pltpu.VMEM((8, 80, LANES), BF16),
            pltpu.VMEM((8, 80, LANES), BF16),
            pltpu.VMEM((K, M), BF16),
            pltpu.VMEM((8, 80, 128), F32),
            pltpu.VMEM((8, 80, 128), F32),
            pltpu.VMEM((384, K), BF16),
            pltpu.VMEM((2, BLOCKS, 16, 128), F32),
            pltpu.VMEM((BLOCKS, 16, 128), F32),
            pltpu.VMEM((BLOCKS, 16, 128), F32),
            pltpu.VMEM((CHIPS, 16, 128), F32),
            pltpu.VMEM((64, 128), F32),
            pltpu.VMEM((2, BLOCKS, 16, 128), BF16),
            pltpu.VMEM((16, 80, 128), BF16),
            dma((4,)), dma((4,)), dma, dma, dma((8,)), dma((8,)), dma, dma,
            dma((CHIPS,)), dma((CHIPS,)), dma((CHIPS,)), dma((CHIPS,)), dma, dma,
            dma((8,)), dma((8,)), dma((8,)), dma((8,)),
        ],
        compiler_params=pltpu.CompilerParams(
            collective_id=0, has_side_effects=True, vmem_limit_bytes=40 * 1024 * 1024
        ),
    )(
        rows(level_fields), rows(wind_field), zonal_step[None], quad_weight[None],
        legendre.transpose(1, 0, 2).reshape(K, M), wave_table[None], damping, vertical,
    )
    fields = grid[:, :160].reshape(2, ROWS, 2, 160).transpose(0, 2, 1, 3)
    spectrum = spec[:ROWS].reshape(ROWS, 2, 2, SLOTS).transpose(0, 3, 1, 2)
    return fields, spectrum


def solution(mesh):
    return jax.shard_map(
        shards,
        mesh=mesh,
        in_specs=(
            P(None, None, "lat", "lon"),
            P(None, None, "lat", "lon"),
            P("lat"),
            P("lat"),
            P("lon", "lat", None),
            P(),
            P(),
            P(),
        ),
        out_specs=(P(None, None, "lat", "lon"), P("lat", "lon", None, None)),
        check_vma=False,
    )
```

```python
import functools

import jax
import jax.numpy as jnp
from jax import lax
from jax.experimental import pallas as pl
from jax.experimental.pallas import tpu as pltpu
from jax.sharding import PartitionSpec as P

NLON = 2560
M = 640
ROWS = 20
GRID = 80
SLOTS = 40
LANES = 256
K = ROWS * SLOTS
CHIPS = 16
BLOCKS = 16
PACK = 48
F32 = jnp.float32
BF16 = jnp.bfloat16
MESH = pl.DeviceIdType.MESH
FAR_FIRST = (12, 11, 13, 4, 10, 14, 3, 5, 9, 15, 8, 2, 6, 1, 7)
Z_FAR_FIRST = (4, 3, 5, 2, 6, 1, 7)


def fiota(shape, dim):
    return lax.broadcasted_iota(jnp.int32, shape, dim).astype(F32)


def fdiv(x, by):
    return jnp.floor((x + 0.5) * (1.0 / by))


def fmod(x, by):
    return x - by * fdiv(x, by)


def dot(a, b):
    return lax.dot_general(a, b, (((1,), (0,)), ((), ())), preferred_element_type=F32)


def dot_nt(a, b):
    return lax.dot_general(a, b, (((1,), (1,)), ((), ())), preferred_element_type=F32)


def split(x):
    high = x.astype(BF16)
    return high, (x - high.astype(F32)).astype(BF16)


def column(row, picked):
    n = row.shape[1]
    rows = picked.shape[0]
    hit = fiota((rows, n), 1) == picked
    return jnp.sum(jnp.where(hit, jnp.broadcast_to(row, (rows, n)), 0.0), axis=1, keepdims=True)


def as_row(col):
    hit = fiota((GRID, 128), 1) == fiota((GRID, 128), 0)
    return jnp.sum(jnp.where(hit, jnp.broadcast_to(col, (GRID, 128)), 0.0), axis=0, keepdims=True)


def trig(waves, first):
    lons = first + fiota((1, LANES), 1)
    turns = waves * lons
    quarter = jnp.floor(turns * (4.0 / NLON) + 0.5)
    rest = turns - quarter * (NLON / 4.0)
    t = rest * (6.283185307179586 / NLON)
    t2 = t * t
    sine = t * (1.0 + t2 * (-1.6666667e-1 + t2 * (8.3333333e-3 + t2 * (-1.9841270e-4 + t2 * 2.7557319e-6))))
    cosine = 1.0 + t2 * (-0.5 + t2 * (4.1666667e-2 + t2 * (-1.3888889e-3 + t2 * 2.4801587e-5)))
    which = quarter.astype(jnp.int32) & 3
    swap = (which & 1) == 1
    c = jnp.where(swap, sine, cosine)
    s = jnp.where(swap, cosine, sine)
    c = jnp.where((which == 1) | (which == 2), -c, c)
    s = jnp.where(which >= 2, s, -s)
    return c, s


def step_field(level, wind, up, down, at_pole, at_equator, east, west, zonal, weight, roll):
    lane = fiota((40, LANES), 1)
    wide = jnp.where(lane == 160.0, east, jnp.where(lane == 255.0, west, level))
    eastward = roll(wide, LANES - 1, 1)
    westward = roll(wide, 1, 1)
    last = level[32:40]
    row8 = fiota((8, LANES), 0)
    swapped = jnp.where(row8 == 0.0, roll(last, 1, 0), roll(last, 3, 0))
    down = jnp.where(at_equator, swapped, down)
    up = jnp.where(at_pole, 0.0, up)
    tall = jnp.concatenate([up, level, down], axis=0)
    toward = roll(tall, 54, 0)[8:48]
    poleward = roll(tall, 2, 0)[8:48]
    change = wind[0] * zonal * (eastward - westward) + 0.25 * wind[1] * (toward - poleward)
    return (level - change) * weight


def row_codes():
    r = fiota((384, 1), 0)
    parity = fdiv(r, 192.0)
    r1 = fmod(r, 192.0)
    h = fdiv(r1, 96.0)
    c = fdiv(fmod(r1, 96.0), 48.0)
    r2 = fmod(r1, 48.0)
    group = fdiv(r2, 16.0)
    level = fdiv(fmod(r2, 16.0), 8.0)
    pair = group * 8.0 + fmod(r2, 8.0)
    slot = jnp.where(pair < 20.0, 2.0 * pair + parity, -1.0)
    return slot, c, level, h


def select_rows():
    slot, c, level, h = row_codes()
    lane = fiota((1, 2 * SLOTS), 1)
    hit = (slot == fmod(lane, 40.0)) & (c == fdiv(lane, 40.0))
    return jnp.where(hit, 1.0, 0.0).astype(BF16)


def select_rows_t():
    r = fiota((1, 384), 1)
    parity = fdiv(r, 192.0)
    r1 = fmod(r, 192.0)
    c = fdiv(fmod(r1, 96.0), 48.0)
    r2 = fmod(r1, 48.0)
    pair = fdiv(r2, 16.0) * 8.0 + fmod(r2, 8.0)
    slot = jnp.where(pair < 20.0, 2.0 * pair + parity, -1.0)
    row = fiota((2 * SLOTS, 1), 0)
    hit = (slot == fmod(row, 40.0)) & (c == fdiv(row, 40.0))
    return jnp.where(hit, 1.0, 0.0).astype(BF16)


def spread_rows():
    g = fiota((128, 1), 0)
    lane = fiota((1, K), 1)
    hit = (fdiv(fmod(g, 40.0), 2.0) == fdiv(lane, 40.0)) & (g < 80.0)
    return jnp.where(hit, 1.0, 0.0).astype(BF16)


def level_mask():
    slot, c, level, h = row_codes()
    g = fiota((1, 128), 1)
    hit = (level == fdiv(g, 40.0)) & (h == fmod(g, 2.0)) & (g < 80.0)
    return hit


def slot_lanes():
    return fmod(fiota((1, K), 1), 40.0)


def reverse_matrix():
    n = fiota((M, M), 0)
    j = fiota((M, M), 1)
    hit = (n + j == M - 2.0) | (n + j == 2.0 * M - 2.0)
    return jnp.where(hit, 1.0, 0.0).astype(BF16)


def first_wave(waves, lon):
    r = fiota((64, 1), 0)
    pair = fdiv(r, 16.0) * 8.0 + fmod(r, 8.0)
    picked = jnp.where(pair < 20.0, lon * 40.0 + 2.0 * pair, -1.0)
    return column(waves, picked)


def parity_sign(first):
    j = fiota((PACK, M), 1)
    odd = (j - first).astype(jnp.int32) & 1
    return jnp.where(odd == 1, -1.0, 1.0)


def spread_weighted(weighted, selector, spreader):
    chosen = dot(selector, weighted)
    chosen = jnp.where(level_mask(), chosen, 0.0).astype(BF16)
    wide = dot(chosen, spreader)
    slot = row_codes()[0]
    return jnp.where(slot == slot_lanes(), wide, 0.0).astype(BF16)


def pack(even, odd, sign, first, c):
    lo = c * PACK
    hi = 96 + c * PACK
    kept = fiota((PACK, M), 1) >= first
    from_odd = odd[lo:lo + PACK] - sign * odd[hi:hi + PACK]
    packed = jnp.where(kept, even[lo:lo + PACK] + sign * even[hi:hi + PACK], from_odd)
    return packed, from_odd[:, M - 1:M]


def correct(total, first, lane0, extra, damping, vertical):
    j = lane0 + fiota((8, 128), 1)
    n = jnp.where(j >= first, j, (M - 2.0) - j)
    n = jnp.where(extra, M - 1.0, n)
    square = n * (n + 1.0) / float(M * M)
    raw = (total[0:8], total[8:16])
    modal = [
        (vertical[k][0] * raw[0] + vertical[k][1] * raw[1]) / (1.0 + damping[k] * square)
        for k in range(2)
    ]
    return jnp.concatenate(
        [vertical[0][l] * modal[0] + vertical[1][l] * modal[1] for l in range(2)], axis=0
    )


def unpack(packed, extra, first):
    j = fiota((PACK, M), 1)
    kept = j >= first
    even = jnp.where(kept, packed, 0.0)
    odd = jnp.where(j == M - 1.0, extra, jnp.where(kept, 0.0, packed))
    return even, odd


def spectrum_rows(even, odd, lat):
    r = fiota((32, 1), 0)
    n = jnp.where(r < ROWS, lat * ROWS + r, -5.0)
    j = fiota((1, M), 1)
    want_even = jnp.where(n == j, 1.0, 0.0).astype(BF16)
    want_odd = jnp.where((n + j == M - 2.0) | (n + j == 2.0 * M - 2.0), 1.0, 0.0).astype(BF16)
    q = fiota((96, 1), 0)
    c = fdiv(q, 48.0)
    q1 = fmod(q, 48.0)
    level = fdiv(fmod(q1, 16.0), 8.0)
    pair = fdiv(q1, 16.0) * 8.0 + fmod(q1, 8.0)
    lane = fiota((1, 160), 1)
    same = (c == fdiv(lane, 80.0)) & (level == fdiv(fmod(lane, 80.0), 40.0)) & (pair < 20.0)
    slot = fmod(lane, 40.0)
    to_even = jnp.where(same & (slot == 2.0 * pair), 1.0, 0.0).astype(BF16)
    to_odd = jnp.where(same & (slot == 2.0 * pair + 1.0), 1.0, 0.0).astype(BF16)
    return dot(dot_nt(want_even, even).astype(BF16), to_even) + dot(
        dot_nt(want_odd, odd).astype(BF16), to_odd
    )


def collapse(x_even, x_odd, selector_t, spreader):
    both = jnp.concatenate([x_even, x_odd], axis=0)
    slot = row_codes()[0]
    both = jnp.where(slot == slot_lanes(), both, 0.0).astype(BF16)
    rows = dot_nt(both, spreader)
    rows = jnp.where(level_mask(), rows, 0.0).astype(BF16)
    return dot(selector_t, rows).astype(BF16)


def kernel(
    level_hbm, wind_hbm, zonal_hbm, weight_hbm, leg_hbm, wave_hbm, damp_hbm, vert_hbm,
    grid_ref, spec_ref,
    native, zonal_ref, weight_ref, leg_ref, wave_ref, damp_ref, vert_ref,
    field_ref, field_near, column_out, column_in, edge_in, own_block, near_block, wave_col,
    table_hi, table_lo, near_hi, near_lo, reversed_ref, part_out, part_in, spread_ref,
    packed_ref, core_in, sum_out, sum_in, first_ref, gathered, coefs,
    load_sem, edge_send, edge_recv, near_send, near_recv, part_send, part_recv, core_send,
    core_recv, sum_send, sum_recv, all_send, all_recv, pair_send, pair_recv, coef_send,
    coef_recv, fwd_send, fwd_recv, heard,
):
    lat = lax.axis_index("lat")
    lon = lax.axis_index("lon")
    chip = lat // 2
    core = lat % 2
    x_lo = lon // 8
    z = lon % 8
    lat_next, lat_prev = (lat + 1) % 32, (lat + 31) % 32
    lon_next, lon_prev = (lon + 1) % 16, (lon + 15) % 16
    near = (lon + 8) % 16
    sibling = chip * 2 + 1 - core
    flat = lat.astype(F32)
    flon = lon.astype(F32)

    def chip_at(offset):
        return (chip // 8 * 8 + offset // 8 * 8) % CHIPS + (chip + offset) % 8

    def y_at(offset):
        return ((chip // 8) * 8 + (chip + offset) % 8) * 2 + core

    def tell(sem, device):
        pl.semaphore_signal(sem, inc=1, device_id=device, device_id_type=MESH)

    def z_at(offset):
        return (z + offset) % 8

    def send(src, dst, send_sem, recv_sem, device):
        copy = pltpu.make_async_remote_copy(
            src_ref=src, dst_ref=dst, send_sem=send_sem, recv_sem=recv_sem,
            device_id=device, device_id_type=MESH,
        )
        copy.start()
        return copy

    def roll(x, amount, axis):
        return pltpu.roll(x, amount, axis)

    barrier = pltpu.get_barrier_semaphore()

    def greet(device):
        pl.semaphore_signal(barrier, inc=1, device_id=device, device_id_type=MESH)

    loads = [
        pltpu.make_async_copy(src, dst, load_sem.at[n])
        for n, (src, dst) in enumerate((
            (level_hbm, native.at[0]), (wind_hbm, native.at[1]), (wave_hbm, wave_ref),
            (zonal_hbm, zonal_ref), (weight_hbm, weight_ref), (damp_hbm, damp_ref),
            (vert_hbm, vert_ref), (leg_hbm, leg_ref),
        ))
    ]
    for copy in loads:
        copy.start()

    across = ((chip + 8) % CHIPS * 2 + core, lon)
    greet(across)
    for step in (1, 7):
        greet((y_at(step), lon))

    @pl.loop(1, 8)
    def _(o):
        greet((lat, x_lo * 8 + z_at(o)))

    edge_devices = (
        ((lat_next, lon), 0, 0), ((lat_prev, lon), 0, 1), ((lat_next, near), 1, 0), ((lat_prev, near), 1, 1),
        ((lat, lon_prev), 0, 0), ((lat, lon_next), 0, 1),
        ((lat, (lon_prev + 8) % 16), 1, 0), ((lat, (lon_next + 8) % 16), 1, 1),
    )
    for device, _, _ in edge_devices:
        greet(device)
    greet((lat, near))

    for copy in loads[:7]:
        copy.wait()

    field_ref[:, :, 128:LANES] = jnp.zeros((4, 40, 128), F32)
    for a in range(2):
        for b in range(2):
            for i in range(ROWS):
                field_ref[2 * a + b, 2 * i:2 * i + 2, 0:160] = native[a, b, i]

    flat_level = jnp.reshape(field_ref[0:2], (GRID, LANES))
    column_out[0] = jnp.broadcast_to(as_row(flat_level[:, 0:1]), (8, 128))
    column_out[1] = jnp.broadcast_to(as_row(flat_level[:, 159:160]), (8, 128))
    waves = wave_ref[...].astype(F32)
    waves = [waves[t:t + 1, :] for t in range(5)]
    for t in range(5):
        wave_col[128 * t:128 * (t + 1), :] = jnp.broadcast_to(waves[t], (128, 128)).T
    waves = jnp.concatenate(waves, axis=1)
    first_ref[...] = jnp.broadcast_to(first_wave(waves, flon), (64, 128))

    def fill(source, hi, lo, at, first):
        w = wave_col[pl.ds(pl.multiple_of(source * SLOTS, 8), SLOTS), 0:1]
        c, s = trig(w, first)
        high, low = split(jnp.concatenate([c, s], axis=0))
        hi[at] = high
        lo[at] = low

    near_first = near.astype(F32) * 160.0

    @pl.loop(0, 8)
    def _(zz):
        fill(x_lo * 8 + zz, table_hi, table_lo, x_lo * 8 + zz, flon * 160.0)
        fill(x_lo * 8 + zz, near_hi, near_lo, zz, near_first)

    pl.semaphore_wait(barrier, 3 + 7 + 9)

    to_near = send(field_ref, field_near, near_send, near_recv, (lat, near))
    edges = []
    for n, (device, block, side) in enumerate(edge_devices):
        if n < 4:
            src = field_ref.at[0:2, 32:40, :] if side == 0 else field_ref.at[0:2, 0:8, :]
            dst = edge_in.at[block, side]
        else:
            src, dst = column_out.at[side], column_in.at[block, side]
        edges.append(send(src, dst, edge_send.at[n], edge_recv.at[n], device))

    for step in (1, 7):
        tell(heard.at[0], (y_at(step), lon))

    picked = fdiv(fiota((40, 1), 0), 2.0)
    zonal = column(zonal_ref[...], picked)
    weight = column(weight_ref[...], picked) * (1.0 / float(NLON) ** 0.5)
    g = fiota((40, 1), 0)
    own_block[80:128, :] = jnp.zeros((48, LANES), F32)
    near_block[80:128, :] = jnp.zeros((48, LANES), F32)
    first = first_ref[0:PACK, 0:1]
    sign = parity_sign(first)
    selector, spreader = select_rows(), spread_rows()

    for copy in edges:
        copy.wait()
    to_near.wait()

    pl.semaphore_wait(heard.at[0], 2)
    for step in (2, 6):
        tell(heard.at[1], (y_at(step), lon))

    def advance(block, field, out):
        for l in range(2):
            east = column(column_in[block, 0, 0:1, :], g + 40.0 * l)
            west = column(column_in[block, 1, 0:1, :], g + 40.0 * l)
            out[40 * l:40 * (l + 1), :] = step_field(
                field[l], (field[2], field[3]), edge_in[block, 0, l], edge_in[block, 1, l],
                lat == 0, lat == 31, east, west, zonal, weight, roll,
            )

    advance(0, field_ref, own_block)
    advance(1, field_near, near_block)

    def wide(ref):
        return jnp.reshape(ref[...], (8 * 80, LANES))

    own_hi, own_lo = split(own_block[...])
    near_h, near_l = split(near_block[...])
    mine = pl.ds(x_lo * 8, 8)
    t_hi = jnp.reshape(table_hi[mine], (640, LANES))
    t_lo = jnp.reshape(table_lo[mine], (640, LANES))
    n_hi, n_lo = wide(near_hi), wide(near_lo)
    partial = dot_nt(t_hi, own_hi) + dot_nt(t_hi, own_lo) + dot_nt(t_lo, own_hi)
    partial = partial + dot_nt(n_hi, near_h) + dot_nt(n_hi, near_l) + dot_nt(n_lo, near_h)
    part_out[...] = jnp.reshape(partial, (8, 80, 128))

    def part_copy(o):
        other = z_at(o)
        return pltpu.make_async_remote_copy(
            src_ref=part_out.at[other], dst_ref=part_in.at[z], send_sem=part_send.at[o],
            recv_sem=part_recv.at[z], device_id=(lat, x_lo * 8 + other), device_id_type=MESH,
        )

    for o in Z_FAR_FIRST:
        part_copy(o).start()

    pl.semaphore_wait(heard.at[1], 2)
    tell(heard.at[2], across)
    part_in[z] = part_out[z]
    loads[7].wait()
    leg = leg_ref[...]
    reversed_ref[...] = dot(leg, reverse_matrix()).astype(BF16)

    @pl.loop(1, 8)
    def _(o):
        other = z_at(o)
        pltpu.make_async_remote_copy(
            src_ref=part_out.at[other], dst_ref=part_in.at[other], send_sem=part_send.at[o],
            recv_sem=part_recv.at[other], device_id=(lat, x_lo * 8 + other), device_id_type=MESH,
        ).wait_recv()

    weighted = jnp.sum(part_in[...], axis=0).astype(BF16)
    spread_ref[...] = spread_weighted(weighted, selector, spreader)
    even = dot(spread_ref[0:192], leg)
    odd = dot(spread_ref[192:384], reversed_ref[...])
    lane128 = fiota((16, 128), 1)
    for c in range(2):
        packed, extra = pack(even, odd, sign, first, c)
        rest = jnp.zeros((16, 128), F32)
        for kb in range(3):
            for t in range(5):
                packed_ref[c, kb * 5 + t] = packed[16 * kb:16 * (kb + 1), 128 * t:128 * (t + 1)]
            rest = jnp.where(lane128 == float(kb), extra[16 * kb:16 * (kb + 1)], rest)
        packed_ref[c, 15] = rest

    to_core = send(packed_ref.at[1 - core], core_in, core_send, core_recv, (sibling, lon))
    to_core.wait()
    sum_out[...] = packed_ref[core] + core_in[...]
    pl.semaphore_wait(heard.at[2], 1)

    def sum_copy(o):
        other = chip_at(o)
        return pltpu.make_async_remote_copy(
            src_ref=sum_out.at[other], dst_ref=sum_in.at[chip], send_sem=sum_send.at[o],
            recv_sem=sum_recv.at[chip], device_id=(other * 2 + core, lon), device_id_type=MESH,
        )

    for o in FAR_FIRST:
        sum_copy(o).start()

    sum_in[chip] = sum_out[chip]

    @pl.loop(0, 8)
    def _(zz):
        source = (1 - x_lo) * 8 + zz
        fill(source, table_hi, table_lo, source, flon * 160.0)


    @pl.loop(1, CHIPS)
    def _(o):
        other = chip_at(o)
        pltpu.make_async_remote_copy(
            src_ref=sum_out.at[other], dst_ref=sum_in.at[other], send_sem=sum_send.at[o],
            recv_sem=sum_recv.at[other], device_id=(other * 2 + core, lon), device_id_type=MESH,
        ).wait_recv()

    total = jnp.sum(sum_in[...], axis=0)
    damping = (damp_ref[0], damp_ref[1])
    vertical = ((vert_ref[0, 0], vert_ref[0, 1]), (vert_ref[1, 0], vert_ref[1, 1]))
    first8 = first_ref[pl.ds(pl.multiple_of((chip // 5) * 16, 8), 8), 0:1]
    lane0 = ((chip % 5) * 128).astype(F32)
    spec = correct(total, first8, lane0, chip == 15, damping, vertical)
    gathered[core, chip] = spec.astype(BF16)

    def all_copy(o):
        return pltpu.make_async_remote_copy(
            src_ref=gathered.at[core, chip], dst_ref=gathered.at[core, chip], send_sem=all_send.at[o],
            recv_sem=all_recv.at[chip], device_id=(chip_at(o) * 2 + core, lon), device_id_type=MESH,
        )

    for o in FAR_FIRST:
        all_copy(o).start()

    @pl.loop(1, CHIPS)
    def _(o):
        other = chip_at(o)
        pltpu.make_async_remote_copy(
            src_ref=gathered.at[core, other], dst_ref=gathered.at[core, other], send_sem=all_send.at[o],
            recv_sem=all_recv.at[other], device_id=(other * 2 + core, lon), device_id_type=MESH,
        ).wait_recv()

    to_pair = send(gathered.at[core], gathered.at[core], pair_send, pair_recv, (sibling, lon))
    to_pair.wait()

    evens, odds = [], []
    for c in range(2):
        tiles = [[gathered[c, kb * 5 + t].astype(F32) for t in range(5)] for kb in range(3)]
        packed = jnp.concatenate([jnp.concatenate(row, axis=1) for row in tiles], axis=0)
        last = gathered[c, 15].astype(F32)
        extra = jnp.concatenate([last[:, kb:kb + 1] for kb in range(3)], axis=0)
        e, o = unpack(packed, extra, first)
        evens.append(e)
        odds.append(o)
    scale_even = jnp.where(first == 0.0, 1.0, 2.0)
    scale_odd = jnp.where(first == M - 1.0, 1.0, 2.0)
    north_e = [e * scale_even for e in evens]
    north_o = [o * scale_odd for o in odds]
    rows_e = jnp.concatenate(north_e + [e * sign for e in north_e], axis=0).astype(BF16)
    rows_o = jnp.concatenate(north_o + [-(o * sign) for o in north_o], axis=0).astype(BF16)
    x_even = dot_nt(rows_e, leg)
    x_odd = dot_nt(rows_o, reversed_ref[...])
    coefs[lon] = collapse(x_even, x_odd, select_rows_t(), spreader)

    def coef_copy(o):
        return pltpu.make_async_remote_copy(
            src_ref=coefs.at[lon], dst_ref=coefs.at[lon], send_sem=coef_send.at[o],
            recv_sem=coef_recv.at[z], device_id=(lat, x_lo * 8 + z_at(o)), device_id_type=MESH,
        )

    def forward_copy(source):
        at = x_lo * 8 + source
        return pltpu.make_async_remote_copy(
            src_ref=coefs.at[at], dst_ref=coefs.at[at], send_sem=fwd_send.at[source],
            recv_sem=fwd_recv.at[source], device_id=(lat, near), device_id_type=MESH,
        )

    forward_copy(z).start()

    for o in Z_FAR_FIRST:
        coef_copy(o).start()

    evens = jnp.concatenate(evens, axis=0).astype(BF16)
    odds = jnp.concatenate(odds, axis=0).astype(BF16)
    spec_ref[...] = spectrum_rows(evens, odds, flat)

    @pl.loop(1, 8)
    def _(o):
        other = z_at(o)
        at = x_lo * 8 + other
        pltpu.make_async_remote_copy(
            src_ref=coefs.at[at], dst_ref=coefs.at[at], send_sem=coef_send.at[o],
            recv_sem=coef_recv.at[other], device_id=(lat, at), device_id_type=MESH,
        ).wait_recv()
        forward_copy(other).start()

    def inverse(half):
        rows = pl.ds(half * 8, 8)
        values = jnp.reshape(coefs[rows], (640, 128)).T
        return dot(values, jnp.reshape(table_hi[rows], (640, LANES))) + dot(
            values, jnp.reshape(table_lo[rows], (640, LANES))
        )

    grid = inverse(x_lo)

    @pl.loop(0, 8)
    def _(source):
        at = (1 - x_lo) * 8 + source
        pltpu.make_async_remote_copy(
            src_ref=coefs.at[at], dst_ref=coefs.at[at], send_sem=fwd_send.at[source],
            recv_sem=fwd_recv.at[source], device_id=(lat, near), device_id_type=MESH,
        ).wait_recv()

    grid = grid + inverse(1 - x_lo)
    grid_ref[...] = grid[0:GRID] * (1.0 / float(NLON * M) ** 0.5)

    @pl.loop(1, 8)
    def _(o):
        part_copy(o).wait_send()
        coef_copy(o).wait_send()

    @pl.loop(0, 8)
    def _(source):
        forward_copy(source).wait_send()

    @pl.loop(1, CHIPS)
    def _(o):
        sum_copy(o).wait_send()
        all_copy(o).wait_send()


def shards(level_fields, wind_field, zonal_step, quad_weight, legendre, wave_table, damping, vertical):
    def rows(x):
        return x.transpose(0, 2, 1, 3)

    vmem = pl.BlockSpec(memory_space=pltpu.VMEM)
    hbm = pl.BlockSpec(memory_space=pl.ANY)
    dma = pltpu.SemaphoreType.DMA
    grid, spec = pl.pallas_call(
        kernel,
        out_shape=(
            jax.ShapeDtypeStruct((GRID, LANES), F32),
            jax.ShapeDtypeStruct((32, 160), F32),
        ),
        in_specs=[hbm] * 8,
        out_specs=(vmem, vmem),
        scratch_shapes=[
            pltpu.VMEM((2, 2, ROWS, 2, 160), F32),
            pltpu.VMEM((1, ROWS), F32),
            pltpu.VMEM((1, ROWS), F32),
            pltpu.VMEM((K, M), BF16),
            pltpu.VMEM((5, 128), jnp.int32),
            pltpu.SMEM((2,), F32),
            pltpu.SMEM((2, 2), F32),
            pltpu.VMEM((4, 40, LANES), F32),
            pltpu.VMEM((4, 40, LANES), F32),
            pltpu.VMEM((2, 8, 128), F32),
            pltpu.VMEM((2, 2, 8, 128), F32),
            pltpu.VMEM((2, 2, 2, 8, LANES), F32),
            pltpu.VMEM((128, LANES), F32),
            pltpu.VMEM((128, LANES), F32),
            pltpu.VMEM((M, 128), F32),
            pltpu.VMEM((16, 80, LANES), BF16),
            pltpu.VMEM((16, 80, LANES), BF16),
            pltpu.VMEM((8, 80, LANES), BF16),
            pltpu.VMEM((8, 80, LANES), BF16),
            pltpu.VMEM((K, M), BF16),
            pltpu.VMEM((8, 80, 128), F32),
            pltpu.VMEM((8, 80, 128), F32),
            pltpu.VMEM((384, K), BF16),
            pltpu.VMEM((2, BLOCKS, 16, 128), F32),
            pltpu.VMEM((BLOCKS, 16, 128), F32),
            pltpu.VMEM((BLOCKS, 16, 128), F32),
            pltpu.VMEM((CHIPS, 16, 128), F32),
            pltpu.VMEM((64, 128), F32),
            pltpu.VMEM((2, BLOCKS, 16, 128), BF16),
            pltpu.VMEM((16, 80, 128), BF16),
            dma((8,)), dma((8,)), dma((8,)), dma, dma, dma((8,)), dma((8,)), dma, dma,
            dma((CHIPS,)), dma((CHIPS,)), dma((CHIPS,)), dma((CHIPS,)), dma, dma,
            dma((8,)), dma((8,)), dma((8,)), dma((8,)),
            pltpu.SemaphoreType.REGULAR((3,)),
        ],
        compiler_params=pltpu.CompilerParams(
            collective_id=0, has_side_effects=True, vmem_limit_bytes=60 * 1024 * 1024
        ),
    )(
        rows(level_fields), rows(wind_field), zonal_step[None], quad_weight[None],
        legendre.transpose(1, 0, 2).reshape(K, M), wave_table.reshape(5, 128), damping, vertical,
    )
    fields = grid[:, :160].reshape(2, ROWS, 2, 160).transpose(0, 2, 1, 3)
    spectrum = spec[:ROWS].reshape(ROWS, 2, 2, SLOTS).transpose(0, 3, 1, 2)
    return fields, spectrum


def solution(mesh):
    return jax.shard_map(
        shards,
        mesh=mesh,
        in_specs=(
            P(None, None, "lat", "lon"),
            P(None, None, "lat", "lon"),
            P("lat"),
            P("lat"),
            P("lon", "lat", None),
            P(),
            P(),
            P(),
        ),
        out_specs=(P(None, None, "lat", "lon"), P("lat", "lon", None, None)),
        check_vma=False,
    )
```

```python
import functools

import jax
import jax.numpy as jnp
from jax import lax
from jax.experimental import pallas as pl
from jax.experimental.pallas import tpu as pltpu
from jax.sharding import PartitionSpec as P

NLON = 2560
M = 640
ROWS = 20
GRID = 80
SLOTS = 40
LANES = 256
K = ROWS * SLOTS
CHIPS = 16
BLOCKS = 16
PACK = 48
FOLDED = 56
FOLDED16 = 64
F32 = jnp.float32
BF16 = jnp.bfloat16
MESH = pl.DeviceIdType.MESH
FAR_FIRST = (12, 11, 13, 4, 10, 14, 3, 5, 9, 15, 8, 2, 6, 1, 7)
Z_FAR_FIRST = (4, 3, 5, 2, 6, 1, 7)


def fiota(shape, dim):
    return lax.broadcasted_iota(jnp.int32, shape, dim).astype(F32)


def fdiv(x, by):
    return jnp.floor((x + 0.5) * (1.0 / by))


def fmod(x, by):
    return x - by * fdiv(x, by)


def dot(a, b):
    return lax.dot_general(a, b, (((1,), (0,)), ((), ())), preferred_element_type=F32)


def dot_nt(a, b):
    return lax.dot_general(a, b, (((1,), (1,)), ((), ())), preferred_element_type=F32)


def split(x):
    high = x.astype(BF16)
    return high, (x - high.astype(F32)).astype(BF16)


def column(row, picked):
    n = row.shape[1]
    rows = picked.shape[0]
    hit = fiota((rows, n), 1) == picked
    return jnp.sum(jnp.where(hit, jnp.broadcast_to(row, (rows, n)), 0.0), axis=1, keepdims=True)


def as_row(col):
    hit = fiota((GRID, 128), 1) == fiota((GRID, 128), 0)
    return jnp.sum(jnp.where(hit, jnp.broadcast_to(col, (GRID, 128)), 0.0), axis=0, keepdims=True)


def trig(waves, first):
    lons = first + fiota((1, LANES), 1)
    turns = waves * lons
    quarter = jnp.floor(turns * (4.0 / NLON) + 0.5)
    rest = turns - quarter * (NLON / 4.0)
    t = rest * (6.283185307179586 / NLON)
    t2 = t * t
    sine = t * (1.0 + t2 * (-1.6666667e-1 + t2 * (8.3333333e-3 + t2 * (-1.9841270e-4 + t2 * 2.7557319e-6))))
    cosine = 1.0 + t2 * (-0.5 + t2 * (4.1666667e-2 + t2 * (-1.3888889e-3 + t2 * 2.4801587e-5)))
    which = quarter.astype(jnp.int32) & 3
    swap = (which & 1) == 1
    c = jnp.where(swap, sine, cosine)
    s = jnp.where(swap, cosine, sine)
    c = jnp.where((which == 1) | (which == 2), -c, c)
    s = jnp.where(which >= 2, s, -s)
    return c, s


def step_field(level, wind, up, down, at_pole, at_equator, east, west, zonal, weight, roll):
    lane = fiota((40, LANES), 1)
    wide = jnp.where(lane == 160.0, east, jnp.where(lane == 255.0, west, level))
    eastward = roll(wide, LANES - 1, 1)
    westward = roll(wide, 1, 1)
    last = level[32:40]
    row8 = fiota((8, LANES), 0)
    swapped = jnp.where(row8 == 0.0, roll(last, 1, 0), roll(last, 3, 0))
    down = jnp.where(at_equator, swapped, down)
    up = jnp.where(at_pole, 0.0, up)
    tall = jnp.concatenate([up, level, down], axis=0)
    toward = roll(tall, 54, 0)[8:48]
    poleward = roll(tall, 2, 0)[8:48]
    change = wind[0] * zonal * (eastward - westward) + 0.25 * wind[1] * (toward - poleward)
    return (level - change) * weight


def row_codes(r):
    parity = fdiv(r, 192.0)
    r1 = fmod(r, 192.0)
    h = fdiv(r1, 96.0)
    c = fdiv(fmod(r1, 96.0), 48.0)
    r2 = fmod(r1, 48.0)
    group = fdiv(r2, 16.0)
    level = fdiv(fmod(r2, 16.0), 8.0)
    pair = group * 8.0 + fmod(r2, 8.0)
    slot = jnp.where(pair < 20.0, 2.0 * pair + parity, -1.0)
    return slot, c, level, h


def folded_rows(slot, c):
    rest = 40.0 + fmod(slot, 8.0) + 8.0 * fdiv(slot, 32.0)
    return slot, jnp.where((c == 1.0) & (slot >= 0.0), rest, -1.0)


def select_rows():
    slot, c, level, h = row_codes(fiota((384, 1), 0))
    lane = fiota((1, FOLDED), 1)
    return tuple(jnp.where(r == lane, 1.0, 0.0).astype(BF16) for r in folded_rows(slot, c))


def select_rows_t():
    slot, c, level, h = row_codes(fiota((1, 384), 1))
    row = fiota((FOLDED16, 1), 0)
    return tuple(jnp.where(r == row, 1.0, 0.0).astype(BF16) for r in folded_rows(slot, c))


def spread_rows():
    lane = fiota((256, 1), 0)
    g = jnp.where(lane < 80.0, lane, jnp.where(lane < 128.0, lane - 80.0, 48.0 + fmod(lane, 32.0)))
    hit = fdiv(fmod(g, 40.0), 2.0) == fdiv(fiota((1, K), 1), 40.0)
    return jnp.where(hit, 1.0, 0.0).astype(BF16)


def level_mask():
    slot, c, level, h = row_codes(fiota((384, 1), 0))
    lane = fiota((1, 256), 1)
    rest = lane >= 128.0
    g = jnp.where(lane < 80.0, lane, jnp.where(rest, 48.0 + fmod(lane, 32.0), lane - 80.0))
    part = jnp.where(lane < 80.0, 0.0, 1.0)
    group = jnp.where(rest, fdiv(lane - 128.0, 32.0), fmod(fdiv(slot, 8.0), 4.0))
    return (
        (level == fdiv(g, 40.0)) & (h == fmod(g, 2.0)) & (c == part)
        & (group == fmod(fdiv(slot, 8.0), 4.0))
    )


def fold(cosine, sine):
    n = cosine.shape[0] // SLOTS
    lane = fiota((1, 1, 128), 2)
    cosine = jnp.reshape(cosine, (n, SLOTS, 128))
    sine = jnp.reshape(sine, (n, SLOTS, 128))
    main = jnp.where(lane < 80.0, cosine, sine)
    rest = jnp.where(lane < 32.0, sine, 0.0)
    first = rest[:, 0:8]
    for b in range(1, 4):
        moved = pltpu.roll(jnp.reshape(rest[:, 8 * b:8 * b + 8], (8 * n, 128)), 32 * b, 1)
        first = first + jnp.reshape(moved, (n, 8, 128))
    return main, first, rest[:, 32:40]


def unfold(folded):
    n = folded.shape[0]
    lane = fiota((1, 1, 128), 2)
    main = folded[:, 0:40]
    first = jnp.reshape(folded[:, 40:48], (8 * n, 128))
    parts = [folded[:, 40:48]]
    for b in range(1, 4):
        parts.append(jnp.reshape(pltpu.roll(first, 128 - 32 * b, 1), (n, 8, 128)))
    parts.append(folded[:, 48:56])
    rest = jnp.concatenate(parts, axis=1)
    cosine = jnp.where(lane < 80.0, main, 0.0)
    sine = jnp.where(lane < 32.0, rest, jnp.where(lane < 80.0, 0.0, main))
    return jnp.reshape(cosine, (n * SLOTS, 128)), jnp.reshape(sine, (n * SLOTS, 128))


def slot_lanes():
    return fmod(fiota((1, K), 1), 40.0)


def reverse_matrix():
    n = fiota((M, M), 0)
    j = fiota((M, M), 1)
    hit = (n + j == M - 2.0) | (n + j == 2.0 * M - 2.0)
    return jnp.where(hit, 1.0, 0.0).astype(BF16)


def first_wave(waves, lon):
    r = fiota((64, 1), 0)
    pair = fdiv(r, 16.0) * 8.0 + fmod(r, 8.0)
    picked = jnp.where(pair < 20.0, lon * 40.0 + 2.0 * pair, -1.0)
    return column(waves, picked)


def parity_sign(first):
    j = fiota((PACK, M), 1)
    odd = (j - first).astype(jnp.int32) & 1
    return jnp.where(odd == 1, -1.0, 1.0)


def spread_weighted(weighted, selector, spreader):
    chosen = jnp.concatenate([dot(q, weighted) for q in selector], axis=1)
    chosen = jnp.where(level_mask(), chosen, 0.0).astype(BF16)
    wide = dot(chosen, spreader)
    slot = row_codes(fiota((384, 1), 0))[0]
    return jnp.where(slot == slot_lanes(), wide, 0.0).astype(BF16)


def pack(even, odd, sign, first, c):
    lo = c * PACK
    hi = 96 + c * PACK
    kept = fiota((PACK, M), 1) >= first
    from_odd = odd[lo:lo + PACK] - sign * odd[hi:hi + PACK]
    packed = jnp.where(kept, even[lo:lo + PACK] + sign * even[hi:hi + PACK], from_odd)
    return packed, from_odd[:, M - 1:M]


def correct(total, first, lane0, extra, damping, vertical):
    j = lane0 + fiota((8, 128), 1)
    n = jnp.where(j >= first, j, (M - 2.0) - j)
    n = jnp.where(extra, M - 1.0, n)
    square = n * (n + 1.0) / float(M * M)
    raw = (total[0:8], total[8:16])
    modal = [
        (vertical[k][0] * raw[0] + vertical[k][1] * raw[1]) / (1.0 + damping[k] * square)
        for k in range(2)
    ]
    return jnp.concatenate(
        [vertical[0][l] * modal[0] + vertical[1][l] * modal[1] for l in range(2)], axis=0
    )


def unpack(packed, extra, first):
    j = fiota((PACK, M), 1)
    kept = j >= first
    even = jnp.where(kept, packed, 0.0)
    odd = jnp.where(j == M - 1.0, extra, jnp.where(kept, 0.0, packed))
    return even, odd


def spectrum_rows(even, odd, lat):
    r = fiota((32, 1), 0)
    n = jnp.where(r < ROWS, lat * ROWS + r, -5.0)
    j = fiota((1, M), 1)
    want_even = jnp.where(n == j, 1.0, 0.0).astype(BF16)
    want_odd = jnp.where((n + j == M - 2.0) | (n + j == 2.0 * M - 2.0), 1.0, 0.0).astype(BF16)
    q = fiota((96, 1), 0)
    c = fdiv(q, 48.0)
    q1 = fmod(q, 48.0)
    level = fdiv(fmod(q1, 16.0), 8.0)
    pair = fdiv(q1, 16.0) * 8.0 + fmod(q1, 8.0)
    lane = fiota((1, 160), 1)
    same = (c == fdiv(lane, 80.0)) & (level == fdiv(fmod(lane, 80.0), 40.0)) & (pair < 20.0)
    slot = fmod(lane, 40.0)
    to_even = jnp.where(same & (slot == 2.0 * pair), 1.0, 0.0).astype(BF16)
    to_odd = jnp.where(same & (slot == 2.0 * pair + 1.0), 1.0, 0.0).astype(BF16)
    return dot(dot_nt(want_even, even).astype(BF16), to_even) + dot(
        dot_nt(want_odd, odd).astype(BF16), to_odd
    )


def collapse(x_even, x_odd, selector_t, spreader):
    both = jnp.concatenate([x_even, x_odd], axis=0)
    slot = row_codes(fiota((384, 1), 0))[0]
    both = jnp.where(slot == slot_lanes(), both, 0.0).astype(BF16)
    rows = dot_nt(both, spreader)
    rows = jnp.where(level_mask(), rows, 0.0).astype(BF16)
    folded = dot(selector_t[0], rows[:, 0:128]) + dot(selector_t[1], rows[:, 128:256])
    return folded.astype(BF16)


def kernel(
    level_hbm, wind_hbm, zonal_hbm, weight_hbm, leg_hbm, wave_hbm, damp_hbm, vert_hbm,
    grid_ref, spec_ref,
    native, zonal_ref, weight_ref, leg_ref, wave_ref, damp_ref, vert_ref,
    field_ref, field_near, column_out, column_in, edge_in, wave_col,
    cos_hi, cos_lo, sin_hi, sin_lo, near_cos_hi, near_cos_lo, near_sin_hi, near_sin_lo, reversed_ref, part_out, part_in, spread_ref,
    packed_ref, core_in, sum_out, sum_in, first_ref, gathered, coefs,
    load_sem, edge_send, edge_recv, near_send, near_recv, part_send, part_recv, core_send,
    core_recv, sum_send, sum_recv, all_send, all_recv, pair_send, pair_recv, coef_send,
    coef_recv, fwd_send, fwd_recv, heard,
):
    lat = lax.axis_index("lat")
    lon = lax.axis_index("lon")
    chip = lat // 2
    core = lat % 2
    x_lo = lon // 8
    z = lon % 8
    lat_next, lat_prev = (lat + 1) % 32, (lat + 31) % 32
    lon_next, lon_prev = (lon + 1) % 16, (lon + 15) % 16
    near = (lon + 8) % 16
    sibling = chip * 2 + 1 - core
    flat = lat.astype(F32)
    flon = lon.astype(F32)

    def chip_at(offset):
        return (chip // 8 * 8 + offset // 8 * 8) % CHIPS + (chip + offset) % 8

    def y_at(offset):
        return ((chip // 8) * 8 + (chip + offset) % 8) * 2 + core

    def tell(sem, device):
        pl.semaphore_signal(sem, inc=1, device_id=device, device_id_type=MESH)

    def z_at(offset):
        return (z + offset) % 8

    def send(src, dst, send_sem, recv_sem, device):
        copy = pltpu.make_async_remote_copy(
            src_ref=src, dst_ref=dst, send_sem=send_sem, recv_sem=recv_sem,
            device_id=device, device_id_type=MESH,
        )
        copy.start()
        return copy

    def roll(x, amount, axis):
        return pltpu.roll(x, amount, axis)

    barrier = pltpu.get_barrier_semaphore()

    def greet(device):
        pl.semaphore_signal(barrier, inc=1, device_id=device, device_id_type=MESH)

    loads = [
        pltpu.make_async_copy(src, dst, load_sem.at[n])
        for n, (src, dst) in enumerate((
            (level_hbm, native.at[0]), (wind_hbm, native.at[1]), (wave_hbm, wave_ref),
            (zonal_hbm, zonal_ref), (weight_hbm, weight_ref), (damp_hbm, damp_ref),
            (vert_hbm, vert_ref), (leg_hbm, leg_ref),
        ))
    ]
    for copy in loads:
        copy.start()

    across = ((chip + 8) % CHIPS * 2 + core, lon)
    greet(across)
    for step in (1, 7):
        greet((y_at(step), lon))

    @pl.loop(1, 8)
    def _(o):
        greet((lat, x_lo * 8 + z_at(o)))

    edge_devices = (
        ((lat_next, lon), 0, 0), ((lat_prev, lon), 0, 1), ((lat_next, near), 1, 0), ((lat_prev, near), 1, 1),
        ((lat, lon_prev), 0, 0), ((lat, lon_next), 0, 1),
        ((lat, (lon_prev + 8) % 16), 1, 0), ((lat, (lon_next + 8) % 16), 1, 1),
    )
    for device, _, _ in edge_devices:
        greet(device)
    greet((lat, near))

    for copy in loads[:7]:
        copy.wait()

    field_ref[:, :, 128:LANES] = jnp.zeros((4, 40, 128), F32)
    for a in range(2):
        for b in range(2):
            for i in range(ROWS):
                field_ref[2 * a + b, 2 * i:2 * i + 2, 0:160] = native[a, b, i]

    flat_level = jnp.reshape(field_ref[0:2], (GRID, LANES))
    column_out[0] = jnp.broadcast_to(as_row(flat_level[:, 0:1]), (8, 128))
    column_out[1] = jnp.broadcast_to(as_row(flat_level[:, 159:160]), (8, 128))
    waves = wave_ref[...].astype(F32)
    waves = [waves[t:t + 1, :] for t in range(5)]
    for t in range(5):
        wave_col[128 * t:128 * (t + 1), :] = jnp.broadcast_to(waves[t], (128, 128)).T
    waves = jnp.concatenate(waves, axis=1)
    first_ref[...] = jnp.broadcast_to(first_wave(waves, flon), (64, 128))

    own_tables = (cos_hi, cos_lo, sin_hi, sin_lo)
    near_tables = (near_cos_hi, near_cos_lo, near_sin_hi, near_sin_lo)

    def fill(source, tables, at, first):
        w = wave_col[pl.ds(pl.multiple_of(source * SLOTS, 80), 2 * SLOTS), 0:1]
        rows = pl.ds(pl.multiple_of(at * SLOTS, 80), 2 * SLOTS)
        c, s = trig(w, first)
        tables[0][rows, :], tables[1][rows, :] = split(c)
        tables[2][rows, :], tables[3][rows, :] = split(s)

    near_first = near.astype(F32) * 160.0

    @pl.loop(0, 4)
    def _(zz):
        source = x_lo * 8 + zz * 2
        fill(source, own_tables, source, flon * 160.0)
        fill(source, near_tables, zz * 2, near_first)

    pl.semaphore_wait(barrier, 3 + 7 + 9)

    to_near = send(field_ref, field_near, near_send, near_recv, (lat, near))
    edges = []
    for n, (device, block, side) in enumerate(edge_devices):
        if n < 4:
            src = field_ref.at[0:2, 32:40, :] if side == 0 else field_ref.at[0:2, 0:8, :]
            dst = edge_in.at[block, side]
        else:
            src, dst = column_out.at[side], column_in.at[block, side]
        edges.append(send(src, dst, edge_send.at[n], edge_recv.at[n], device))

    for step in (1, 7):
        tell(heard.at[0], (y_at(step), lon))

    picked = fdiv(fiota((40, 1), 0), 2.0)
    zonal = column(zonal_ref[...], picked)
    weight = column(weight_ref[...], picked) * (1.0 / float(NLON) ** 0.5)
    g = fiota((40, 1), 0)
    first = first_ref[0:PACK, 0:1]
    sign = parity_sign(first)
    selector, spreader = select_rows(), spread_rows()

    for copy in edges:
        copy.wait()
    to_near.wait()

    pl.semaphore_wait(heard.at[0], 2)
    for step in (2, 6):
        tell(heard.at[1], (y_at(step), lon))

    def advance(block, field):
        levels = []
        for l in range(2):
            east = column(column_in[block, 0, 0:1, :], g + 40.0 * l)
            west = column(column_in[block, 1, 0:1, :], g + 40.0 * l)
            levels.append(step_field(
                field[l], (field[2], field[3]), edge_in[block, 0, l], edge_in[block, 1, l],
                lat == 0, lat == 31, east, west, zonal, weight, roll,
            ))
        return jnp.concatenate(levels, axis=0)

    mine = pl.ds(pl.multiple_of(x_lo * 320, 320), 320)

    def fourier(values, tables, rows):
        zeros = jnp.zeros((48, LANES), F32)
        sums = []
        for part, v in enumerate((
            jnp.concatenate([values, zeros], axis=0),
            jnp.concatenate([values[48:80], zeros, values[0:48]], axis=0),
        )):
            v_hi, v_lo = split(v)
            t_hi, t_lo = tables[2 * part][rows, :], tables[2 * part + 1][rows, :]
            sums.append(dot_nt(t_hi, v_hi) + dot_nt(t_hi, v_lo) + dot_nt(t_lo, v_hi))
        return sums

    own_sums = fourier(advance(0, field_ref), own_tables, mine)
    near_sums = fourier(advance(1, field_near), near_tables, pl.ds(0, 320))
    main, rest, rest2 = fold(*(a + b for a, b in zip(own_sums, near_sums)))
    part_out[:, 0:40, :] = main
    part_out[:, 40:48, :] = rest
    part_out[:, 48:56, :] = rest2

    def part_copy(o):
        other = z_at(o)
        return pltpu.make_async_remote_copy(
            src_ref=part_out.at[other], dst_ref=part_in.at[z], send_sem=part_send.at[o],
            recv_sem=part_recv.at[z], device_id=(lat, x_lo * 8 + other), device_id_type=MESH,
        )

    for o in Z_FAR_FIRST:
        part_copy(o).start()

    pl.semaphore_wait(heard.at[1], 2)
    tell(heard.at[2], across)
    part_in[z] = part_out[z]
    loads[7].wait()
    leg = leg_ref[...]
    reversed_ref[...] = dot(leg, reverse_matrix()).astype(BF16)

    @pl.loop(1, 8)
    def _(o):
        other = z_at(o)
        pltpu.make_async_remote_copy(
            src_ref=part_out.at[other], dst_ref=part_in.at[other], send_sem=part_send.at[o],
            recv_sem=part_recv.at[other], device_id=(lat, x_lo * 8 + other), device_id_type=MESH,
        ).wait_recv()

    weighted = jnp.sum(part_in[...], axis=0).astype(BF16)
    spread_ref[...] = spread_weighted(weighted, selector, spreader)
    even = dot(spread_ref[0:192], leg)
    odd = dot(spread_ref[192:384], reversed_ref[...])
    lane128 = fiota((16, 128), 1)
    for c in range(2):
        packed, extra = pack(even, odd, sign, first, c)
        rest = jnp.zeros((16, 128), F32)
        for kb in range(3):
            for t in range(5):
                packed_ref[c, kb * 5 + t] = packed[16 * kb:16 * (kb + 1), 128 * t:128 * (t + 1)]
            rest = jnp.where(lane128 == float(kb), extra[16 * kb:16 * (kb + 1)], rest)
        packed_ref[c, 15] = rest

    to_core = send(packed_ref.at[1 - core], core_in, core_send, core_recv, (sibling, lon))
    to_core.wait()
    sum_out[...] = packed_ref[core] + core_in[...]
    pl.semaphore_wait(heard.at[2], 1)

    def sum_copy(o):
        other = chip_at(o)
        return pltpu.make_async_remote_copy(
            src_ref=sum_out.at[other], dst_ref=sum_in.at[chip], send_sem=sum_send.at[o],
            recv_sem=sum_recv.at[chip], device_id=(other * 2 + core, lon), device_id_type=MESH,
        )

    for o in FAR_FIRST:
        sum_copy(o).start()

    sum_in[chip] = sum_out[chip]

    @pl.loop(0, 4)
    def _(zz):
        source = (1 - x_lo) * 8 + zz * 2
        fill(source, own_tables, source, flon * 160.0)


    @pl.loop(1, CHIPS)
    def _(o):
        other = chip_at(o)
        pltpu.make_async_remote_copy(
            src_ref=sum_out.at[other], dst_ref=sum_in.at[other], send_sem=sum_send.at[o],
            recv_sem=sum_recv.at[other], device_id=(other * 2 + core, lon), device_id_type=MESH,
        ).wait_recv()

    total = jnp.sum(sum_in[...], axis=0)
    damping = (damp_ref[0], damp_ref[1])
    vertical = ((vert_ref[0, 0], vert_ref[0, 1]), (vert_ref[1, 0], vert_ref[1, 1]))
    first8 = first_ref[pl.ds(pl.multiple_of((chip // 5) * 16, 8), 8), 0:1]
    lane0 = ((chip % 5) * 128).astype(F32)
    spec = correct(total, first8, lane0, chip == 15, damping, vertical)
    gathered[core, chip] = spec.astype(BF16)

    def all_copy(o):
        return pltpu.make_async_remote_copy(
            src_ref=gathered.at[core, chip], dst_ref=gathered.at[core, chip], send_sem=all_send.at[o],
            recv_sem=all_recv.at[chip], device_id=(chip_at(o) * 2 + core, lon), device_id_type=MESH,
        )

    for o in FAR_FIRST:
        all_copy(o).start()

    @pl.loop(1, CHIPS)
    def _(o):
        other = chip_at(o)
        pltpu.make_async_remote_copy(
            src_ref=gathered.at[core, other], dst_ref=gathered.at[core, other], send_sem=all_send.at[o],
            recv_sem=all_recv.at[other], device_id=(other * 2 + core, lon), device_id_type=MESH,
        ).wait_recv()

    to_pair = send(gathered.at[core], gathered.at[core], pair_send, pair_recv, (sibling, lon))
    to_pair.wait()

    evens, odds = [], []
    for c in range(2):
        tiles = [[gathered[c, kb * 5 + t].astype(F32) for t in range(5)] for kb in range(3)]
        packed = jnp.concatenate([jnp.concatenate(row, axis=1) for row in tiles], axis=0)
        last = gathered[c, 15].astype(F32)
        extra = jnp.concatenate([last[:, kb:kb + 1] for kb in range(3)], axis=0)
        e, o = unpack(packed, extra, first)
        evens.append(e)
        odds.append(o)
    scale_even = jnp.where(first == 0.0, 1.0, 2.0)
    scale_odd = jnp.where(first == M - 1.0, 1.0, 2.0)
    north_e = [e * scale_even for e in evens]
    north_o = [o * scale_odd for o in odds]
    rows_e = jnp.concatenate(north_e + [e * sign for e in north_e], axis=0).astype(BF16)
    rows_o = jnp.concatenate(north_o + [-(o * sign) for o in north_o], axis=0).astype(BF16)
    x_even = dot_nt(rows_e, leg)
    x_odd = dot_nt(rows_o, reversed_ref[...])
    coefs[lon] = collapse(x_even, x_odd, select_rows_t(), spreader)

    def coef_copy(o):
        return pltpu.make_async_remote_copy(
            src_ref=coefs.at[lon], dst_ref=coefs.at[lon], send_sem=coef_send.at[o],
            recv_sem=coef_recv.at[z], device_id=(lat, x_lo * 8 + z_at(o)), device_id_type=MESH,
        )

    def forward_copy(source):
        at = x_lo * 8 + source
        return pltpu.make_async_remote_copy(
            src_ref=coefs.at[at], dst_ref=coefs.at[at], send_sem=fwd_send.at[source],
            recv_sem=fwd_recv.at[source], device_id=(lat, near), device_id_type=MESH,
        )

    forward_copy(z).start()

    for o in Z_FAR_FIRST:
        coef_copy(o).start()

    evens = jnp.concatenate(evens, axis=0).astype(BF16)
    odds = jnp.concatenate(odds, axis=0).astype(BF16)
    spec_ref[...] = spectrum_rows(evens, odds, flat)

    @pl.loop(1, 8)
    def _(o):
        other = z_at(o)
        at = x_lo * 8 + other
        pltpu.make_async_remote_copy(
            src_ref=coefs.at[at], dst_ref=coefs.at[at], send_sem=coef_send.at[o],
            recv_sem=coef_recv.at[other], device_id=(lat, at), device_id_type=MESH,
        ).wait_recv()
        forward_copy(other).start()

    def inverse(half):
        rows = pl.ds(pl.multiple_of(half * 320, 320), 320)
        parts = []
        for part, v in enumerate(unfold(coefs[pl.ds(half * 8, 8)].astype(F32))):
            v = v.T.astype(BF16)
            parts.append(dot(v, own_tables[2 * part][rows, :]) + dot(v, own_tables[2 * part + 1][rows, :]))
        return parts[0][0:80] + jnp.concatenate([parts[1][80:128], parts[1][0:32]], axis=0)

    grid = inverse(x_lo)

    @pl.loop(0, 8)
    def _(source):
        at = (1 - x_lo) * 8 + source
        pltpu.make_async_remote_copy(
            src_ref=coefs.at[at], dst_ref=coefs.at[at], send_sem=fwd_send.at[source],
            recv_sem=fwd_recv.at[source], device_id=(lat, near), device_id_type=MESH,
        ).wait_recv()

    grid = grid + inverse(1 - x_lo)
    grid_ref[...] = grid * (1.0 / float(NLON * M) ** 0.5)

    @pl.loop(1, 8)
    def _(o):
        part_copy(o).wait_send()
        coef_copy(o).wait_send()

    @pl.loop(0, 8)
    def _(source):
        forward_copy(source).wait_send()

    @pl.loop(1, CHIPS)
    def _(o):
        sum_copy(o).wait_send()
        all_copy(o).wait_send()


def shards(level_fields, wind_field, zonal_step, quad_weight, legendre, wave_table, damping, vertical):
    def rows(x):
        return x.transpose(0, 2, 1, 3)

    vmem = pl.BlockSpec(memory_space=pltpu.VMEM)
    hbm = pl.BlockSpec(memory_space=pl.ANY)
    dma = pltpu.SemaphoreType.DMA
    grid, spec = pl.pallas_call(
        kernel,
        out_shape=(
            jax.ShapeDtypeStruct((GRID, LANES), F32),
            jax.ShapeDtypeStruct((32, 160), F32),
        ),
        in_specs=[hbm] * 8,
        out_specs=(vmem, vmem),
        scratch_shapes=[
            pltpu.VMEM((2, 2, ROWS, 2, 160), F32),
            pltpu.VMEM((1, ROWS), F32),
            pltpu.VMEM((1, ROWS), F32),
            pltpu.VMEM((K, M), BF16),
            pltpu.VMEM((5, 128), jnp.int32),
            pltpu.SMEM((2,), F32),
            pltpu.SMEM((2, 2), F32),
            pltpu.VMEM((4, 40, LANES), F32),
            pltpu.VMEM((4, 40, LANES), F32),
            pltpu.VMEM((2, 8, 128), F32),
            pltpu.VMEM((2, 2, 8, 128), F32),
            pltpu.VMEM((2, 2, 2, 8, LANES), F32),
            pltpu.VMEM((M, 128), F32),
            pltpu.VMEM((M, LANES), BF16),
            pltpu.VMEM((M, LANES), BF16),
            pltpu.VMEM((M, LANES), BF16),
            pltpu.VMEM((M, LANES), BF16),
            pltpu.VMEM((M // 2, LANES), BF16),
            pltpu.VMEM((M // 2, LANES), BF16),
            pltpu.VMEM((M // 2, LANES), BF16),
            pltpu.VMEM((M // 2, LANES), BF16),
            pltpu.VMEM((K, M), BF16),
            pltpu.VMEM((8, FOLDED, 128), F32),
            pltpu.VMEM((8, FOLDED, 128), F32),
            pltpu.VMEM((384, K), BF16),
            pltpu.VMEM((2, BLOCKS, 16, 128), F32),
            pltpu.VMEM((BLOCKS, 16, 128), F32),
            pltpu.VMEM((BLOCKS, 16, 128), F32),
            pltpu.VMEM((CHIPS, 16, 128), F32),
            pltpu.VMEM((64, 128), F32),
            pltpu.VMEM((2, BLOCKS, 16, 128), BF16),
            pltpu.VMEM((16, FOLDED16, 128), BF16),
            dma((8,)), dma((8,)), dma((8,)), dma, dma, dma((8,)), dma((8,)), dma, dma,
            dma((CHIPS,)), dma((CHIPS,)), dma((CHIPS,)), dma((CHIPS,)), dma, dma,
            dma((8,)), dma((8,)), dma((8,)), dma((8,)),
            pltpu.SemaphoreType.REGULAR((3,)),
        ],
        compiler_params=pltpu.CompilerParams(
            collective_id=0, has_side_effects=True, vmem_limit_bytes=60 * 1024 * 1024
        ),
    )(
        rows(level_fields), rows(wind_field), zonal_step[None], quad_weight[None],
        legendre.transpose(1, 0, 2).reshape(K, M), wave_table.reshape(5, 128), damping, vertical,
    )
    fields = grid[:, :160].reshape(2, ROWS, 2, 160).transpose(0, 2, 1, 3)
    spectrum = spec[:ROWS].reshape(ROWS, 2, 2, SLOTS).transpose(0, 3, 1, 2)
    return fields, spectrum


def solution(mesh):
    return jax.shard_map(
        shards,
        mesh=mesh,
        in_specs=(
            P(None, None, "lat", "lon"),
            P(None, None, "lat", "lon"),
            P("lat"),
            P("lat"),
            P("lon", "lat", None),
            P(),
            P(),
            P(),
        ),
        out_specs=(P(None, None, "lat", "lon"), P("lat", "lon", None, None)),
        check_vma=False,
    )
```

```python
import functools

import jax
import jax.numpy as jnp
from jax import lax
from jax.experimental import pallas as pl
from jax.experimental.pallas import tpu as pltpu
from jax.sharding import PartitionSpec as P

NLON = 2560
M = 640
ROWS = 20
GRID = 80
SLOTS = 40
LANES = 256
K = ROWS * SLOTS
CHIPS = 16
BLOCKS = 16
PACK = 48
FOLDED = 56
FOLDED16 = 64
F32 = jnp.float32
BF16 = jnp.bfloat16
MESH = pl.DeviceIdType.MESH
FAR_FIRST = (12, 13, 15, 11, 14, 10, 9, 4, 8, 5, 7, 3, 6, 2, 1)
Z_FAR_FIRST = (4, 5, 7, 3, 6, 2, 1)


def fiota(shape, dim):
    return lax.broadcasted_iota(jnp.int32, shape, dim).astype(F32)


def fdiv(x, by):
    return jnp.floor((x + 0.5) * (1.0 / by))


def fmod(x, by):
    return x - by * fdiv(x, by)


def dot(a, b):
    return lax.dot_general(a, b, (((1,), (0,)), ((), ())), preferred_element_type=F32)


def dot_nt(a, b):
    return lax.dot_general(a, b, (((1,), (1,)), ((), ())), preferred_element_type=F32)


def split(x):
    high = x.astype(BF16)
    return high, (x - high.astype(F32)).astype(BF16)


def column(row, picked):
    n = row.shape[1]
    rows = picked.shape[0]
    hit = fiota((rows, n), 1) == picked
    return jnp.sum(jnp.where(hit, jnp.broadcast_to(row, (rows, n)), 0.0), axis=1, keepdims=True)


def as_row(col):
    hit = fiota((GRID, 128), 1) == fiota((GRID, 128), 0)
    return jnp.sum(jnp.where(hit, jnp.broadcast_to(col, (GRID, 128)), 0.0), axis=0, keepdims=True)


def trig(waves, first):
    lons = first + fiota((1, LANES), 1)
    turns = waves * lons
    quarter = jnp.floor(turns * (4.0 / NLON) + 0.5)
    rest = turns - quarter * (NLON / 4.0)
    t = rest * (6.283185307179586 / NLON)
    t2 = t * t
    sine = t * (1.0 + t2 * (-1.6666667e-1 + t2 * (8.3333333e-3 + t2 * (-1.9841270e-4 + t2 * 2.7557319e-6))))
    cosine = 1.0 + t2 * (-0.5 + t2 * (4.1666667e-2 + t2 * (-1.3888889e-3 + t2 * 2.4801587e-5)))
    which = quarter.astype(jnp.int32) & 3
    swap = (which & 1) == 1
    c = jnp.where(swap, sine, cosine)
    s = jnp.where(swap, cosine, sine)
    c = jnp.where((which == 1) | (which == 2), -c, c)
    s = jnp.where(which >= 2, s, -s)
    return c, s


def step_field(level, wind, up, down, at_pole, at_equator, east, west, zonal, weight, roll):
    lane = fiota((40, LANES), 1)
    wide = jnp.where(lane == 160.0, east, jnp.where(lane == 255.0, west, level))
    eastward = roll(wide, LANES - 1, 1)
    westward = roll(wide, 1, 1)
    last = level[32:40]
    row8 = fiota((8, LANES), 0)
    swapped = jnp.where(row8 == 0.0, roll(last, 1, 0), roll(last, 3, 0))
    down = jnp.where(at_equator, swapped, down)
    up = jnp.where(at_pole, 0.0, up)
    tall = jnp.concatenate([up, level, down], axis=0)
    toward = roll(tall, 54, 0)[8:48]
    poleward = roll(tall, 2, 0)[8:48]
    change = wind[0] * zonal * (eastward - westward) + 0.25 * wind[1] * (toward - poleward)
    return (level - change) * weight


def row_codes(r):
    parity = fdiv(r, 192.0)
    r1 = fmod(r, 192.0)
    h = fdiv(r1, 96.0)
    c = fdiv(fmod(r1, 96.0), 48.0)
    r2 = fmod(r1, 48.0)
    group = fdiv(r2, 16.0)
    level = fdiv(fmod(r2, 16.0), 8.0)
    pair = group * 8.0 + fmod(r2, 8.0)
    slot = jnp.where(pair < 20.0, 2.0 * pair + parity, -1.0)
    return slot, c, level, h


def folded_rows(slot, c):
    rest = 40.0 + fmod(slot, 8.0) + 8.0 * fdiv(slot, 32.0)
    return slot, jnp.where((c == 1.0) & (slot >= 0.0), rest, -1.0)


def select_rows():
    slot, c, level, h = row_codes(fiota((384, 1), 0))
    lane = fiota((1, FOLDED), 1)
    return tuple(jnp.where(r == lane, 1.0, 0.0).astype(BF16) for r in folded_rows(slot, c))


def select_rows_t():
    slot, c, level, h = row_codes(fiota((1, 384), 1))
    row = fiota((FOLDED16, 1), 0)
    return tuple(jnp.where(r == row, 1.0, 0.0).astype(BF16) for r in folded_rows(slot, c))


def spread_rows():
    lane = fiota((256, 1), 0)
    g = jnp.where(lane < 80.0, lane, jnp.where(lane < 128.0, lane - 80.0, 48.0 + fmod(lane, 32.0)))
    hit = fdiv(fmod(g, 40.0), 2.0) == fdiv(fiota((1, K), 1), 40.0)
    return jnp.where(hit, 1.0, 0.0).astype(BF16)


def level_mask():
    slot, c, level, h = row_codes(fiota((384, 1), 0))
    lane = fiota((1, 256), 1)
    rest = lane >= 128.0
    g = jnp.where(lane < 80.0, lane, jnp.where(rest, 48.0 + fmod(lane, 32.0), lane - 80.0))
    part = jnp.where(lane < 80.0, 0.0, 1.0)
    group = jnp.where(rest, fdiv(lane - 128.0, 32.0), fmod(fdiv(slot, 8.0), 4.0))
    return (
        (level == fdiv(g, 40.0)) & (h == fmod(g, 2.0)) & (c == part)
        & (group == fmod(fdiv(slot, 8.0), 4.0))
    )


def fold(cosine, sine):
    n = cosine.shape[0] // SLOTS
    lane = fiota((1, 1, 128), 2)
    cosine = jnp.reshape(cosine, (n, SLOTS, 128))
    sine = jnp.reshape(sine, (n, SLOTS, 128))
    main = jnp.where(lane < 80.0, cosine, sine)
    rest = jnp.where(lane < 32.0, sine, 0.0)
    first = rest[:, 0:8]
    for b in range(1, 4):
        moved = pltpu.roll(jnp.reshape(rest[:, 8 * b:8 * b + 8], (8 * n, 128)), 32 * b, 1)
        first = first + jnp.reshape(moved, (n, 8, 128))
    return main, first, rest[:, 32:40]


def unfold(folded):
    n = folded.shape[0]
    lane = fiota((1, 1, 128), 2)
    main = folded[:, 0:40]
    first = jnp.reshape(folded[:, 40:48], (8 * n, 128))
    parts = [folded[:, 40:48]]
    for b in range(1, 4):
        parts.append(jnp.reshape(pltpu.roll(first, 128 - 32 * b, 1), (n, 8, 128)))
    parts.append(folded[:, 48:56])
    rest = jnp.concatenate(parts, axis=1)
    cosine = jnp.where(lane < 80.0, main, 0.0)
    sine = jnp.where(lane < 32.0, rest, jnp.where(lane < 80.0, 0.0, main))
    return jnp.reshape(cosine, (n * SLOTS, 128)), jnp.reshape(sine, (n * SLOTS, 128))


def slot_lanes():
    return fmod(fiota((1, K), 1), 40.0)


def reverse_matrix():
    n = fiota((M, M), 0)
    j = fiota((M, M), 1)
    hit = (n + j == M - 2.0) | (n + j == 2.0 * M - 2.0)
    return jnp.where(hit, 1.0, 0.0).astype(BF16)


def first_wave(waves, lon):
    r = fiota((64, 1), 0)
    pair = fdiv(r, 16.0) * 8.0 + fmod(r, 8.0)
    picked = jnp.where(pair < 20.0, lon * 40.0 + 2.0 * pair, -1.0)
    return column(waves, picked)


def parity_sign(first):
    j = fiota((PACK, M), 1)
    odd = (j - first).astype(jnp.int32) & 1
    return jnp.where(odd == 1, -1.0, 1.0)


def spread_weighted(weighted, selector, spreader):
    chosen = jnp.concatenate([dot(q, weighted) for q in selector], axis=1)
    chosen = jnp.where(level_mask(), chosen, 0.0).astype(BF16)
    wide = dot(chosen, spreader)
    slot = row_codes(fiota((384, 1), 0))[0]
    return jnp.where(slot == slot_lanes(), wide, 0.0).astype(BF16)


def pack(even, odd, sign, first, c):
    lo = c * PACK
    hi = 96 + c * PACK
    kept = fiota((PACK, M), 1) >= first
    from_odd = odd[lo:lo + PACK] - sign * odd[hi:hi + PACK]
    packed = jnp.where(kept, even[lo:lo + PACK] + sign * even[hi:hi + PACK], from_odd)
    return packed, from_odd[:, M - 1:M]


def correct(total, first, lane0, extra, damping, vertical):
    j = lane0 + fiota((8, 128), 1)
    n = jnp.where(j >= first, j, (M - 2.0) - j)
    n = jnp.where(extra, M - 1.0, n)
    square = n * (n + 1.0) / float(M * M)
    raw = (total[0:8], total[8:16])
    modal = [
        (vertical[k][0] * raw[0] + vertical[k][1] * raw[1]) / (1.0 + damping[k] * square)
        for k in range(2)
    ]
    return jnp.concatenate(
        [vertical[0][l] * modal[0] + vertical[1][l] * modal[1] for l in range(2)], axis=0
    )


def unpack(packed, extra, first):
    j = fiota((PACK, M), 1)
    kept = j >= first
    even = jnp.where(kept, packed, 0.0)
    odd = jnp.where(j == M - 1.0, extra, jnp.where(kept, 0.0, packed))
    return even, odd


def spectrum_rows(even, odd, lat):
    r = fiota((32, 1), 0)
    n = jnp.where(r < ROWS, lat * ROWS + r, -5.0)
    j = fiota((1, M), 1)
    want_even = jnp.where(n == j, 1.0, 0.0).astype(BF16)
    want_odd = jnp.where((n + j == M - 2.0) | (n + j == 2.0 * M - 2.0), 1.0, 0.0).astype(BF16)
    q = fiota((96, 1), 0)
    c = fdiv(q, 48.0)
    q1 = fmod(q, 48.0)
    level = fdiv(fmod(q1, 16.0), 8.0)
    pair = fdiv(q1, 16.0) * 8.0 + fmod(q1, 8.0)
    lane = fiota((1, 160), 1)
    same = (c == fdiv(lane, 80.0)) & (level == fdiv(fmod(lane, 80.0), 40.0)) & (pair < 20.0)
    slot = fmod(lane, 40.0)
    to_even = jnp.where(same & (slot == 2.0 * pair), 1.0, 0.0).astype(BF16)
    to_odd = jnp.where(same & (slot == 2.0 * pair + 1.0), 1.0, 0.0).astype(BF16)
    return dot(dot_nt(want_even, even).astype(BF16), to_even) + dot(
        dot_nt(want_odd, odd).astype(BF16), to_odd
    )


def collapse(x_even, x_odd, selector_t, spreader):
    both = jnp.concatenate([x_even, x_odd], axis=0)
    slot = row_codes(fiota((384, 1), 0))[0]
    both = jnp.where(slot == slot_lanes(), both, 0.0).astype(BF16)
    rows = dot_nt(both, spreader)
    rows = jnp.where(level_mask(), rows, 0.0).astype(BF16)
    folded = dot(selector_t[0], rows[:, 0:128]) + dot(selector_t[1], rows[:, 128:256])
    return folded.astype(BF16)


def kernel(
    level_hbm, wind_hbm, zonal_hbm, weight_hbm, leg_hbm, wave_hbm, damp_hbm, vert_hbm,
    grid_ref, spec_ref,
    native, zonal_ref, weight_ref, leg_ref, wave_ref, damp_ref, vert_ref,
    field_ref, tail_out, near_in, column_out, column_in, edge_in, wave_col,
    cos_hi, cos_lo, sin_hi, sin_lo, near_cos_hi, near_cos_lo, near_sin_hi, near_sin_lo, reversed_ref, part_out, part_in, spread_ref,
    packed_ref, core_in, sum_out, sum_in, first_ref, gathered, coefs,
    load_sem, edge_send, edge_recv, near_send, near_recv, part_send, part_recv, core_send,
    core_recv, sum_send, sum_recv, all_send, all_recv, pair_send, pair_recv, coef_send,
    coef_recv, fwd_send, fwd_recv, heard,
):
    lat = lax.axis_index("lat")
    lon = lax.axis_index("lon")
    chip = lat // 2
    core = lat % 2
    x_lo = lon // 8
    z = lon % 8
    lat_next, lat_prev = (lat + 1) % 32, (lat + 31) % 32
    lon_next, lon_prev = (lon + 1) % 16, (lon + 15) % 16
    near = (lon + 8) % 16
    sibling = chip * 2 + 1 - core
    flat = lat.astype(F32)
    flon = lon.astype(F32)

    def partners(at, bits):
        flips = [(1 - 2 * ((at // 2**k) % 2)) * 2**k for k in range(bits)]
        return [at + sum(f for k, f in enumerate(flips) if (o >> k) & 1) for o in range(2**bits)]

    chips = partners(chip, 4)
    zs = partners(z, 3)
    lons = [x_lo * 8 + other for other in zs]

    def y_at(offset):
        return ((chip // 8) * 8 + (chip + offset) % 8) * 2 + core

    def tell(sem, device):
        pl.semaphore_signal(sem, inc=1, device_id=device, device_id_type=MESH)

    def send(src, dst, send_sem, recv_sem, device):
        copy = pltpu.make_async_remote_copy(
            src_ref=src, dst_ref=dst, send_sem=send_sem, recv_sem=recv_sem,
            device_id=device, device_id_type=MESH,
        )
        copy.start()
        return copy

    def roll(x, amount, axis):
        return pltpu.roll(x, amount, axis)

    barrier = pltpu.get_barrier_semaphore()

    def greet(device):
        pl.semaphore_signal(barrier, inc=1, device_id=device, device_id_type=MESH)

    loads = [
        pltpu.make_async_copy(src, dst, load_sem.at[n])
        for n, (src, dst) in enumerate((
            (level_hbm, native.at[0]), (wind_hbm, native.at[1]), (wave_hbm, wave_ref),
            (zonal_hbm, zonal_ref), (weight_hbm, weight_ref), (damp_hbm, damp_ref),
            (vert_hbm, vert_ref), (leg_hbm, leg_ref),
        ))
    ]
    for copy in loads:
        copy.start()

    across = ((chip + 8) % CHIPS * 2 + core, lon)
    greet(across)
    for step in (1, 7):
        greet((y_at(step), lon))

    for o in range(1, 8):
        greet((lat, lons[o]))

    edge_devices = (
        ((lat_next, lon), 0, 0), ((lat_prev, lon), 0, 1), ((lat_next, near), 1, 0), ((lat_prev, near), 1, 1),
        ((lat, lon_prev), 0, 0), ((lat, lon_next), 0, 1),
        ((lat, (lon_prev + 8) % 16), 1, 0), ((lat, (lon_next + 8) % 16), 1, 1),
    )
    for device, _, _ in edge_devices:
        greet(device)
    greet((lat, near))

    for copy in loads[:7]:
        copy.wait()

    field_ref[:, :, 128:LANES] = jnp.zeros((4, 40, 128), F32)
    for a in range(2):
        for b in range(2):
            for i in range(ROWS):
                field_ref[2 * a + b, 2 * i:2 * i + 2, 0:160] = native[a, b, i]

    tail = field_ref[0, :, 128:LANES]
    for f in range(1, 4):
        tail = tail + pltpu.roll(field_ref[f, :, 128:LANES], 32 * f, 1)
    tail_out[...] = tail

    flat_level = jnp.reshape(field_ref[0:2], (GRID, LANES))
    column_out[0] = jnp.broadcast_to(as_row(flat_level[:, 0:1]), (8, 128))
    column_out[1] = jnp.broadcast_to(as_row(flat_level[:, 159:160]), (8, 128))
    own_tables = (cos_hi, cos_lo, sin_hi, sin_lo)
    near_tables = (near_cos_hi, near_cos_lo, near_sin_hi, near_sin_lo)

    def fill(source, tables, at, first):
        w = wave_col[pl.ds(pl.multiple_of(source * SLOTS, 80), 2 * SLOTS), 0:1]
        rows = pl.ds(pl.multiple_of(at * SLOTS, 80), 2 * SLOTS)
        c, s = trig(w, first)
        tables[0][rows, :], tables[1][rows, :] = split(c)
        tables[2][rows, :], tables[3][rows, :] = split(s)

    near_first = near.astype(F32) * 160.0

    pl.semaphore_wait(barrier, 3 + 7 + 9)

    to_near = send(field_ref.at[:, :, 0:128], near_in.at[0:4], near_send.at[0], near_recv.at[0], (lat, near))
    to_near2 = send(tail_out, near_in.at[4], near_send.at[1], near_recv.at[1], (lat, near))
    edges = []
    for n, (device, block, side) in enumerate(edge_devices):
        if n < 4:
            src = field_ref.at[0:2, 32:40, :] if side == 0 else field_ref.at[0:2, 0:8, :]
            dst = edge_in.at[block, side]
        else:
            src, dst = column_out.at[side], column_in.at[block, side]
        edges.append(send(src, dst, edge_send.at[n], edge_recv.at[n], device))

    for step in (1, 7):
        tell(heard.at[0], (y_at(step), lon))

    waves = wave_ref[...].astype(F32)
    waves = [waves[t:t + 1, :] for t in range(5)]
    for t in range(5):
        wave_col[128 * t:128 * (t + 1), :] = jnp.broadcast_to(waves[t], (128, 128)).T
    waves = jnp.concatenate(waves, axis=1)
    first_ref[...] = jnp.broadcast_to(first_wave(waves, flon), (64, 128))

    @pl.loop(0, 4)
    def _(zz):
        source = x_lo * 8 + zz * 2
        fill(source, own_tables, source, flon * 160.0)
        fill(source, near_tables, zz * 2, near_first)

    picked = fdiv(fiota((40, 1), 0), 2.0)
    zonal = column(zonal_ref[...], picked)
    weight = column(weight_ref[...], picked) * (1.0 / float(NLON) ** 0.5)
    g = fiota((40, 1), 0)
    first = first_ref[0:PACK, 0:1]
    sign = parity_sign(first)
    selector, spreader = select_rows(), spread_rows()

    for copy in edges:
        copy.wait()
    to_near.wait()
    to_near2.wait()
    tail = near_in[4]
    in_tail = fiota((40, 128), 1) < 32.0
    field_near = [
        jnp.concatenate(
            [near_in[f], jnp.where(in_tail, pltpu.roll(tail, (128 - 32 * f) % 128, 1) if f else tail, 0.0)], axis=1
        )
        for f in range(4)
    ]

    pl.semaphore_wait(heard.at[0], 2)
    for step in (2, 6):
        tell(heard.at[1], (y_at(step), lon))

    def advance(block, field):
        levels = []
        for l in range(2):
            east = column(column_in[block, 0, 0:1, :], g + 40.0 * l)
            west = column(column_in[block, 1, 0:1, :], g + 40.0 * l)
            levels.append(step_field(
                field[l], (field[2], field[3]), edge_in[block, 0, l], edge_in[block, 1, l],
                lat == 0, lat == 31, east, west, zonal, weight, roll,
            ))
        return jnp.concatenate(levels, axis=0)

    mine = pl.ds(pl.multiple_of(x_lo * 320, 320), 320)

    def fourier(values, tables, rows):
        zeros = jnp.zeros((48, LANES), F32)
        sums = []
        for part, v in enumerate((
            jnp.concatenate([values, zeros], axis=0),
            jnp.concatenate([values[48:80], zeros, values[0:48]], axis=0),
        )):
            v_hi, v_lo = split(v)
            t_hi, t_lo = tables[2 * part][rows, :], tables[2 * part + 1][rows, :]
            sums.append(dot_nt(t_hi, v_hi) + dot_nt(t_hi, v_lo) + dot_nt(t_lo, v_hi))
        return sums

    own_sums = fourier(advance(0, field_ref), own_tables, mine)
    near_sums = fourier(advance(1, field_near), near_tables, pl.ds(0, 320))
    main, rest, rest2 = fold(*(a + b for a, b in zip(own_sums, near_sums)))
    part_out[:, 0:40, :] = main
    part_out[:, 40:48, :] = rest
    part_out[:, 48:56, :] = rest2

    def remote(src, dst, send_sem, recv_sem, device):
        return pltpu.make_async_remote_copy(
            src_ref=src, dst_ref=dst, send_sem=send_sem, recv_sem=recv_sem,
            device_id=device, device_id_type=MESH,
        )

    def part_copy(o):
        return remote(part_out.at[zs[o]], part_in.at[o], part_send, part_recv, (lat, lons[o]))

    part_all = remote(part_out.at[0:7], part_in.at[1:8], part_send, part_recv, (lat, lons[1]))
    for o in Z_FAR_FIRST:
        part_copy(o).start()

    pl.semaphore_wait(heard.at[1], 2)
    tell(heard.at[2], across)
    part_in[0] = part_out[z]
    loads[7].wait()
    leg = leg_ref[...]
    reversed_ref[...] = dot(leg, reverse_matrix()).astype(BF16)

    part_all.wait_recv()
    weighted = jnp.sum(part_in[...], axis=0).astype(BF16)
    spread_ref[...] = spread_weighted(weighted, selector, spreader)
    even = dot(spread_ref[0:192], leg)
    odd = dot(spread_ref[192:384], reversed_ref[...])
    lane128 = fiota((16, 128), 1)
    for c in range(2):
        packed, extra = pack(even, odd, sign, first, c)
        rest = jnp.zeros((16, 128), F32)
        for kb in range(3):
            for t in range(5):
                packed_ref[c, kb * 5 + t] = packed[16 * kb:16 * (kb + 1), 128 * t:128 * (t + 1)]
            rest = jnp.where(lane128 == float(kb), extra[16 * kb:16 * (kb + 1)], rest)
        packed_ref[c, 15] = rest

    to_core = send(packed_ref.at[1 - core], core_in, core_send, core_recv, (sibling, lon))
    to_core.wait()
    sum_out[...] = packed_ref[core] + core_in[...]
    pl.semaphore_wait(heard.at[2], 1)

    def lat_device(o):
        return (chips[o] * 2 + core, lon)

    def sum_copy(o):
        return remote(sum_out.at[chips[o]], sum_in.at[o], sum_send, sum_recv, lat_device(o))

    sum_all = remote(sum_out.at[0:15], sum_in.at[1:16], sum_send, sum_recv, lat_device(1))
    for o in FAR_FIRST:
        sum_copy(o).start()

    sum_in[0] = sum_out[chip]

    @pl.loop(0, 4)
    def _(zz):
        source = (1 - x_lo) * 8 + zz * 2
        fill(source, own_tables, source, flon * 160.0)


    sum_all.wait_recv()
    total = jnp.sum(sum_in[...], axis=0)
    damping = (damp_ref[0], damp_ref[1])
    vertical = ((vert_ref[0, 0], vert_ref[0, 1]), (vert_ref[1, 0], vert_ref[1, 1]))
    first8 = first_ref[pl.ds(pl.multiple_of((chip // 5) * 16, 8), 8), 0:1]
    lane0 = ((chip % 5) * 128).astype(F32)
    spec = correct(total, first8, lane0, chip == 15, damping, vertical)
    gathered[core, chip] = spec.astype(BF16)

    mine_all = gathered.at[core, chip]
    others = gathered.at[core, 0:15]
    all_all = remote(others, others, all_send, all_recv, lat_device(1))
    for o in FAR_FIRST:
        remote(mine_all, mine_all, all_send, all_recv, lat_device(o)).start()
    all_all.wait_recv()

    to_pair = send(gathered.at[core], gathered.at[core], pair_send, pair_recv, (sibling, lon))
    to_pair.wait()

    evens, odds = [], []
    for c in range(2):
        tiles = [[gathered[c, kb * 5 + t].astype(F32) for t in range(5)] for kb in range(3)]
        packed = jnp.concatenate([jnp.concatenate(row, axis=1) for row in tiles], axis=0)
        last = gathered[c, 15].astype(F32)
        extra = jnp.concatenate([last[:, kb:kb + 1] for kb in range(3)], axis=0)
        e, o = unpack(packed, extra, first)
        evens.append(e)
        odds.append(o)
    scale_even = jnp.where(first == 0.0, 1.0, 2.0)
    scale_odd = jnp.where(first == M - 1.0, 1.0, 2.0)
    north_e = [e * scale_even for e in evens]
    north_o = [o * scale_odd for o in odds]
    rows_e = jnp.concatenate(north_e + [e * sign for e in north_e], axis=0).astype(BF16)
    rows_o = jnp.concatenate(north_o + [-(o * sign) for o in north_o], axis=0).astype(BF16)
    x_even = dot_nt(rows_e, leg)
    x_odd = dot_nt(rows_o, reversed_ref[...])
    coefs[lon] = collapse(x_even, x_odd, select_rows_t(), spreader)

    def coef_copy(o, at):
        return remote(coefs.at[at], coefs.at[at], coef_send, coef_recv.at[o], (lat, lons[o]))

    def forward_copy(o):
        return remote(coefs.at[lons[o]], coefs.at[lons[o]], fwd_send, fwd_recv, (lat, near))

    for o in Z_FAR_FIRST:
        coef_copy(o, lon).start()
    forward_copy(0).start()

    evens = jnp.concatenate(evens, axis=0).astype(BF16)
    odds = jnp.concatenate(odds, axis=0).astype(BF16)
    spec_ref[...] = spectrum_rows(evens, odds, flat)

    for o in (1, 2, 6, 3, 7, 5, 4):
        coef_copy(o, lons[o]).wait_recv()
        forward_copy(o).start()

    def inverse(half):
        rows = pl.ds(pl.multiple_of(half * 320, 320), 320)
        parts = []
        for part, v in enumerate(unfold(coefs[pl.ds(half * 8, 8)].astype(F32))):
            v = v.T.astype(BF16)
            parts.append(dot(v, own_tables[2 * part][rows, :]) + dot(v, own_tables[2 * part + 1][rows, :]))
        return parts[0][0:80] + jnp.concatenate([parts[1][80:128], parts[1][0:32]], axis=0)

    grid = inverse(x_lo)

    forward_all = remote(coefs.at[0:8], coefs.at[0:8], fwd_send, fwd_recv, (lat, near))
    forward_all.wait_recv()

    grid = grid + inverse(1 - x_lo)
    grid = grid * (1.0 / float(NLON * M) ** 0.5)
    for l in range(2):
        for i in range(ROWS):
            at = 40 * l + 2 * i
            grid_ref[l, i] = grid[at:at + 2, 0:160]

    part_all.wait_send()
    sum_all.wait_send()
    all_all.wait_send()
    remote(coefs.at[0:7], coefs.at[0:7], coef_send, coef_recv.at[0], (lat, near)).wait_send()
    forward_all.wait_send()


def shards(level_fields, wind_field, zonal_step, quad_weight, legendre, wave_table, damping, vertical):
    def rows(x):
        return x.transpose(0, 2, 1, 3)

    vmem = pl.BlockSpec(memory_space=pltpu.VMEM)
    hbm = pl.BlockSpec(memory_space=pl.ANY)
    dma = pltpu.SemaphoreType.DMA
    grid, spec = pl.pallas_call(
        kernel,
        out_shape=(
            jax.ShapeDtypeStruct((2, ROWS, 2, 160), F32),
            jax.ShapeDtypeStruct((32, 160), F32),
        ),
        in_specs=[hbm] * 8,
        out_specs=(vmem, vmem),
        scratch_shapes=[
            pltpu.VMEM((2, 2, ROWS, 2, 160), F32),
            pltpu.VMEM((1, ROWS), F32),
            pltpu.VMEM((1, ROWS), F32),
            pltpu.VMEM((K, M), BF16),
            pltpu.VMEM((5, 128), jnp.int32),
            pltpu.SMEM((2,), F32),
            pltpu.SMEM((2, 2), F32),
            pltpu.VMEM((4, 40, LANES), F32),
            pltpu.VMEM((40, 128), F32),
            pltpu.VMEM((5, 40, 128), F32),
            pltpu.VMEM((2, 8, 128), F32),
            pltpu.VMEM((2, 2, 8, 128), F32),
            pltpu.VMEM((2, 2, 2, 8, LANES), F32),
            pltpu.VMEM((M, 128), F32),
            pltpu.VMEM((M, LANES), BF16),
            pltpu.VMEM((M, LANES), BF16),
            pltpu.VMEM((M, LANES), BF16),
            pltpu.VMEM((M, LANES), BF16),
            pltpu.VMEM((M // 2, LANES), BF16),
            pltpu.VMEM((M // 2, LANES), BF16),
            pltpu.VMEM((M // 2, LANES), BF16),
            pltpu.VMEM((M // 2, LANES), BF16),
            pltpu.VMEM((K, M), BF16),
            pltpu.VMEM((8, FOLDED, 128), F32),
            pltpu.VMEM((8, FOLDED, 128), F32),
            pltpu.VMEM((384, K), BF16),
            pltpu.VMEM((2, BLOCKS, 16, 128), F32),
            pltpu.VMEM((BLOCKS, 16, 128), F32),
            pltpu.VMEM((BLOCKS, 16, 128), F32),
            pltpu.VMEM((CHIPS, 16, 128), F32),
            pltpu.VMEM((64, 128), F32),
            pltpu.VMEM((2, BLOCKS, 16, 128), BF16),
            pltpu.VMEM((16, FOLDED16, 128), BF16),
            dma((8,)), dma((8,)), dma((8,)), dma((2,)), dma((2,)), dma, dma, dma,
            dma, dma, dma, dma, dma, dma, dma, dma,
            dma((8,)), dma, dma, pltpu.SemaphoreType.REGULAR((3,)),
        ],
        compiler_params=pltpu.CompilerParams(
            collective_id=0, has_side_effects=True, vmem_limit_bytes=60 * 1024 * 1024
        ),
    )(
        rows(level_fields), rows(wind_field), zonal_step[None], quad_weight[None],
        legendre.transpose(1, 0, 2).reshape(K, M), wave_table.reshape(5, 128), damping, vertical,
    )
    fields = grid.transpose(0, 2, 1, 3)
    spectrum = spec[:ROWS].reshape(ROWS, 2, 2, SLOTS).transpose(0, 3, 1, 2)
    return fields, spectrum


def solution(mesh):
    return jax.shard_map(
        shards,
        mesh=mesh,
        in_specs=(
            P(None, None, "lat", "lon"),
            P(None, None, "lat", "lon"),
            P("lat"),
            P("lat"),
            P("lon", "lat", None),
            P(),
            P(),
            P(),
        ),
        out_specs=(P(None, None, "lat", "lon"), P("lat", "lon", None, None)),
        check_vma=False,
    )
```

```python
import functools

import jax
import jax.numpy as jnp
from jax import lax
from jax.experimental import pallas as pl
from jax.experimental.pallas import tpu as pltpu
from jax.sharding import PartitionSpec as P

NLON = 2560
M = 640
ROWS = 20
GRID = 80
SLOTS = 40
LANES = 256
K = ROWS * SLOTS
CHIPS = 16
BLOCKS = 16
PACK = 48
FOLDED = 56
FOLDED16 = 64
F32 = jnp.float32
BF16 = jnp.bfloat16
MESH = pl.DeviceIdType.MESH
FAR_FIRST = (12, 13, 15, 11, 14, 10, 9, 4, 8, 5, 7, 3, 6, 2, 1)
Z_FAR_FIRST = (4, 5, 7, 3, 6, 2, 1)


def fiota(shape, dim):
    return lax.broadcasted_iota(jnp.int32, shape, dim).astype(F32)


def fdiv(x, by):
    return jnp.floor((x + 0.5) * (1.0 / by))


def fmod(x, by):
    return x - by * fdiv(x, by)


def dot(a, b):
    return lax.dot_general(a, b, (((1,), (0,)), ((), ())), preferred_element_type=F32)


def dot_nt(a, b):
    return lax.dot_general(a, b, (((1,), (1,)), ((), ())), preferred_element_type=F32)


def split(x):
    high = x.astype(BF16)
    return high, (x - high.astype(F32)).astype(BF16)


def column(row, picked):
    n = row.shape[1]
    rows = picked.shape[0]
    hit = fiota((rows, n), 1) == picked
    return jnp.sum(jnp.where(hit, jnp.broadcast_to(row, (rows, n)), 0.0), axis=1, keepdims=True)


def as_row(col):
    hit = fiota((GRID, 128), 1) == fiota((GRID, 128), 0)
    return jnp.sum(jnp.where(hit, jnp.broadcast_to(col, (GRID, 128)), 0.0), axis=0, keepdims=True)


def trig(waves, first):
    lons = first + fiota((1, LANES), 1)
    turns = waves * lons
    quarter = jnp.floor(turns * (4.0 / NLON) + 0.5)
    rest = turns - quarter * (NLON / 4.0)
    t = rest * (6.283185307179586 / NLON)
    t2 = t * t
    sine = t * (1.0 + t2 * (-1.6666667e-1 + t2 * (8.3333333e-3 + t2 * (-1.9841270e-4 + t2 * 2.7557319e-6))))
    cosine = 1.0 + t2 * (-0.5 + t2 * (4.1666667e-2 + t2 * (-1.3888889e-3 + t2 * 2.4801587e-5)))
    which = quarter.astype(jnp.int32) & 3
    swap = (which & 1) == 1
    c = jnp.where(swap, sine, cosine)
    s = jnp.where(swap, cosine, sine)
    c = jnp.where((which == 1) | (which == 2), -c, c)
    s = jnp.where(which >= 2, s, -s)
    return c, s


def step_field(level, wind, up, down, at_pole, at_equator, east, west, zonal, weight, roll):
    lane = fiota((40, LANES), 1)
    wide = jnp.where(lane == 160.0, east, jnp.where(lane == 255.0, west, level))
    eastward = roll(wide, LANES - 1, 1)
    westward = roll(wide, 1, 1)
    last = level[32:40]
    row8 = fiota((8, LANES), 0)
    swapped = jnp.where(row8 == 0.0, roll(last, 1, 0), roll(last, 3, 0))
    down = jnp.where(at_equator, swapped, down)
    up = jnp.where(at_pole, 0.0, up)
    tall = jnp.concatenate([up, level, down], axis=0)
    toward = roll(tall, 54, 0)[8:48]
    poleward = roll(tall, 2, 0)[8:48]
    change = wind[0] * zonal * (eastward - westward) + 0.25 * wind[1] * (toward - poleward)
    return (level - change) * weight


def row_codes(r):
    parity = fdiv(r, 192.0)
    r1 = fmod(r, 192.0)
    h = fdiv(r1, 96.0)
    c = fdiv(fmod(r1, 96.0), 48.0)
    r2 = fmod(r1, 48.0)
    group = fdiv(r2, 16.0)
    level = fdiv(fmod(r2, 16.0), 8.0)
    pair = group * 8.0 + fmod(r2, 8.0)
    slot = jnp.where(pair < 20.0, 2.0 * pair + parity, -1.0)
    return slot, c, level, h


def folded_rows(slot, c):
    rest = 40.0 + fmod(slot, 8.0) + 8.0 * fdiv(slot, 32.0)
    return slot, jnp.where((c == 1.0) & (slot >= 0.0), rest, -1.0)


def select_rows():
    slot, c, level, h = row_codes(fiota((384, 1), 0))
    lane = fiota((1, FOLDED), 1)
    return tuple(jnp.where(r == lane, 1.0, 0.0).astype(BF16) for r in folded_rows(slot, c))


def select_rows_t():
    slot, c, level, h = row_codes(fiota((1, 384), 1))
    row = fiota((FOLDED16, 1), 0)
    return tuple(jnp.where(r == row, 1.0, 0.0).astype(BF16) for r in folded_rows(slot, c))


def spread_rows():
    lane = fiota((256, 1), 0)
    g = jnp.where(lane < 80.0, lane, jnp.where(lane < 128.0, lane - 80.0, 48.0 + fmod(lane, 32.0)))
    hit = fdiv(fmod(g, 40.0), 2.0) == fdiv(fiota((1, K), 1), 40.0)
    return jnp.where(hit, 1.0, 0.0).astype(BF16)


def level_mask():
    slot, c, level, h = row_codes(fiota((384, 1), 0))
    lane = fiota((1, 256), 1)
    rest = lane >= 128.0
    g = jnp.where(lane < 80.0, lane, jnp.where(rest, 48.0 + fmod(lane, 32.0), lane - 80.0))
    part = jnp.where(lane < 80.0, 0.0, 1.0)
    group = jnp.where(rest, fdiv(lane - 128.0, 32.0), fmod(fdiv(slot, 8.0), 4.0))
    return (
        (level == fdiv(g, 40.0)) & (h == fmod(g, 2.0)) & (c == part)
        & (group == fmod(fdiv(slot, 8.0), 4.0))
    )


def fold(cosine, sine):
    n = cosine.shape[0] // SLOTS
    lane = fiota((1, 1, 128), 2)
    cosine = jnp.reshape(cosine, (n, SLOTS, 128))
    sine = jnp.reshape(sine, (n, SLOTS, 128))
    main = jnp.where(lane < 80.0, cosine, sine)
    rest = jnp.where(lane < 32.0, sine, 0.0)
    first = rest[:, 0:8]
    for b in range(1, 4):
        moved = pltpu.roll(jnp.reshape(rest[:, 8 * b:8 * b + 8], (8 * n, 128)), 32 * b, 1)
        first = first + jnp.reshape(moved, (n, 8, 128))
    return main, first, rest[:, 32:40]


def unfold(folded):
    n = folded.shape[0]
    lane = fiota((1, 1, 128), 2)
    main = folded[:, 0:40]
    first = jnp.reshape(folded[:, 40:48], (8 * n, 128))
    parts = [folded[:, 40:48]]
    for b in range(1, 4):
        parts.append(jnp.reshape(pltpu.roll(first, 128 - 32 * b, 1), (n, 8, 128)))
    parts.append(folded[:, 48:56])
    rest = jnp.concatenate(parts, axis=1)
    cosine = jnp.where(lane < 80.0, main, 0.0)
    sine = jnp.where(lane < 32.0, rest, jnp.where(lane < 80.0, 0.0, main))
    return jnp.reshape(cosine, (n * SLOTS, 128)), jnp.reshape(sine, (n * SLOTS, 128))


def slot_lanes():
    return fmod(fiota((1, K), 1), 40.0)


def reverse_matrix():
    n = fiota((M, M), 0)
    j = fiota((M, M), 1)
    hit = (n + j == M - 2.0) | (n + j == 2.0 * M - 2.0)
    return jnp.where(hit, 1.0, 0.0).astype(BF16)


def first_wave(waves, lon):
    r = fiota((64, 1), 0)
    pair = fdiv(r, 16.0) * 8.0 + fmod(r, 8.0)
    picked = jnp.where(pair < 20.0, lon * 40.0 + 2.0 * pair, -1.0)
    return column(waves, picked)


def parity_sign(first):
    j = fiota((PACK, M), 1)
    odd = (j - first).astype(jnp.int32) & 1
    return jnp.where(odd == 1, -1.0, 1.0)


def spread_weighted(weighted, selector, spreader):
    chosen = jnp.concatenate([dot(q, weighted) for q in selector], axis=1)
    chosen = jnp.where(level_mask(), chosen, 0.0).astype(BF16)
    wide = dot(chosen, spreader)
    slot = row_codes(fiota((384, 1), 0))[0]
    return jnp.where(slot == slot_lanes(), wide, 0.0).astype(BF16)


def pack(even, odd, sign, first, c):
    lo = c * PACK
    hi = 96 + c * PACK
    kept = fiota((PACK, M), 1) >= first
    from_odd = odd[lo:lo + PACK] - sign * odd[hi:hi + PACK]
    packed = jnp.where(kept, even[lo:lo + PACK] + sign * even[hi:hi + PACK], from_odd)
    return packed, from_odd[:, M - 1:M]


def correct(total, first, lane0, extra, damping, vertical):
    j = lane0 + fiota((8, 128), 1)
    n = jnp.where(j >= first, j, (M - 2.0) - j)
    n = jnp.where(extra, M - 1.0, n)
    square = n * (n + 1.0) / float(M * M)
    raw = (total[0:8], total[8:16])
    modal = [
        (vertical[k][0] * raw[0] + vertical[k][1] * raw[1]) / (1.0 + damping[k] * square)
        for k in range(2)
    ]
    return jnp.concatenate(
        [vertical[0][l] * modal[0] + vertical[1][l] * modal[1] for l in range(2)], axis=0
    )


def unpack(packed, extra, first):
    j = fiota((PACK, M), 1)
    kept = j >= first
    even = jnp.where(kept, packed, 0.0)
    odd = jnp.where(j == M - 1.0, extra, jnp.where(kept, 0.0, packed))
    return even, odd


def spectrum_rows(even, odd, lat):
    r = fiota((32, 1), 0)
    n = jnp.where(r < ROWS, lat * ROWS + r, -5.0)
    j = fiota((1, M), 1)
    want_even = jnp.where(n == j, 1.0, 0.0).astype(BF16)
    want_odd = jnp.where((n + j == M - 2.0) | (n + j == 2.0 * M - 2.0), 1.0, 0.0).astype(BF16)
    q = fiota((96, 1), 0)
    c = fdiv(q, 48.0)
    q1 = fmod(q, 48.0)
    level = fdiv(fmod(q1, 16.0), 8.0)
    pair = fdiv(q1, 16.0) * 8.0 + fmod(q1, 8.0)
    lane = fiota((1, 160), 1)
    same = (c == fdiv(lane, 80.0)) & (level == fdiv(fmod(lane, 80.0), 40.0)) & (pair < 20.0)
    slot = fmod(lane, 40.0)
    to_even = jnp.where(same & (slot == 2.0 * pair), 1.0, 0.0).astype(BF16)
    to_odd = jnp.where(same & (slot == 2.0 * pair + 1.0), 1.0, 0.0).astype(BF16)
    return dot(dot_nt(want_even, even).astype(BF16), to_even) + dot(
        dot_nt(want_odd, odd).astype(BF16), to_odd
    )


def collapse(x_even, x_odd, selector_t, spreader):
    both = jnp.concatenate([x_even, x_odd], axis=0)
    slot = row_codes(fiota((384, 1), 0))[0]
    both = jnp.where(slot == slot_lanes(), both, 0.0).astype(BF16)
    rows = dot_nt(both, spreader)
    rows = jnp.where(level_mask(), rows, 0.0).astype(BF16)
    folded = dot(selector_t[0], rows[:, 0:128]) + dot(selector_t[1], rows[:, 128:256])
    return folded.astype(BF16)


def kernel(
    level_hbm, wind_hbm, zonal_hbm, weight_hbm, leg_hbm, wave_hbm, damp_hbm, vert_hbm,
    grid_ref, spec_ref,
    native, zonal_ref, weight_ref, leg_ref, wave_ref, damp_ref, vert_ref,
    field_ref, tail_out, near_in, column_out, column_in, edge_in, wave_col,
    cos_hi, cos_lo, sin_hi, sin_lo, near_cos_hi, near_cos_lo, near_sin_hi, near_sin_lo, reversed_ref, part_out, part_in, spread_ref,
    packed_ref, core_in, sum_out, sum_in, first_ref, gathered, coefs,
    load_sem, edge_send, edge_recv, near_send, near_recv, part_send, part_recv, core_send,
    core_recv, sum_send, sum_recv, all_send, all_recv, pair_send, pair_recv, coef_send,
    coef_recv, fwd_send, fwd_recv, heard,
):
    lat = lax.axis_index("lat")
    lon = lax.axis_index("lon")
    chip = lat // 2
    core = lat % 2
    x_lo = lon // 8
    z = lon % 8
    lat_next, lat_prev = (lat + 1) % 32, (lat + 31) % 32
    lon_next, lon_prev = (lon + 1) % 16, (lon + 15) % 16
    near = (lon + 8) % 16
    sibling = chip * 2 + 1 - core
    flat = lat.astype(F32)
    flon = lon.astype(F32)

    def partners(at, bits):
        flips = [(1 - 2 * ((at // 2**k) % 2)) * 2**k for k in range(bits)]
        return [at + sum(f for k, f in enumerate(flips) if (o >> k) & 1) for o in range(2**bits)]

    chips = partners(chip, 4)
    zs = partners(z, 3)
    lons = [x_lo * 8 + other for other in zs]

    def y_at(offset):
        return ((chip // 8) * 8 + (chip + offset) % 8) * 2 + core

    def tell(sem, device):
        pl.semaphore_signal(sem, inc=1, device_id=device, device_id_type=MESH)

    def send(src, dst, send_sem, recv_sem, device):
        copy = pltpu.make_async_remote_copy(
            src_ref=src, dst_ref=dst, send_sem=send_sem, recv_sem=recv_sem,
            device_id=device, device_id_type=MESH,
        )
        copy.start()
        return copy

    def roll(x, amount, axis):
        return pltpu.roll(x, amount, axis)

    barrier = pltpu.get_barrier_semaphore()

    def greet(device):
        pl.semaphore_signal(barrier, inc=1, device_id=device, device_id_type=MESH)

    loads = [
        pltpu.make_async_copy(src, dst, load_sem.at[n])
        for n, (src, dst) in enumerate((
            (level_hbm, native.at[0]), (wind_hbm, native.at[1]), (wave_hbm, wave_ref),
            (zonal_hbm, zonal_ref), (weight_hbm, weight_ref), (damp_hbm, damp_ref),
            (vert_hbm, vert_ref), (leg_hbm, leg_ref),
        ))
    ]
    for copy in loads:
        copy.start()

    across = ((chip + 8) % CHIPS * 2 + core, lon)
    greet(across)
    for step in (1, 7):
        greet((y_at(step), lon))

    for o in range(1, 8):
        greet((lat, lons[o]))

    edge_devices = (
        ((lat_next, lon), 0, 0), ((lat_prev, lon), 0, 1), ((lat_next, near), 1, 0), ((lat_prev, near), 1, 1),
        ((lat, lon_prev), 0, 0), ((lat, lon_next), 0, 1),
        ((lat, (lon_prev + 8) % 16), 1, 0), ((lat, (lon_next + 8) % 16), 1, 1),
    )
    for device, _, _ in edge_devices:
        greet(device)
    greet((lat, near))

    for copy in loads[:7]:
        copy.wait()

    field_ref[:, :, 128:LANES] = jnp.zeros((4, 40, 128), F32)
    for a in range(2):
        for b in range(2):
            for i in range(ROWS):
                field_ref[2 * a + b, 2 * i:2 * i + 2, 0:160] = native[a, b, i]

    tail = field_ref[0, :, 128:LANES]
    for f in range(1, 4):
        tail = tail + pltpu.roll(field_ref[f, :, 128:LANES], 32 * f, 1)
    tail_out[...] = tail

    flat_level = jnp.reshape(field_ref[0:2], (GRID, LANES))
    column_out[0] = jnp.broadcast_to(as_row(flat_level[:, 0:1]), (8, 128))
    column_out[1] = jnp.broadcast_to(as_row(flat_level[:, 159:160]), (8, 128))
    own_tables = (cos_hi, cos_lo, sin_hi, sin_lo)
    near_tables = (near_cos_hi, near_cos_lo, near_sin_hi, near_sin_lo)

    def fill(source, tables, at, first):
        w = wave_col[pl.ds(pl.multiple_of(source * SLOTS, 80), 2 * SLOTS), 0:1]
        rows = pl.ds(pl.multiple_of(at * SLOTS, 80), 2 * SLOTS)
        c, s = trig(w, first)
        tables[0][rows, :], tables[1][rows, :] = split(c)
        tables[2][rows, :], tables[3][rows, :] = split(s)

    near_first = near.astype(F32) * 160.0

    pl.semaphore_wait(barrier, 3 + 7 + 9)

    edges = []
    for n, (device, block, side) in enumerate(edge_devices):
        if n < 4:
            src = field_ref.at[0:2, 32:40, :] if side == 0 else field_ref.at[0:2, 0:8, :]
            dst = edge_in.at[block, side]
        else:
            src, dst = column_out.at[side], column_in.at[block, side]
        edges.append(send(src, dst, edge_send.at[n], edge_recv.at[n], device))

    to_near = send(field_ref.at[:, :, 0:128], near_in.at[0:4], near_send.at[0], near_recv.at[0], (lat, near))
    to_near2 = send(tail_out, near_in.at[4], near_send.at[1], near_recv.at[1], (lat, near))
    for step in (1, 7):
        tell(heard.at[0], (y_at(step), lon))

    waves = wave_ref[...].astype(F32)
    waves = [waves[t:t + 1, :] for t in range(5)]
    for t in range(5):
        wave_col[128 * t:128 * (t + 1), :] = jnp.broadcast_to(waves[t], (128, 128)).T
    waves = jnp.concatenate(waves, axis=1)
    first_ref[...] = jnp.broadcast_to(first_wave(waves, flon), (64, 128))

    @pl.loop(0, 4)
    def _(zz):
        source = x_lo * 8 + zz * 2
        fill(source, own_tables, source, flon * 160.0)
        fill(source, near_tables, zz * 2, near_first)

    picked = fdiv(fiota((40, 1), 0), 2.0)
    zonal = column(zonal_ref[...], picked)
    weight = column(weight_ref[...], picked) * (1.0 / float(NLON) ** 0.5)
    g = fiota((40, 1), 0)
    first = first_ref[0:PACK, 0:1]
    sign = parity_sign(first)
    selector, spreader = select_rows(), spread_rows()

    for n in (0, 1, 4, 5):
        edges[n].wait()

    pl.semaphore_wait(heard.at[0], 2)
    for step in (2, 6):
        tell(heard.at[1], (y_at(step), lon))

    def advance(block, field):
        levels = []
        for l in range(2):
            east = column(column_in[block, 0, 0:1, :], g + 40.0 * l)
            west = column(column_in[block, 1, 0:1, :], g + 40.0 * l)
            levels.append(step_field(
                field[l], (field[2], field[3]), edge_in[block, 0, l], edge_in[block, 1, l],
                lat == 0, lat == 31, east, west, zonal, weight, roll,
            ))
        return jnp.concatenate(levels, axis=0)

    mine = pl.ds(pl.multiple_of(x_lo * 320, 320), 320)

    def fourier(values, tables, rows):
        zeros = jnp.zeros((48, LANES), F32)
        sums = []
        for part, v in enumerate((
            jnp.concatenate([values, zeros], axis=0),
            jnp.concatenate([values[48:80], zeros, values[0:48]], axis=0),
        )):
            v_hi, v_lo = split(v)
            t_hi, t_lo = tables[2 * part][rows, :], tables[2 * part + 1][rows, :]
            both = dot_nt(t_hi, jnp.concatenate([v_hi, v_lo], axis=0))
            sums.append(both[:, 0:128] + both[:, 128:256] + dot_nt(t_lo, v_hi))
        return sums

    own_sums = fourier(advance(0, field_ref), own_tables, mine)
    for n in (2, 3, 6, 7):
        edges[n].wait()
    to_near.wait()
    to_near2.wait()
    tail = near_in[4]
    in_tail = fiota((40, 128), 1) < 32.0
    field_near = [
        jnp.concatenate(
            [near_in[f], jnp.where(in_tail, pltpu.roll(tail, (128 - 32 * f) % 128, 1) if f else tail, 0.0)], axis=1
        )
        for f in range(4)
    ]
    near_sums = fourier(advance(1, field_near), near_tables, pl.ds(0, 320))
    main, rest, rest2 = fold(*(a + b for a, b in zip(own_sums, near_sums)))
    part_out[:, 0:40, :] = main
    part_out[:, 40:48, :] = rest
    part_out[:, 48:56, :] = rest2

    def remote(src, dst, send_sem, recv_sem, device):
        return pltpu.make_async_remote_copy(
            src_ref=src, dst_ref=dst, send_sem=send_sem, recv_sem=recv_sem,
            device_id=device, device_id_type=MESH,
        )

    def part_copy(o):
        return remote(part_out.at[zs[o]], part_in.at[o], part_send, part_recv, (lat, lons[o]))

    part_all = remote(part_out.at[0:7], part_in.at[1:8], part_send, part_recv, (lat, lons[1]))
    for o in Z_FAR_FIRST:
        part_copy(o).start()

    pl.semaphore_wait(heard.at[1], 2)
    tell(heard.at[2], across)
    part_in[0] = part_out[z]
    loads[7].wait()
    leg = leg_ref[...]
    reversed_ref[...] = dot(leg, reverse_matrix()).astype(BF16)

    part_all.wait_recv()
    weighted = jnp.sum(part_in[...], axis=0).astype(BF16)
    spread_ref[...] = spread_weighted(weighted, selector, spreader)
    even = dot(spread_ref[0:192], leg)
    odd = dot(spread_ref[192:384], reversed_ref[...])
    lane128 = fiota((16, 128), 1)
    for c in range(2):
        packed, extra = pack(even, odd, sign, first, c)
        rest = jnp.zeros((16, 128), F32)
        for kb in range(3):
            for t in range(5):
                packed_ref[c, kb * 5 + t] = packed[16 * kb:16 * (kb + 1), 128 * t:128 * (t + 1)]
            rest = jnp.where(lane128 == float(kb), extra[16 * kb:16 * (kb + 1)], rest)
        packed_ref[c, 15] = rest

    to_core = send(packed_ref.at[1 - core], core_in, core_send, core_recv, (sibling, lon))
    to_core.wait()
    sum_out[...] = packed_ref[core] + core_in[...]
    pl.semaphore_wait(heard.at[2], 1)

    def lat_device(o):
        return (chips[o] * 2 + core, lon)

    def sum_copy(o):
        return remote(sum_out.at[chips[o]], sum_in.at[o], sum_send, sum_recv, lat_device(o))

    sum_all = remote(sum_out.at[0:15], sum_in.at[1:16], sum_send, sum_recv, lat_device(1))
    for o in FAR_FIRST:
        sum_copy(o).start()

    sum_in[0] = sum_out[chip]

    @pl.loop(0, 4)
    def _(zz):
        source = (1 - x_lo) * 8 + zz * 2
        fill(source, own_tables, source, flon * 160.0)


    sum_all.wait_recv()
    total = jnp.sum(sum_in[...], axis=0)
    damping = (damp_ref[0], damp_ref[1])
    vertical = ((vert_ref[0, 0], vert_ref[0, 1]), (vert_ref[1, 0], vert_ref[1, 1]))
    first8 = first_ref[pl.ds(pl.multiple_of((chip // 5) * 16, 8), 8), 0:1]
    lane0 = ((chip % 5) * 128).astype(F32)
    spec = correct(total, first8, lane0, chip == 15, damping, vertical)
    gathered[core, chip] = spec.astype(BF16)

    mine_all = gathered.at[core, chip]
    others = gathered.at[core, 0:15]
    all_all = remote(others, others, all_send, all_recv, lat_device(1))
    for o in FAR_FIRST:
        remote(mine_all, mine_all, all_send, all_recv, lat_device(o)).start()
    all_all.wait_recv()

    to_pair = send(gathered.at[core], gathered.at[core], pair_send, pair_recv, (sibling, lon))
    to_pair.wait()

    evens, odds = [], []
    for c in range(2):
        tiles = [[gathered[c, kb * 5 + t].astype(F32) for t in range(5)] for kb in range(3)]
        packed = jnp.concatenate([jnp.concatenate(row, axis=1) for row in tiles], axis=0)
        last = gathered[c, 15].astype(F32)
        extra = jnp.concatenate([last[:, kb:kb + 1] for kb in range(3)], axis=0)
        e, o = unpack(packed, extra, first)
        evens.append(e)
        odds.append(o)
    scale_even = jnp.where(first == 0.0, 1.0, 2.0)
    scale_odd = jnp.where(first == M - 1.0, 1.0, 2.0)
    north_e = [e * scale_even for e in evens]
    north_o = [o * scale_odd for o in odds]
    rows_e = jnp.concatenate(north_e + [e * sign for e in north_e], axis=0).astype(BF16)
    rows_o = jnp.concatenate(north_o + [-(o * sign) for o in north_o], axis=0).astype(BF16)
    x_even = dot_nt(rows_e, leg)
    x_odd = dot_nt(rows_o, reversed_ref[...])
    coefs[lon] = collapse(x_even, x_odd, select_rows_t(), spreader)

    def coef_copy(o, at):
        return remote(coefs.at[at], coefs.at[at], coef_send, coef_recv.at[o], (lat, lons[o]))

    def forward_copy(o):
        return remote(coefs.at[lons[o]], coefs.at[lons[o]], fwd_send, fwd_recv, (lat, near))

    for o in Z_FAR_FIRST:
        coef_copy(o, lon).start()
    forward_copy(0).start()

    evens = jnp.concatenate(evens, axis=0).astype(BF16)
    odds = jnp.concatenate(odds, axis=0).astype(BF16)
    spec_ref[...] = spectrum_rows(evens, odds, flat)

    for o in (1, 2, 6, 3, 7, 5, 4):
        coef_copy(o, lons[o]).wait_recv()
        forward_copy(o).start()

    def inverse(half):
        rows = pl.ds(pl.multiple_of(half * 320, 320), 320)
        parts = []
        for part, v in enumerate(unfold(coefs[pl.ds(half * 8, 8)].astype(F32))):
            v = v.T.astype(BF16)
            parts.append(dot(v, own_tables[2 * part][rows, :]) + dot(v, own_tables[2 * part + 1][rows, :]))
        return parts[0][0:80] + jnp.concatenate([parts[1][80:128], parts[1][0:32]], axis=0)

    grid = inverse(x_lo)

    forward_all = remote(coefs.at[0:8], coefs.at[0:8], fwd_send, fwd_recv, (lat, near))
    forward_all.wait_recv()

    grid = grid + inverse(1 - x_lo)
    grid = grid * (1.0 / float(NLON * M) ** 0.5)
    for l in range(2):
        for i in range(ROWS):
            at = 40 * l + 2 * i
            grid_ref[l, i] = grid[at:at + 2, 0:160]

    part_all.wait_send()
    sum_all.wait_send()
    all_all.wait_send()
    remote(coefs.at[0:7], coefs.at[0:7], coef_send, coef_recv.at[0], (lat, near)).wait_send()
    forward_all.wait_send()


def shards(level_fields, wind_field, zonal_step, quad_weight, legendre, wave_table, damping, vertical):
    def rows(x):
        return x.transpose(0, 2, 1, 3)

    vmem = pl.BlockSpec(memory_space=pltpu.VMEM)
    hbm = pl.BlockSpec(memory_space=pl.ANY)
    dma = pltpu.SemaphoreType.DMA
    grid, spec = pl.pallas_call(
        kernel,
        out_shape=(
            jax.ShapeDtypeStruct((2, ROWS, 2, 160), F32),
            jax.ShapeDtypeStruct((32, 160), F32),
        ),
        in_specs=[hbm] * 8,
        out_specs=(vmem, vmem),
        scratch_shapes=[
            pltpu.VMEM((2, 2, ROWS, 2, 160), F32),
            pltpu.VMEM((1, ROWS), F32),
            pltpu.VMEM((1, ROWS), F32),
            pltpu.VMEM((K, M), BF16),
            pltpu.VMEM((5, 128), jnp.int32),
            pltpu.SMEM((2,), F32),
            pltpu.SMEM((2, 2), F32),
            pltpu.VMEM((4, 40, LANES), F32),
            pltpu.VMEM((40, 128), F32),
            pltpu.VMEM((5, 40, 128), F32),
            pltpu.VMEM((2, 8, 128), F32),
            pltpu.VMEM((2, 2, 8, 128), F32),
            pltpu.VMEM((2, 2, 2, 8, LANES), F32),
            pltpu.VMEM((M, 128), F32),
            pltpu.VMEM((M, LANES), BF16),
            pltpu.VMEM((M, LANES), BF16),
            pltpu.VMEM((M, LANES), BF16),
            pltpu.VMEM((M, LANES), BF16),
            pltpu.VMEM((M // 2, LANES), BF16),
            pltpu.VMEM((M // 2, LANES), BF16),
            pltpu.VMEM((M // 2, LANES), BF16),
            pltpu.VMEM((M // 2, LANES), BF16),
            pltpu.VMEM((K, M), BF16),
            pltpu.VMEM((8, FOLDED, 128), F32),
            pltpu.VMEM((8, FOLDED, 128), F32),
            pltpu.VMEM((384, K), BF16),
            pltpu.VMEM((2, BLOCKS, 16, 128), F32),
            pltpu.VMEM((BLOCKS, 16, 128), F32),
            pltpu.VMEM((BLOCKS, 16, 128), F32),
            pltpu.VMEM((CHIPS, 16, 128), F32),
            pltpu.VMEM((64, 128), F32),
            pltpu.VMEM((2, BLOCKS, 16, 128), BF16),
            pltpu.VMEM((16, FOLDED16, 128), BF16),
            dma((8,)), dma((8,)), dma((8,)), dma((2,)), dma((2,)), dma, dma, dma,
            dma, dma, dma, dma, dma, dma, dma, dma,
            dma((8,)), dma, dma, pltpu.SemaphoreType.REGULAR((3,)),
        ],
        compiler_params=pltpu.CompilerParams(
            collective_id=0, has_side_effects=True, vmem_limit_bytes=60 * 1024 * 1024
        ),
    )(
        rows(level_fields), rows(wind_field), zonal_step[None], quad_weight[None],
        legendre.transpose(1, 0, 2).reshape(K, M), wave_table.reshape(5, 128), damping, vertical,
    )
    fields = grid.transpose(0, 2, 1, 3)
    spectrum = spec[:ROWS].reshape(ROWS, 2, 2, SLOTS).transpose(0, 3, 1, 2)
    return fields, spectrum


def solution(mesh):
    return jax.shard_map(
        shards,
        mesh=mesh,
        in_specs=(
            P(None, None, "lat", "lon"),
            P(None, None, "lat", "lon"),
            P("lat"),
            P("lat"),
            P("lon", "lat", None),
            P(),
            P(),
            P(),
        ),
        out_specs=(P(None, None, "lat", "lon"), P("lat", "lon", None, None)),
        check_vma=False,
    )
```

```python
import functools

import jax
import jax.numpy as jnp
from jax import lax
from jax.experimental import pallas as pl
from jax.experimental.pallas import tpu as pltpu
from jax.sharding import PartitionSpec as P

NLON = 2560
M = 640
ROWS = 20
GRID = 80
SLOTS = 40
LANES = 256
K = ROWS * SLOTS
CHIPS = 16
BLOCKS = 16
PACK = 48
FOLDED = 56
FOLDED16 = 64
F32 = jnp.float32
BF16 = jnp.bfloat16
MESH = pl.DeviceIdType.MESH
FAR_FIRST = (12, 13, 15, 11, 14, 10, 9, 4, 8, 5, 7, 3, 6, 2, 1)
Z_FAR_FIRST = (4, 5, 7, 3, 6, 2, 1)


def fiota(shape, dim):
    return lax.broadcasted_iota(jnp.int32, shape, dim).astype(F32)


def fdiv(x, by):
    return jnp.floor((x + 0.5) * (1.0 / by))


def fmod(x, by):
    return x - by * fdiv(x, by)


def dot(a, b):
    return lax.dot_general(a, b, (((1,), (0,)), ((), ())), preferred_element_type=F32)


def dot_nt(a, b):
    return lax.dot_general(a, b, (((1,), (1,)), ((), ())), preferred_element_type=F32)


def split(x):
    high = x.astype(BF16)
    return high, (x - high.astype(F32)).astype(BF16)


def column(row, picked):
    n = row.shape[1]
    rows = picked.shape[0]
    hit = fiota((rows, n), 1) == picked
    return jnp.sum(jnp.where(hit, jnp.broadcast_to(row, (rows, n)), 0.0), axis=1, keepdims=True)


def as_row(col):
    hit = fiota((GRID, 128), 1) == fiota((GRID, 128), 0)
    return jnp.sum(jnp.where(hit, jnp.broadcast_to(col, (GRID, 128)), 0.0), axis=0, keepdims=True)


def trig(waves, first):
    lons = first + fiota((1, LANES), 1)
    turns = waves * lons
    quarter = jnp.floor(turns * (4.0 / NLON) + 0.5)
    rest = turns - quarter * (NLON / 4.0)
    t = rest * (6.283185307179586 / NLON)
    t2 = t * t
    sine = t * (1.0 + t2 * (-1.6666667e-1 + t2 * (8.3333333e-3 + t2 * (-1.9841270e-4 + t2 * 2.7557319e-6))))
    cosine = 1.0 + t2 * (-0.5 + t2 * (4.1666667e-2 + t2 * (-1.3888889e-3 + t2 * 2.4801587e-5)))
    which = quarter.astype(jnp.int32) & 3
    swap = (which & 1) == 1
    c = jnp.where(swap, sine, cosine)
    s = jnp.where(swap, cosine, sine)
    c = jnp.where((which == 1) | (which == 2), -c, c)
    s = jnp.where(which >= 2, s, -s)
    return c, s


def step_field(level, wind, up, down, at_pole, at_equator, east, west, zonal, weight, roll):
    lane = fiota((40, LANES), 1)
    wide = jnp.where(lane == 160.0, east, jnp.where(lane == 255.0, west, level))
    eastward = roll(wide, LANES - 1, 1)
    westward = roll(wide, 1, 1)
    last = level[32:40]
    row8 = fiota((8, LANES), 0)
    swapped = jnp.where(row8 == 0.0, roll(last, 1, 0), roll(last, 3, 0))
    down = jnp.where(at_equator, swapped, down)
    up = jnp.where(at_pole, 0.0, up)
    tall = jnp.concatenate([up, level, down], axis=0)
    toward = roll(tall, 54, 0)[8:48]
    poleward = roll(tall, 2, 0)[8:48]
    change = wind[0] * zonal * (eastward - westward) + 0.25 * wind[1] * (toward - poleward)
    return (level - change) * weight


def row_codes(r):
    parity = fdiv(r, 192.0)
    r1 = fmod(r, 192.0)
    h = fdiv(r1, 96.0)
    c = fdiv(fmod(r1, 96.0), 48.0)
    r2 = fmod(r1, 48.0)
    group = fdiv(r2, 16.0)
    level = fdiv(fmod(r2, 16.0), 8.0)
    pair = group * 8.0 + fmod(r2, 8.0)
    slot = jnp.where(pair < 20.0, 2.0 * pair + parity, -1.0)
    return slot, c, level, h


def folded_rows(slot, c):
    rest = 40.0 + fmod(slot, 8.0) + 8.0 * fdiv(slot, 32.0)
    return slot, jnp.where((c == 1.0) & (slot >= 0.0), rest, -1.0)


def select_rows():
    slot, c, level, h = row_codes(fiota((384, 1), 0))
    lane = fiota((1, FOLDED), 1)
    return tuple(jnp.where(r == lane, 1.0, 0.0).astype(BF16) for r in folded_rows(slot, c))


def select_rows_t():
    slot, c, level, h = row_codes(fiota((1, 384), 1))
    row = fiota((FOLDED16, 1), 0)
    return tuple(jnp.where(r == row, 1.0, 0.0).astype(BF16) for r in folded_rows(slot, c))


def spread_rows():
    lane = fiota((256, 1), 0)
    g = jnp.where(lane < 80.0, lane, jnp.where(lane < 128.0, lane - 80.0, 48.0 + fmod(lane, 32.0)))
    hit = fdiv(fmod(g, 40.0), 2.0) == fdiv(fiota((1, K), 1), 40.0)
    return jnp.where(hit, 1.0, 0.0).astype(BF16)


def level_mask():
    slot, c, level, h = row_codes(fiota((384, 1), 0))
    lane = fiota((1, 256), 1)
    rest = lane >= 128.0
    g = jnp.where(lane < 80.0, lane, jnp.where(rest, 48.0 + fmod(lane, 32.0), lane - 80.0))
    part = jnp.where(lane < 80.0, 0.0, 1.0)
    group = jnp.where(rest, fdiv(lane - 128.0, 32.0), fmod(fdiv(slot, 8.0), 4.0))
    return (
        (level == fdiv(g, 40.0)) & (h == fmod(g, 2.0)) & (c == part)
        & (group == fmod(fdiv(slot, 8.0), 4.0))
    )


def fold(cosine, sine):
    n = cosine.shape[0] // SLOTS
    lane = fiota((1, 1, 128), 2)
    cosine = jnp.reshape(cosine, (n, SLOTS, 128))
    sine = jnp.reshape(sine, (n, SLOTS, 128))
    main = jnp.where(lane < 80.0, cosine, sine)
    rest = jnp.where(lane < 32.0, sine, 0.0)
    first = rest[:, 0:8]
    for b in range(1, 4):
        moved = pltpu.roll(jnp.reshape(rest[:, 8 * b:8 * b + 8], (8 * n, 128)), 32 * b, 1)
        first = first + jnp.reshape(moved, (n, 8, 128))
    return main, first, rest[:, 32:40]


def unfold(folded):
    n = folded.shape[0]
    lane = fiota((1, 1, 128), 2)
    main = folded[:, 0:40]
    first = jnp.reshape(folded[:, 40:48], (8 * n, 128))
    parts = [folded[:, 40:48]]
    for b in range(1, 4):
        parts.append(jnp.reshape(pltpu.roll(first, 128 - 32 * b, 1), (n, 8, 128)))
    parts.append(folded[:, 48:56])
    rest = jnp.concatenate(parts, axis=1)
    cosine = jnp.where(lane < 80.0, main, 0.0)
    sine = jnp.where(lane < 32.0, rest, jnp.where(lane < 80.0, 0.0, main))
    return jnp.reshape(cosine, (n * SLOTS, 128)), jnp.reshape(sine, (n * SLOTS, 128))


def slot_lanes():
    return fmod(fiota((1, K), 1), 40.0)


def reverse_matrix():
    n = fiota((M, M), 0)
    j = fiota((M, M), 1)
    hit = (n + j == M - 2.0) | (n + j == 2.0 * M - 2.0)
    return jnp.where(hit, 1.0, 0.0).astype(BF16)


def first_wave(waves, lon):
    r = fiota((64, 1), 0)
    pair = fdiv(r, 16.0) * 8.0 + fmod(r, 8.0)
    picked = jnp.where(pair < 20.0, lon * 40.0 + 2.0 * pair, -1.0)
    return column(waves, picked)


def parity_sign(first):
    j = fiota((PACK, M), 1)
    odd = (j - first).astype(jnp.int32) & 1
    return jnp.where(odd == 1, -1.0, 1.0)


def spread_weighted(weighted, selector, spreader):
    chosen = jnp.concatenate([dot(q, weighted) for q in selector], axis=1)
    chosen = jnp.where(level_mask(), chosen, 0.0).astype(BF16)
    wide = dot(chosen, spreader)
    slot = row_codes(fiota((384, 1), 0))[0]
    return jnp.where(slot == slot_lanes(), wide, 0.0).astype(BF16)


def pack(even, odd, sign, first, c):
    lo = c * PACK
    hi = 96 + c * PACK
    kept = fiota((PACK, M), 1) >= first
    from_odd = odd[lo:lo + PACK] - sign * odd[hi:hi + PACK]
    packed = jnp.where(kept, even[lo:lo + PACK] + sign * even[hi:hi + PACK], from_odd)
    return packed, from_odd[:, M - 1:M]


def correct(total, first, lane0, extra, damping, vertical):
    j = lane0 + fiota((8, 128), 1)
    n = jnp.where(j >= first, j, (M - 2.0) - j)
    n = jnp.where(extra, M - 1.0, n)
    square = n * (n + 1.0) / float(M * M)
    raw = (total[0:8], total[8:16])
    modal = [
        (vertical[k][0] * raw[0] + vertical[k][1] * raw[1]) / (1.0 + damping[k] * square)
        for k in range(2)
    ]
    return jnp.concatenate(
        [vertical[0][l] * modal[0] + vertical[1][l] * modal[1] for l in range(2)], axis=0
    )


def unpack(packed, extra, first):
    j = fiota((PACK, M), 1)
    kept = j >= first
    even = jnp.where(kept, packed, 0.0)
    odd = jnp.where(j == M - 1.0, extra, jnp.where(kept, 0.0, packed))
    return even, odd


def spectrum_rows(even, odd, lat):
    r = fiota((32, 1), 0)
    n = jnp.where(r < ROWS, lat * ROWS + r, -5.0)
    j = fiota((1, M), 1)
    want_even = jnp.where(n == j, 1.0, 0.0).astype(BF16)
    want_odd = jnp.where((n + j == M - 2.0) | (n + j == 2.0 * M - 2.0), 1.0, 0.0).astype(BF16)
    q = fiota((96, 1), 0)
    c = fdiv(q, 48.0)
    q1 = fmod(q, 48.0)
    level = fdiv(fmod(q1, 16.0), 8.0)
    pair = fdiv(q1, 16.0) * 8.0 + fmod(q1, 8.0)
    lane = fiota((1, 160), 1)
    same = (c == fdiv(lane, 80.0)) & (level == fdiv(fmod(lane, 80.0), 40.0)) & (pair < 20.0)
    slot = fmod(lane, 40.0)
    to_even = jnp.where(same & (slot == 2.0 * pair), 1.0, 0.0).astype(BF16)
    to_odd = jnp.where(same & (slot == 2.0 * pair + 1.0), 1.0, 0.0).astype(BF16)
    return dot(dot_nt(want_even, even).astype(BF16), to_even) + dot(
        dot_nt(want_odd, odd).astype(BF16), to_odd
    )


def collapse(x_even, x_odd, selector_t, spreader):
    both = jnp.concatenate([x_even, x_odd], axis=0)
    slot = row_codes(fiota((384, 1), 0))[0]
    both = jnp.where(slot == slot_lanes(), both, 0.0).astype(BF16)
    rows = dot_nt(both, spreader)
    rows = jnp.where(level_mask(), rows, 0.0).astype(BF16)
    folded = dot(selector_t[0], rows[:, 0:128]) + dot(selector_t[1], rows[:, 128:256])
    return folded.astype(BF16)


def kernel(
    level_hbm, wind_hbm, zonal_hbm, weight_hbm, leg_hbm, wave_hbm, damp_hbm, vert_hbm,
    grid_ref, spec_ref,
    native, zonal_ref, weight_ref, leg_ref, wave_ref, damp_ref, vert_ref,
    field_ref, tail_out, near_in, column_out, column_in, edge_in, wave_col,
    cos_hi, cos_lo, sin_hi, sin_lo, near_cos_hi, near_cos_lo, near_sin_hi, near_sin_lo, reversed_ref, part_out, part_in, spread_ref,
    packed_ref, core_in, sum_out, sum_in, first_ref, gathered, coefs,
    load_sem, edge_send, edge_recv, near_send, near_recv, part_send, part_recv, core_send,
    core_recv, sum_send, sum_recv, all_send, all_recv, pair_send, pair_recv, coef_send,
    coef_recv, fwd_send, fwd_recv, heard,
):
    lat = lax.axis_index("lat")
    lon = lax.axis_index("lon")
    chip = lat // 2
    core = lat % 2
    x_lo = lon // 8
    z = lon % 8
    lat_next, lat_prev = (lat + 1) % 32, (lat + 31) % 32
    lon_next, lon_prev = (lon + 1) % 16, (lon + 15) % 16
    near = (lon + 8) % 16
    sibling = chip * 2 + 1 - core
    flat = lat.astype(F32)
    flon = lon.astype(F32)

    def partners(at, bits):
        flips = [(1 - 2 * ((at // 2**k) % 2)) * 2**k for k in range(bits)]
        return [at + sum(f for k, f in enumerate(flips) if (o >> k) & 1) for o in range(2**bits)]

    chips = partners(chip, 4)
    zs = partners(z, 3)
    lons = [x_lo * 8 + other for other in zs]

    def y_at(offset):
        return ((chip // 8) * 8 + (chip + offset) % 8) * 2 + core

    def tell(sem, device):
        pl.semaphore_signal(sem, inc=1, device_id=device, device_id_type=MESH)

    def send(src, dst, send_sem, recv_sem, device):
        copy = pltpu.make_async_remote_copy(
            src_ref=src, dst_ref=dst, send_sem=send_sem, recv_sem=recv_sem,
            device_id=device, device_id_type=MESH,
        )
        copy.start()
        return copy

    def roll(x, amount, axis):
        return pltpu.roll(x, amount, axis)

    barrier = pltpu.get_barrier_semaphore()

    def greet(device):
        pl.semaphore_signal(barrier, inc=1, device_id=device, device_id_type=MESH)

    loads = [
        pltpu.make_async_copy(src, dst, load_sem.at[n])
        for n, (src, dst) in enumerate((
            (level_hbm, native.at[0]), (wind_hbm, native.at[1]), (wave_hbm, wave_ref),
            (zonal_hbm, zonal_ref), (weight_hbm, weight_ref), (damp_hbm, damp_ref),
            (vert_hbm, vert_ref), (leg_hbm, leg_ref),
        ))
    ]
    for copy in loads:
        copy.start()

    across = ((chip + 8) % CHIPS * 2 + core, lon)
    greet(across)
    for step in (1, 7):
        greet((y_at(step), lon))

    for o in range(1, 8):
        greet((lat, lons[o]))

    edge_devices = (
        ((lat_next, lon), 0, 0), ((lat_prev, lon), 0, 1), ((lat_next, near), 1, 0), ((lat_prev, near), 1, 1),
        ((lat, lon_prev), 0, 0), ((lat, lon_next), 0, 1),
        ((lat, (lon_prev + 8) % 16), 1, 0), ((lat, (lon_next + 8) % 16), 1, 1),
    )
    for device, _, _ in edge_devices:
        greet(device)
    greet((lat, near))

    for copy in loads[:7]:
        copy.wait()

    field_ref[:, :, 128:LANES] = jnp.zeros((4, 40, 128), F32)
    for a in range(2):
        for b in range(2):
            for i in range(ROWS):
                field_ref[2 * a + b, 2 * i:2 * i + 2, 0:160] = native[a, b, i]

    tail = field_ref[0, :, 128:LANES]
    for f in range(1, 4):
        tail = tail + pltpu.roll(field_ref[f, :, 128:LANES], 32 * f, 1)
    tail_out[...] = tail

    flat_level = jnp.reshape(field_ref[0:2], (GRID, LANES))
    column_out[0] = jnp.broadcast_to(as_row(flat_level[:, 0:1]), (8, 128))
    column_out[1] = jnp.broadcast_to(as_row(flat_level[:, 159:160]), (8, 128))
    own_tables = (cos_hi, cos_lo, sin_hi, sin_lo)
    near_tables = (near_cos_hi, near_cos_lo, near_sin_hi, near_sin_lo)

    def fill(source, tables, at, first):
        w = wave_col[pl.ds(pl.multiple_of(source * SLOTS, 80), 2 * SLOTS), 0:1]
        rows = pl.ds(pl.multiple_of(at * SLOTS, 80), 2 * SLOTS)
        c, s = trig(w, first)
        tables[0][rows, :], tables[1][rows, :] = split(c)
        tables[2][rows, :], tables[3][rows, :] = split(s)

    near_first = near.astype(F32) * 160.0

    pl.semaphore_wait(barrier, 3 + 7 + 9)

    edges = []
    for n, (device, block, side) in enumerate(edge_devices):
        if n < 4:
            src = field_ref.at[0:2, 32:40, :] if side == 0 else field_ref.at[0:2, 0:8, :]
            dst = edge_in.at[block, side]
        else:
            src, dst = column_out.at[side], column_in.at[block, side]
        edges.append(send(src, dst, edge_send.at[n], edge_recv.at[n], device))

    to_near = send(field_ref.at[:, :, 0:128], near_in.at[0:4], near_send.at[0], near_recv.at[0], (lat, near))
    to_near2 = send(tail_out, near_in.at[4], near_send.at[1], near_recv.at[1], (lat, near))
    for step in (1, 7):
        tell(heard.at[0], (y_at(step), lon))

    waves = wave_ref[...].astype(F32)
    waves = [waves[t:t + 1, :] for t in range(5)]
    for t in range(5):
        wave_col[128 * t:128 * (t + 1), :] = jnp.broadcast_to(waves[t], (128, 128)).T
    waves = jnp.concatenate(waves, axis=1)
    first_ref[...] = jnp.broadcast_to(first_wave(waves, flon), (64, 128))

    @pl.loop(0, 4)
    def _(zz):
        source = x_lo * 8 + zz * 2
        fill(source, own_tables, source, flon * 160.0)
        fill(source, near_tables, zz * 2, near_first)

    picked = fdiv(fiota((40, 1), 0), 2.0)
    zonal = column(zonal_ref[...], picked)
    weight = column(weight_ref[...], picked) * (1.0 / float(NLON) ** 0.5)
    g = fiota((40, 1), 0)
    first = first_ref[0:PACK, 0:1]
    sign = parity_sign(first)
    selector, spreader = select_rows(), spread_rows()

    for n in (0, 1, 4, 5):
        edges[n].wait()

    pl.semaphore_wait(heard.at[0], 2)
    for step in (2, 6):
        tell(heard.at[1], (y_at(step), lon))

    def advance(block, field):
        levels = []
        for l in range(2):
            east = column(column_in[block, 0, 0:1, :], g + 40.0 * l)
            west = column(column_in[block, 1, 0:1, :], g + 40.0 * l)
            levels.append(step_field(
                field[l], (field[2], field[3]), edge_in[block, 0, l], edge_in[block, 1, l],
                lat == 0, lat == 31, east, west, zonal, weight, roll,
            ))
        return jnp.concatenate(levels, axis=0)

    def parts_of(values):
        zeros = jnp.zeros((48, LANES), F32)
        parts = []
        for v in (
            jnp.concatenate([values, zeros], axis=0),
            jnp.concatenate([values[48:80], zeros, values[0:48]], axis=0),
        ):
            v_hi, v_lo = split(v)
            parts.append((jnp.concatenate([v_hi, v_lo], axis=0), v_hi))
        return parts

    def fourier(parts, tables, first_row):
        rows = pl.ds(pl.multiple_of(first_row, 32), 160)
        sums = []
        for part, (v_both, v_hi) in enumerate(parts):
            both = dot_nt(tables[2 * part][rows, :], v_both)
            sums.append(both[:, 0:128] + both[:, 128:256] + dot_nt(tables[2 * part + 1][rows, :], v_hi))
        return sums

    far_half = 1 - z // 4
    halves = (far_half, 1 - far_half)
    own_parts = parts_of(advance(0, field_ref))
    own_sums = [fourier(own_parts, own_tables, x_lo * 320 + half * 160) for half in halves]
    for n in (2, 3, 6, 7):
        edges[n].wait()
    to_near.wait()
    to_near2.wait()
    tail = near_in[4]
    in_tail = fiota((40, 128), 1) < 32.0
    field_near = [
        jnp.concatenate(
            [near_in[f], jnp.where(in_tail, pltpu.roll(tail, (128 - 32 * f) % 128, 1) if f else tail, 0.0)], axis=1
        )
        for f in range(4)
    ]
    def remote(src, dst, send_sem, recv_sem, device):
        return pltpu.make_async_remote_copy(
            src_ref=src, dst_ref=dst, send_sem=send_sem, recv_sem=recv_sem,
            device_id=device, device_id_type=MESH,
        )

    def part_copy(o):
        return remote(part_out.at[zs[o]], part_in.at[o], part_send, part_recv, (lat, lons[o]))

    part_all = remote(part_out.at[0:7], part_in.at[1:8], part_send, part_recv, (lat, lons[1]))
    near_parts = parts_of(advance(1, field_near))
    for n, half in enumerate(halves):
        near_sums = fourier(near_parts, near_tables, half * 160)
        main, rest, rest2 = fold(*(a + b for a, b in zip(own_sums[n], near_sums)))
        block = pl.ds(half * 4, 4)
        part_out[block, 0:40, :] = main
        part_out[block, 40:48, :] = rest
        part_out[block, 48:56, :] = rest2
        for o in Z_FAR_FIRST:
            if (o >= 4) == (n == 0):
                part_copy(o).start()

    pl.semaphore_wait(heard.at[1], 2)
    tell(heard.at[2], across)
    part_in[0] = part_out[z]
    loads[7].wait()
    leg = leg_ref[...]
    reversed_ref[...] = dot(leg, reverse_matrix()).astype(BF16)

    part_all.wait_recv()
    weighted = jnp.sum(part_in[...], axis=0).astype(BF16)
    spread_ref[...] = spread_weighted(weighted, selector, spreader)
    even = dot(spread_ref[0:192], leg)
    odd = dot(spread_ref[192:384], reversed_ref[...])
    lane128 = fiota((16, 128), 1)
    for c in range(2):
        packed, extra = pack(even, odd, sign, first, c)
        rest = jnp.zeros((16, 128), F32)
        for kb in range(3):
            for t in range(5):
                packed_ref[c, kb * 5 + t] = packed[16 * kb:16 * (kb + 1), 128 * t:128 * (t + 1)]
            rest = jnp.where(lane128 == float(kb), extra[16 * kb:16 * (kb + 1)], rest)
        packed_ref[c, 15] = rest

    pl.semaphore_wait(heard.at[2], 1)
    to_core = send(packed_ref.at[1 - core], core_in, core_send, core_recv, (sibling, lon))
    to_core.wait()
    sum_out[...] = packed_ref[core] + core_in[...]

    def lat_device(o):
        return (chips[o] * 2 + core, lon)

    def sum_copy(o):
        return remote(sum_out.at[chips[o]], sum_in.at[o], sum_send, sum_recv, lat_device(o))

    sum_all = remote(sum_out.at[0:15], sum_in.at[1:16], sum_send, sum_recv, lat_device(1))
    for o in FAR_FIRST:
        sum_copy(o).start()

    sum_in[0] = sum_out[chip]

    @pl.loop(0, 4)
    def _(zz):
        source = (1 - x_lo) * 8 + zz * 2
        fill(source, own_tables, source, flon * 160.0)


    sum_all.wait_recv()
    total = jnp.sum(sum_in[...], axis=0)
    damping = (damp_ref[0], damp_ref[1])
    vertical = ((vert_ref[0, 0], vert_ref[0, 1]), (vert_ref[1, 0], vert_ref[1, 1]))
    first8 = first_ref[pl.ds(pl.multiple_of((chip // 5) * 16, 8), 8), 0:1]
    lane0 = ((chip % 5) * 128).astype(F32)
    spec = correct(total, first8, lane0, chip == 15, damping, vertical)
    gathered[core, chip] = spec.astype(BF16)

    mine_all = gathered.at[core, chip]
    others = gathered.at[core, 0:15]
    all_all = remote(others, others, all_send, all_recv, lat_device(1))
    both_all = remote(gathered.at[1 - core], gathered.at[1 - core], pair_send, pair_recv, (sibling, lon))
    for o in FAR_FIRST + (0,):
        if o:
            remote(mine_all, mine_all, all_send, all_recv, lat_device(o)).start()
        remote(mine_all, mine_all, pair_send, pair_recv, (chips[o] * 2 + 1 - core, lon)).start()
    all_all.wait_recv()
    both_all.wait_recv()

    evens, odds = [], []
    for c in range(2):
        tiles = [[gathered[c, kb * 5 + t].astype(F32) for t in range(5)] for kb in range(3)]
        packed = jnp.concatenate([jnp.concatenate(row, axis=1) for row in tiles], axis=0)
        last = gathered[c, 15].astype(F32)
        extra = jnp.concatenate([last[:, kb:kb + 1] for kb in range(3)], axis=0)
        e, o = unpack(packed, extra, first)
        evens.append(e)
        odds.append(o)
    scale_even = jnp.where(first == 0.0, 1.0, 2.0)
    scale_odd = jnp.where(first == M - 1.0, 1.0, 2.0)
    north_e = [e * scale_even for e in evens]
    north_o = [o * scale_odd for o in odds]
    rows_e = jnp.concatenate(north_e + [e * sign for e in north_e], axis=0).astype(BF16)
    rows_o = jnp.concatenate(north_o + [-(o * sign) for o in north_o], axis=0).astype(BF16)
    x_even = dot_nt(rows_e, leg)
    x_odd = dot_nt(rows_o, reversed_ref[...])
    coefs[lon] = collapse(x_even, x_odd, select_rows_t(), spreader)

    def coef_copy(o, at):
        return remote(coefs.at[at], coefs.at[at], coef_send, coef_recv.at[o], (lat, lons[o]))

    def forward_copy(o):
        return remote(coefs.at[lons[o]], coefs.at[lons[o]], fwd_send, fwd_recv, (lat, near))

    for o in Z_FAR_FIRST:
        coef_copy(o, lon).start()
    forward_copy(0).start()

    evens = jnp.concatenate(evens, axis=0).astype(BF16)
    odds = jnp.concatenate(odds, axis=0).astype(BF16)
    spec_ref[...] = spectrum_rows(evens, odds, flat)

    for o in (1, 2, 6, 3, 7, 5, 4):
        coef_copy(o, lons[o]).wait_recv()
        forward_copy(o).start()

    def inverse(half):
        rows = pl.ds(pl.multiple_of(half * 320, 320), 320)
        parts = []
        for part, v in enumerate(unfold(coefs[pl.ds(half * 8, 8)].astype(F32))):
            v = v.T.astype(BF16)
            parts.append(dot(v, own_tables[2 * part][rows, :]) + dot(v, own_tables[2 * part + 1][rows, :]))
        return parts[0][0:80] + jnp.concatenate([parts[1][80:128], parts[1][0:32]], axis=0)

    grid = inverse(x_lo)

    forward_all = remote(coefs.at[0:8], coefs.at[0:8], fwd_send, fwd_recv, (lat, near))
    forward_all.wait_recv()

    grid = grid + inverse(1 - x_lo)
    grid = grid * (1.0 / float(NLON * M) ** 0.5)
    for l in range(2):
        for i in range(ROWS):
            at = 40 * l + 2 * i
            grid_ref[l, i] = grid[at:at + 2, 0:160]

    part_all.wait_send()
    sum_all.wait_send()
    all_all.wait_send()
    both_all.wait_send()
    remote(coefs.at[0:7], coefs.at[0:7], coef_send, coef_recv.at[0], (lat, near)).wait_send()
    forward_all.wait_send()


def shards(level_fields, wind_field, zonal_step, quad_weight, legendre, wave_table, damping, vertical):
    def rows(x):
        return x.transpose(0, 2, 1, 3)

    vmem = pl.BlockSpec(memory_space=pltpu.VMEM)
    hbm = pl.BlockSpec(memory_space=pl.ANY)
    dma = pltpu.SemaphoreType.DMA
    grid, spec = pl.pallas_call(
        kernel,
        out_shape=(
            jax.ShapeDtypeStruct((2, ROWS, 2, 160), F32),
            jax.ShapeDtypeStruct((32, 160), F32),
        ),
        in_specs=[hbm] * 8,
        out_specs=(vmem, vmem),
        scratch_shapes=[
            pltpu.VMEM((2, 2, ROWS, 2, 160), F32),
            pltpu.VMEM((1, ROWS), F32),
            pltpu.VMEM((1, ROWS), F32),
            pltpu.VMEM((K, M), BF16),
            pltpu.VMEM((5, 128), jnp.int32),
            pltpu.SMEM((2,), F32),
            pltpu.SMEM((2, 2), F32),
            pltpu.VMEM((4, 40, LANES), F32),
            pltpu.VMEM((40, 128), F32),
            pltpu.VMEM((5, 40, 128), F32),
            pltpu.VMEM((2, 8, 128), F32),
            pltpu.VMEM((2, 2, 8, 128), F32),
            pltpu.VMEM((2, 2, 2, 8, LANES), F32),
            pltpu.VMEM((M, 128), F32),
            pltpu.VMEM((M, LANES), BF16),
            pltpu.VMEM((M, LANES), BF16),
            pltpu.VMEM((M, LANES), BF16),
            pltpu.VMEM((M, LANES), BF16),
            pltpu.VMEM((M // 2, LANES), BF16),
            pltpu.VMEM((M // 2, LANES), BF16),
            pltpu.VMEM((M // 2, LANES), BF16),
            pltpu.VMEM((M // 2, LANES), BF16),
            pltpu.VMEM((K, M), BF16),
            pltpu.VMEM((8, FOLDED, 128), F32),
            pltpu.VMEM((8, FOLDED, 128), F32),
            pltpu.VMEM((384, K), BF16),
            pltpu.VMEM((2, BLOCKS, 16, 128), F32),
            pltpu.VMEM((BLOCKS, 16, 128), F32),
            pltpu.VMEM((BLOCKS, 16, 128), F32),
            pltpu.VMEM((CHIPS, 16, 128), F32),
            pltpu.VMEM((64, 128), F32),
            pltpu.VMEM((2, BLOCKS, 16, 128), BF16),
            pltpu.VMEM((16, FOLDED16, 128), BF16),
            dma((8,)), dma((8,)), dma((8,)), dma((2,)), dma((2,)), dma, dma, dma,
            dma, dma, dma, dma, dma, dma, dma, dma,
            dma((8,)), dma, dma, pltpu.SemaphoreType.REGULAR((3,)),
        ],
        compiler_params=pltpu.CompilerParams(
            collective_id=0, has_side_effects=True, vmem_limit_bytes=60 * 1024 * 1024
        ),
    )(
        rows(level_fields), rows(wind_field), zonal_step[None], quad_weight[None],
        legendre.transpose(1, 0, 2).reshape(K, M), wave_table.reshape(5, 128), damping, vertical,
    )
    fields = grid.transpose(0, 2, 1, 3)
    spectrum = spec[:ROWS].reshape(ROWS, 2, 2, SLOTS).transpose(0, 3, 1, 2)
    return fields, spectrum


def solution(mesh):
    return jax.shard_map(
        shards,
        mesh=mesh,
        in_specs=(
            P(None, None, "lat", "lon"),
            P(None, None, "lat", "lon"),
            P("lat"),
            P("lat"),
            P("lon", "lat", None),
            P(),
            P(),
            P(),
        ),
        out_specs=(P(None, None, "lat", "lon"), P("lat", "lon", None, None)),
        check_vma=False,
    )
```

```python
import functools

import jax
import jax.numpy as jnp
from jax import lax
from jax.experimental import pallas as pl
from jax.experimental.pallas import tpu as pltpu
from jax.sharding import PartitionSpec as P

NLON = 2560
M = 640
ROWS = 20
GRID = 80
SLOTS = 40
LANES = 256
K = ROWS * SLOTS
CHIPS = 16
BLOCKS = 16
PACK = 48
FOLDED = 56
FOLDED16 = 64
F32 = jnp.float32
BF16 = jnp.bfloat16
MESH = pl.DeviceIdType.MESH
FAR_FIRST = (12, 13, 15, 11, 14, 10, 9, 4, 8, 5, 7, 3, 6, 2, 1)
Z_FAR_FIRST = (4, 5, 7, 3, 6, 2, 1)


def fiota(shape, dim):
    return lax.broadcasted_iota(jnp.int32, shape, dim).astype(F32)


def fdiv(x, by):
    return jnp.floor((x + 0.5) * (1.0 / by))


def fmod(x, by):
    return x - by * fdiv(x, by)


def dot(a, b):
    return lax.dot_general(a, b, (((1,), (0,)), ((), ())), preferred_element_type=F32)


def dot_nt(a, b):
    return lax.dot_general(a, b, (((1,), (1,)), ((), ())), preferred_element_type=F32)


def split(x):
    high = x.astype(BF16)
    return high, (x - high.astype(F32)).astype(BF16)


def column(row, picked):
    n = row.shape[1]
    rows = picked.shape[0]
    hit = fiota((rows, n), 1) == picked
    return jnp.sum(jnp.where(hit, jnp.broadcast_to(row, (rows, n)), 0.0), axis=1, keepdims=True)


def as_row(col):
    hit = fiota((GRID, 128), 1) == fiota((GRID, 128), 0)
    return jnp.sum(jnp.where(hit, jnp.broadcast_to(col, (GRID, 128)), 0.0), axis=0, keepdims=True)


def trig(waves, first):
    lons = first + fiota((1, LANES), 1)
    turns = waves * lons
    quarter = jnp.floor(turns * (4.0 / NLON) + 0.5)
    rest = turns - quarter * (NLON / 4.0)
    t = rest * (6.283185307179586 / NLON)
    t2 = t * t
    sine = t * (1.0 + t2 * (-1.6666667e-1 + t2 * (8.3333333e-3 + t2 * (-1.9841270e-4 + t2 * 2.7557319e-6))))
    cosine = 1.0 + t2 * (-0.5 + t2 * (4.1666667e-2 + t2 * (-1.3888889e-3 + t2 * 2.4801587e-5)))
    which = quarter.astype(jnp.int32) & 3
    swap = (which & 1) == 1
    c = jnp.where(swap, sine, cosine)
    s = jnp.where(swap, cosine, sine)
    c = jnp.where((which == 1) | (which == 2), -c, c)
    s = jnp.where(which >= 2, s, -s)
    return c, s


def step_field(level, wind, up, down, at_pole, at_equator, east, west, zonal, weight, roll):
    lane = fiota((40, LANES), 1)
    wide = jnp.where(lane == 160.0, east, jnp.where(lane == 255.0, west, level))
    eastward = roll(wide, LANES - 1, 1)
    westward = roll(wide, 1, 1)
    last = level[32:40]
    row8 = fiota((8, LANES), 0)
    swapped = jnp.where(row8 == 0.0, roll(last, 1, 0), roll(last, 3, 0))
    down = jnp.where(at_equator, swapped, down)
    up = jnp.where(at_pole, 0.0, up)
    tall = jnp.concatenate([up, level, down], axis=0)
    toward = roll(tall, 54, 0)[8:48]
    poleward = roll(tall, 2, 0)[8:48]
    change = wind[0] * zonal * (eastward - westward) + 0.25 * wind[1] * (toward - poleward)
    return (level - change) * weight


def row_codes(r):
    parity = fdiv(r, 192.0)
    r1 = fmod(r, 192.0)
    h = fdiv(r1, 96.0)
    c = fdiv(fmod(r1, 96.0), 48.0)
    r2 = fmod(r1, 48.0)
    group = fdiv(r2, 16.0)
    level = fdiv(fmod(r2, 16.0), 8.0)
    pair = group * 8.0 + fmod(r2, 8.0)
    slot = jnp.where(pair < 20.0, 2.0 * pair + parity, -1.0)
    return slot, c, level, h


def folded_rows(slot, c):
    rest = 40.0 + fmod(slot, 8.0) + 8.0 * fdiv(slot, 32.0)
    return slot, jnp.where((c == 1.0) & (slot >= 0.0), rest, -1.0)


def select_rows():
    slot, c, level, h = row_codes(fiota((384, 1), 0))
    lane = fiota((1, FOLDED), 1)
    return tuple(jnp.where(r == lane, 1.0, 0.0).astype(BF16) for r in folded_rows(slot, c))


def select_rows_t():
    slot, c, level, h = row_codes(fiota((1, 384), 1))
    row = fiota((FOLDED16, 1), 0)
    return tuple(jnp.where(r == row, 1.0, 0.0).astype(BF16) for r in folded_rows(slot, c))


def spread_rows():
    lane = fiota((256, 1), 0)
    g = jnp.where(lane < 80.0, lane, jnp.where(lane < 128.0, lane - 80.0, 48.0 + fmod(lane, 32.0)))
    hit = fdiv(fmod(g, 40.0), 2.0) == fdiv(fiota((1, K), 1), 40.0)
    return jnp.where(hit, 1.0, 0.0).astype(BF16)


def level_mask():
    slot, c, level, h = row_codes(fiota((384, 1), 0))
    lane = fiota((1, 256), 1)
    rest = lane >= 128.0
    g = jnp.where(lane < 80.0, lane, jnp.where(rest, 48.0 + fmod(lane, 32.0), lane - 80.0))
    part = jnp.where(lane < 80.0, 0.0, 1.0)
    group = jnp.where(rest, fdiv(lane - 128.0, 32.0), fmod(fdiv(slot, 8.0), 4.0))
    return (
        (level == fdiv(g, 40.0)) & (h == fmod(g, 2.0)) & (c == part)
        & (group == fmod(fdiv(slot, 8.0), 4.0))
    )


def fold(cosine, sine):
    n = cosine.shape[0] // SLOTS
    lane = fiota((1, 1, 128), 2)
    cosine = jnp.reshape(cosine, (n, SLOTS, 128))
    sine = jnp.reshape(sine, (n, SLOTS, 128))
    main = jnp.where(lane < 80.0, cosine, sine)
    rest = jnp.where(lane < 32.0, sine, 0.0)
    first = rest[:, 0:8]
    for b in range(1, 4):
        moved = pltpu.roll(jnp.reshape(rest[:, 8 * b:8 * b + 8], (8 * n, 128)), 32 * b, 1)
        first = first + jnp.reshape(moved, (n, 8, 128))
    return main, first, rest[:, 32:40]


def unfold(folded):
    n = folded.shape[0]
    lane = fiota((1, 1, 128), 2)
    main = folded[:, 0:40]
    first = jnp.reshape(folded[:, 40:48], (8 * n, 128))
    parts = [folded[:, 40:48]]
    for b in range(1, 4):
        parts.append(jnp.reshape(pltpu.roll(first, 128 - 32 * b, 1), (n, 8, 128)))
    parts.append(folded[:, 48:56])
    rest = jnp.concatenate(parts, axis=1)
    cosine = jnp.where(lane < 80.0, main, 0.0)
    sine = jnp.where(lane < 32.0, rest, jnp.where(lane < 80.0, 0.0, main))
    return jnp.reshape(cosine, (n * SLOTS, 128)), jnp.reshape(sine, (n * SLOTS, 128))


def slot_lanes():
    return fmod(fiota((1, K), 1), 40.0)


def reverse_matrix():
    n = fiota((M, M), 0)
    j = fiota((M, M), 1)
    hit = (n + j == M - 2.0) | (n + j == 2.0 * M - 2.0)
    return jnp.where(hit, 1.0, 0.0).astype(BF16)


def first_wave(waves, lon):
    r = fiota((64, 1), 0)
    pair = fdiv(r, 16.0) * 8.0 + fmod(r, 8.0)
    picked = jnp.where(pair < 20.0, lon * 40.0 + 2.0 * pair, -1.0)
    return column(waves, picked)


def parity_sign(first):
    j = fiota((PACK, M), 1)
    odd = (j - first).astype(jnp.int32) & 1
    return jnp.where(odd == 1, -1.0, 1.0)


def spread_weighted(weighted, selector, spreader):
    chosen = jnp.concatenate([dot(q, weighted) for q in selector], axis=1)
    chosen = jnp.where(level_mask(), chosen, 0.0).astype(BF16)
    wide = dot(chosen, spreader)
    slot = row_codes(fiota((384, 1), 0))[0]
    return jnp.where(slot == slot_lanes(), wide, 0.0).astype(BF16)


def pack(even, odd, sign, first, c):
    lo = c * PACK
    hi = 96 + c * PACK
    kept = fiota((PACK, M), 1) >= first
    from_odd = odd[lo:lo + PACK] - sign * odd[hi:hi + PACK]
    packed = jnp.where(kept, even[lo:lo + PACK] + sign * even[hi:hi + PACK], from_odd)
    return packed, from_odd[:, M - 1:M]


def correct(total, first, lane0, extra, damping, vertical):
    j = lane0 + fiota((8, 128), 1)
    n = jnp.where(j >= first, j, (M - 2.0) - j)
    n = jnp.where(extra, M - 1.0, n)
    square = n * (n + 1.0) / float(M * M)
    raw = (total[0:8], total[8:16])
    modal = [
        (vertical[k][0] * raw[0] + vertical[k][1] * raw[1]) / (1.0 + damping[k] * square)
        for k in range(2)
    ]
    return jnp.concatenate(
        [vertical[0][l] * modal[0] + vertical[1][l] * modal[1] for l in range(2)], axis=0
    )


def unpack(packed, extra, first):
    j = fiota((PACK, M), 1)
    kept = j >= first
    even = jnp.where(kept, packed, 0.0)
    odd = jnp.where(j == M - 1.0, extra, jnp.where(kept, 0.0, packed))
    return even, odd


def spectrum_rows(even, odd, lat):
    r = fiota((32, 1), 0)
    n = jnp.where(r < ROWS, lat * ROWS + r, -5.0)
    j = fiota((1, M), 1)
    want_even = jnp.where(n == j, 1.0, 0.0).astype(BF16)
    want_odd = jnp.where((n + j == M - 2.0) | (n + j == 2.0 * M - 2.0), 1.0, 0.0).astype(BF16)
    q = fiota((96, 1), 0)
    c = fdiv(q, 48.0)
    q1 = fmod(q, 48.0)
    level = fdiv(fmod(q1, 16.0), 8.0)
    pair = fdiv(q1, 16.0) * 8.0 + fmod(q1, 8.0)
    lane = fiota((1, 160), 1)
    same = (c == fdiv(lane, 80.0)) & (level == fdiv(fmod(lane, 80.0), 40.0)) & (pair < 20.0)
    slot = fmod(lane, 40.0)
    to_even = jnp.where(same & (slot == 2.0 * pair), 1.0, 0.0).astype(BF16)
    to_odd = jnp.where(same & (slot == 2.0 * pair + 1.0), 1.0, 0.0).astype(BF16)
    return dot(dot_nt(want_even, even).astype(BF16), to_even) + dot(
        dot_nt(want_odd, odd).astype(BF16), to_odd
    )


def collapse(x_even, x_odd, selector_t, spreader):
    both = jnp.concatenate([x_even, x_odd], axis=0)
    slot = row_codes(fiota((384, 1), 0))[0]
    both = jnp.where(slot == slot_lanes(), both, 0.0).astype(BF16)
    rows = dot_nt(both, spreader)
    rows = jnp.where(level_mask(), rows, 0.0).astype(BF16)
    folded = dot(selector_t[0], rows[:, 0:128]) + dot(selector_t[1], rows[:, 128:256])
    return folded.astype(BF16)


def kernel(
    level_hbm, wind_hbm, zonal_hbm, weight_hbm, leg_hbm, wave_hbm, damp_hbm, vert_hbm,
    grid_ref, spec_ref,
    native, zonal_ref, weight_ref, leg_ref, wave_ref, damp_ref, vert_ref,
    field_ref, tail_out, near_in, column_out, column_in, edge_in, wave_col,
    cos_hi, cos_lo, sin_hi, sin_lo, near_cos_hi, near_cos_lo, near_sin_hi, near_sin_lo, reversed_ref, part_out, part_in, spread_ref,
    packed_ref, core_in, sum_out, sum_in, first_ref, gathered, coefs,
    load_sem, edge_send, edge_recv, near_send, near_recv, part_send, part_recv, core_send,
    core_recv, sum_send, sum_recv, all_send, all_recv, pair_send, pair_recv, coef_send,
    coef_recv, fwd_send, fwd_recv, heard,
):
    lat = lax.axis_index("lat")
    lon = lax.axis_index("lon")
    chip = lat // 2
    core = lat % 2
    x_lo = lon // 8
    z = lon % 8
    lat_next, lat_prev = (lat + 1) % 32, (lat + 31) % 32
    lon_next, lon_prev = (lon + 1) % 16, (lon + 15) % 16
    near = (lon + 8) % 16
    sibling = chip * 2 + 1 - core
    flat = lat.astype(F32)
    flon = lon.astype(F32)

    def partners(at, bits):
        flips = [(1 - 2 * ((at // 2**k) % 2)) * 2**k for k in range(bits)]
        return [at + sum(f for k, f in enumerate(flips) if (o >> k) & 1) for o in range(2**bits)]

    chips = partners(chip, 4)
    zs = partners(z, 3)
    lons = [x_lo * 8 + other for other in zs]

    def y_at(offset):
        return ((chip // 8) * 8 + (chip + offset) % 8) * 2 + core

    def tell(sem, device):
        pl.semaphore_signal(sem, inc=1, device_id=device, device_id_type=MESH)

    def send(src, dst, send_sem, recv_sem, device):
        copy = pltpu.make_async_remote_copy(
            src_ref=src, dst_ref=dst, send_sem=send_sem, recv_sem=recv_sem,
            device_id=device, device_id_type=MESH,
        )
        copy.start()
        return copy

    def roll(x, amount, axis):
        return pltpu.roll(x, amount, axis)

    barrier = pltpu.get_barrier_semaphore()

    def greet(device):
        pl.semaphore_signal(barrier, inc=1, device_id=device, device_id_type=MESH)

    loads = [
        pltpu.make_async_copy(src, dst, load_sem.at[n])
        for n, (src, dst) in enumerate((
            (level_hbm, native.at[0]), (wind_hbm, native.at[1]), (wave_hbm, wave_ref),
            (zonal_hbm, zonal_ref), (weight_hbm, weight_ref), (damp_hbm, damp_ref),
            (vert_hbm, vert_ref), (leg_hbm, leg_ref),
        ))
    ]
    for copy in loads:
        copy.start()

    across = ((chip + 8) % CHIPS * 2 + core, lon)
    greet(across)
    for step in (1, 7):
        greet((y_at(step), lon))

    for o in range(1, 8):
        greet((lat, lons[o]))

    edge_devices = (
        ((lat_next, lon), 0, 0), ((lat_prev, lon), 0, 1), ((lat_next, near), 1, 0), ((lat_prev, near), 1, 1),
        ((lat, lon_prev), 0, 0), ((lat, lon_next), 0, 1),
        ((lat, (lon_prev + 8) % 16), 1, 0), ((lat, (lon_next + 8) % 16), 1, 1),
    )
    for device, _, _ in edge_devices:
        greet(device)
    greet((lat, near))

    for copy in loads[:2]:
        copy.wait()

    field_ref[:, :, 128:LANES] = jnp.zeros((4, 40, 128), F32)
    for a in range(2):
        for b in range(2):
            for i in range(ROWS):
                field_ref[2 * a + b, 2 * i:2 * i + 2, 0:160] = native[a, b, i]

    tail = field_ref[0, :, 128:LANES]
    for f in range(1, 4):
        tail = tail + pltpu.roll(field_ref[f, :, 128:LANES], 32 * f, 1)
    tail_out[...] = tail

    flat_level = jnp.reshape(field_ref[0:2], (GRID, LANES))
    column_out[0] = jnp.broadcast_to(as_row(flat_level[:, 0:1]), (8, 128))
    column_out[1] = jnp.broadcast_to(as_row(flat_level[:, 159:160]), (8, 128))
    own_tables = (cos_hi, cos_lo, sin_hi, sin_lo)
    near_tables = (near_cos_hi, near_cos_lo, near_sin_hi, near_sin_lo)

    def fill(source, tables, at, first):
        w = wave_col[pl.ds(pl.multiple_of(source * SLOTS, 80), 2 * SLOTS), 0:1]
        rows = pl.ds(pl.multiple_of(at * SLOTS, 80), 2 * SLOTS)
        c, s = trig(w, first)
        tables[0][rows, :], tables[1][rows, :] = split(c)
        tables[2][rows, :], tables[3][rows, :] = split(s)

    near_first = near.astype(F32) * 160.0

    pl.semaphore_wait(barrier, 3 + 7 + 9)

    edges = []
    for n, (device, block, side) in enumerate(edge_devices):
        if n < 4:
            src = field_ref.at[0:2, 32:40, :] if side == 0 else field_ref.at[0:2, 0:8, :]
            dst = edge_in.at[block, side]
        else:
            src, dst = column_out.at[side], column_in.at[block, side]
        edges.append(send(src, dst, edge_send.at[n], edge_recv.at[n], device))

    to_near = send(field_ref.at[:, :, 0:128], near_in.at[0:4], near_send.at[0], near_recv.at[0], (lat, near))
    to_near2 = send(tail_out, near_in.at[4], near_send.at[1], near_recv.at[1], (lat, near))
    for step in (1, 7):
        tell(heard.at[0], (y_at(step), lon))

    for copy in loads[2:7]:
        copy.wait()
    waves = wave_ref[...].astype(F32)
    waves = [waves[t:t + 1, :] for t in range(5)]
    for t in range(5):
        wave_col[128 * t:128 * (t + 1), :] = jnp.broadcast_to(waves[t], (128, 128)).T
    waves = jnp.concatenate(waves, axis=1)
    first_ref[...] = jnp.broadcast_to(first_wave(waves, flon), (64, 128))

    @pl.loop(0, 4)
    def _(zz):
        source = x_lo * 8 + zz * 2
        fill(source, own_tables, source, flon * 160.0)

    picked = fdiv(fiota((40, 1), 0), 2.0)
    zonal = column(zonal_ref[...], picked)
    weight = column(weight_ref[...], picked) * (1.0 / float(NLON) ** 0.5)
    g = fiota((40, 1), 0)
    first = first_ref[0:PACK, 0:1]
    sign = parity_sign(first)
    selector, spreader = select_rows(), spread_rows()

    for n in (0, 1, 4, 5):
        edges[n].wait()

    pl.semaphore_wait(heard.at[0], 2)
    for step in (2, 6):
        tell(heard.at[1], (y_at(step), lon))

    def advance(block, field):
        levels = []
        for l in range(2):
            east = column(column_in[block, 0, 0:1, :], g + 40.0 * l)
            west = column(column_in[block, 1, 0:1, :], g + 40.0 * l)
            levels.append(step_field(
                field[l], (field[2], field[3]), edge_in[block, 0, l], edge_in[block, 1, l],
                lat == 0, lat == 31, east, west, zonal, weight, roll,
            ))
        return jnp.concatenate(levels, axis=0)

    def parts_of(values):
        zeros = jnp.zeros((48, LANES), F32)
        parts = []
        for v in (
            jnp.concatenate([values, zeros], axis=0),
            jnp.concatenate([values[48:80], zeros, values[0:48]], axis=0),
        ):
            v_hi, v_lo = split(v)
            parts.append((jnp.concatenate([v_hi, v_lo], axis=0), v_hi))
        return parts

    def fourier(parts, tables, first_row):
        rows = pl.ds(pl.multiple_of(first_row, 32), 160)
        sums = []
        for part, (v_both, v_hi) in enumerate(parts):
            both = dot_nt(tables[2 * part][rows, :], v_both)
            sums.append(both[:, 0:128] + both[:, 128:256] + dot_nt(tables[2 * part + 1][rows, :], v_hi))
        return sums

    far_half = 1 - z // 4
    halves = (far_half, 1 - far_half)
    own_parts = parts_of(advance(0, field_ref))
    own_sums = [fourier(own_parts, own_tables, x_lo * 320 + half * 160) for half in halves]

    @pl.loop(0, 4)
    def _(zz):
        fill(x_lo * 8 + zz * 2, near_tables, zz * 2, near_first)

    for n in (2, 3, 6, 7):
        edges[n].wait()
    to_near.wait()
    to_near2.wait()
    tail = near_in[4]
    in_tail = fiota((40, 128), 1) < 32.0
    field_near = [
        jnp.concatenate(
            [near_in[f], jnp.where(in_tail, pltpu.roll(tail, (128 - 32 * f) % 128, 1) if f else tail, 0.0)], axis=1
        )
        for f in range(4)
    ]
    def remote(src, dst, send_sem, recv_sem, device):
        return pltpu.make_async_remote_copy(
            src_ref=src, dst_ref=dst, send_sem=send_sem, recv_sem=recv_sem,
            device_id=device, device_id_type=MESH,
        )

    def part_copy(o):
        return remote(part_out.at[zs[o]], part_in.at[o], part_send, part_recv, (lat, lons[o]))

    part_all = remote(part_out.at[0:7], part_in.at[1:8], part_send, part_recv, (lat, lons[1]))
    near_parts = parts_of(advance(1, field_near))
    for n, half in enumerate(halves):
        near_sums = fourier(near_parts, near_tables, half * 160)
        main, rest, rest2 = fold(*(a + b for a, b in zip(own_sums[n], near_sums)))
        block = pl.ds(half * 4, 4)
        part_out[block, 0:40, :] = main
        part_out[block, 40:48, :] = rest
        part_out[block, 48:56, :] = rest2
        for o in Z_FAR_FIRST:
            if (o >= 4) == (n == 0):
                part_copy(o).start()

    pl.semaphore_wait(heard.at[1], 2)
    tell(heard.at[2], across)
    part_in[0] = part_out[z]
    loads[7].wait()
    leg = leg_ref[...]
    reversed_ref[...] = dot(leg, reverse_matrix()).astype(BF16)

    part_all.wait_recv()
    weighted = jnp.sum(part_in[...], axis=0).astype(BF16)
    spread_ref[...] = spread_weighted(weighted, selector, spreader)
    even = dot(spread_ref[0:192], leg)
    odd = dot(spread_ref[192:384], reversed_ref[...])
    lane128 = fiota((16, 128), 1)
    for c in range(2):
        packed, extra = pack(even, odd, sign, first, c)
        rest = jnp.zeros((16, 128), F32)
        for kb in range(3):
            for t in range(5):
                packed_ref[c, kb * 5 + t] = packed[16 * kb:16 * (kb + 1), 128 * t:128 * (t + 1)]
            rest = jnp.where(lane128 == float(kb), extra[16 * kb:16 * (kb + 1)], rest)
        packed_ref[c, 15] = rest

    pl.semaphore_wait(heard.at[2], 1)
    to_core = send(packed_ref.at[1 - core], core_in, core_send, core_recv, (sibling, lon))
    to_core.wait()
    sum_out[...] = packed_ref[core] + core_in[...]

    def lat_device(o):
        return (chips[o] * 2 + core, lon)

    def sum_copy(o):
        return remote(sum_out.at[chips[o]], sum_in.at[o], sum_send, sum_recv, lat_device(o))

    sum_all = remote(sum_out.at[0:15], sum_in.at[1:16], sum_send, sum_recv, lat_device(1))
    for o in FAR_FIRST:
        sum_copy(o).start()

    sum_in[0] = sum_out[chip]

    @pl.loop(0, 4)
    def _(zz):
        source = (1 - x_lo) * 8 + zz * 2
        fill(source, own_tables, source, flon * 160.0)


    sum_all.wait_recv()
    total = jnp.sum(sum_in[...], axis=0)
    damping = (damp_ref[0], damp_ref[1])
    vertical = ((vert_ref[0, 0], vert_ref[0, 1]), (vert_ref[1, 0], vert_ref[1, 1]))
    first8 = first_ref[pl.ds(pl.multiple_of((chip // 5) * 16, 8), 8), 0:1]
    lane0 = ((chip % 5) * 128).astype(F32)
    spec = correct(total, first8, lane0, chip == 15, damping, vertical)
    gathered[core, chip] = spec.astype(BF16)

    mine_all = gathered.at[core, chip]
    others = gathered.at[core, 0:15]
    all_all = remote(others, others, all_send, all_recv, lat_device(1))
    both_all = remote(gathered.at[1 - core], gathered.at[1 - core], pair_send, pair_recv, (sibling, lon))
    for o in FAR_FIRST + (0,):
        if o:
            remote(mine_all, mine_all, all_send, all_recv, lat_device(o)).start()
        remote(mine_all, mine_all, pair_send, pair_recv, (chips[o] * 2 + 1 - core, lon)).start()
    all_all.wait_recv()
    both_all.wait_recv()

    evens, odds = [], []
    for c in range(2):
        tiles = [[gathered[c, kb * 5 + t].astype(F32) for t in range(5)] for kb in range(3)]
        packed = jnp.concatenate([jnp.concatenate(row, axis=1) for row in tiles], axis=0)
        last = gathered[c, 15].astype(F32)
        extra = jnp.concatenate([last[:, kb:kb + 1] for kb in range(3)], axis=0)
        e, o = unpack(packed, extra, first)
        evens.append(e)
        odds.append(o)
    scale_even = jnp.where(first == 0.0, 1.0, 2.0)
    scale_odd = jnp.where(first == M - 1.0, 1.0, 2.0)
    north_e = [e * scale_even for e in evens]
    north_o = [o * scale_odd for o in odds]
    rows_e = jnp.concatenate(north_e + [e * sign for e in north_e], axis=0).astype(BF16)
    rows_o = jnp.concatenate(north_o + [-(o * sign) for o in north_o], axis=0).astype(BF16)
    x_even = dot_nt(rows_e, leg)
    x_odd = dot_nt(rows_o, reversed_ref[...])
    coefs[lon] = collapse(x_even, x_odd, select_rows_t(), spreader)

    def coef_copy(o, at):
        return remote(coefs.at[at], coefs.at[at], coef_send, coef_recv.at[o], (lat, lons[o]))

    def forward_copy(o):
        return remote(coefs.at[lons[o]], coefs.at[lons[o]], fwd_send, fwd_recv, (lat, near))

    for o in Z_FAR_FIRST:
        coef_copy(o, lon).start()
    forward_copy(0).start()

    evens = jnp.concatenate(evens, axis=0).astype(BF16)
    odds = jnp.concatenate(odds, axis=0).astype(BF16)
    spec_ref[...] = spectrum_rows(evens, odds, flat)

    for o in (1, 2, 6, 3, 7, 5, 4):
        coef_copy(o, lons[o]).wait_recv()
        forward_copy(o).start()

    def inverse(half):
        rows = pl.ds(pl.multiple_of(half * 320, 320), 320)
        parts = []
        for part, v in enumerate(unfold(coefs[pl.ds(half * 8, 8)].astype(F32))):
            v = v.T.astype(BF16)
            parts.append(dot(v, own_tables[2 * part][rows, :]) + dot(v, own_tables[2 * part + 1][rows, :]))
        return parts[0][0:80] + jnp.concatenate([parts[1][80:128], parts[1][0:32]], axis=0)

    grid = inverse(x_lo)

    forward_all = remote(coefs.at[0:8], coefs.at[0:8], fwd_send, fwd_recv, (lat, near))
    forward_all.wait_recv()

    grid = grid + inverse(1 - x_lo)
    grid = grid * (1.0 / float(NLON * M) ** 0.5)
    for l in range(2):
        for i in range(ROWS):
            at = 40 * l + 2 * i
            grid_ref[l, i] = grid[at:at + 2, 0:160]

    part_all.wait_send()
    sum_all.wait_send()
    all_all.wait_send()
    both_all.wait_send()
    remote(coefs.at[0:7], coefs.at[0:7], coef_send, coef_recv.at[0], (lat, near)).wait_send()
    forward_all.wait_send()


def shards(level_fields, wind_field, zonal_step, quad_weight, legendre, wave_table, damping, vertical):
    def rows(x):
        return x.transpose(0, 2, 1, 3)

    vmem = pl.BlockSpec(memory_space=pltpu.VMEM)
    hbm = pl.BlockSpec(memory_space=pl.ANY)
    dma = pltpu.SemaphoreType.DMA
    grid, spec = pl.pallas_call(
        kernel,
        out_shape=(
            jax.ShapeDtypeStruct((2, ROWS, 2, 160), F32),
            jax.ShapeDtypeStruct((32, 160), F32),
        ),
        in_specs=[hbm] * 8,
        out_specs=(vmem, vmem),
        scratch_shapes=[
            pltpu.VMEM((2, 2, ROWS, 2, 160), F32),
            pltpu.VMEM((1, ROWS), F32),
            pltpu.VMEM((1, ROWS), F32),
            pltpu.VMEM((K, M), BF16),
            pltpu.VMEM((5, 128), jnp.int32),
            pltpu.SMEM((2,), F32),
            pltpu.SMEM((2, 2), F32),
            pltpu.VMEM((4, 40, LANES), F32),
            pltpu.VMEM((40, 128), F32),
            pltpu.VMEM((5, 40, 128), F32),
            pltpu.VMEM((2, 8, 128), F32),
            pltpu.VMEM((2, 2, 8, 128), F32),
            pltpu.VMEM((2, 2, 2, 8, LANES), F32),
            pltpu.VMEM((M, 128), F32),
            pltpu.VMEM((M, LANES), BF16),
            pltpu.VMEM((M, LANES), BF16),
            pltpu.VMEM((M, LANES), BF16),
            pltpu.VMEM((M, LANES), BF16),
            pltpu.VMEM((M // 2, LANES), BF16),
            pltpu.VMEM((M // 2, LANES), BF16),
            pltpu.VMEM((M // 2, LANES), BF16),
            pltpu.VMEM((M // 2, LANES), BF16),
            pltpu.VMEM((K, M), BF16),
            pltpu.VMEM((8, FOLDED, 128), F32),
            pltpu.VMEM((8, FOLDED, 128), F32),
            pltpu.VMEM((384, K), BF16),
            pltpu.VMEM((2, BLOCKS, 16, 128), F32),
            pltpu.VMEM((BLOCKS, 16, 128), F32),
            pltpu.VMEM((BLOCKS, 16, 128), F32),
            pltpu.VMEM((CHIPS, 16, 128), F32),
            pltpu.VMEM((64, 128), F32),
            pltpu.VMEM((2, BLOCKS, 16, 128), BF16),
            pltpu.VMEM((16, FOLDED16, 128), BF16),
            dma((8,)), dma((8,)), dma((8,)), dma((2,)), dma((2,)), dma, dma, dma,
            dma, dma, dma, dma, dma, dma, dma, dma,
            dma((8,)), dma, dma, pltpu.SemaphoreType.REGULAR((3,)),
        ],
        compiler_params=pltpu.CompilerParams(
            collective_id=0, has_side_effects=True, vmem_limit_bytes=60 * 1024 * 1024
        ),
    )(
        rows(level_fields), rows(wind_field), zonal_step[None], quad_weight[None],
        legendre.transpose(1, 0, 2).reshape(K, M), wave_table.reshape(5, 128), damping, vertical,
    )
    fields = grid.transpose(0, 2, 1, 3)
    spectrum = spec[:ROWS].reshape(ROWS, 2, 2, SLOTS).transpose(0, 3, 1, 2)
    return fields, spectrum


def solution(mesh):
    return jax.shard_map(
        shards,
        mesh=mesh,
        in_specs=(
            P(None, None, "lat", "lon"),
            P(None, None, "lat", "lon"),
            P("lat"),
            P("lat"),
            P("lon", "lat", None),
            P(),
            P(),
            P(),
        ),
        out_specs=(P(None, None, "lat", "lon"), P("lat", "lon", None, None)),
        check_vma=False,
    )
```
